32 devices in a mesh: section: 2 (over core), dp: 16 (over z, y, x).
Axes of the slice: x: 2, y: 2, z: 4, core: 2. Of those that a mesh axis runs over, the one named last changes fastest.
Arguments:
- section_inputs: bfloat16 [2, 2, 16384, 800], P('section', None, 'dp'), may hold values from -6 to 6
- seq_lengths: int32 [2, 128], P(None, 'dp'), may hold values from 0 to 1024, as said below
- dilations: int32 [2], P('section'), may hold values from 1 to 16, as said below
- gains_in: float32 [2, 800], P('section'), may hold values from 0.5 to 1.5
- biases_in: float32 [2, 800], P('section'), may hold values from -1.5 to 1.5
- gains_mid: float32 [2, 2, 400], P('section'), may hold values from 0.5 to 1.5
- biases_mid: float32 [2, 2, 400], P('section'), may hold values from -1.5 to 1.5
- out_bias: float32 [2, 800], P('section'), may hold values from -1.5 to 1.5
- w_in: bfloat16 [2, 800, 400], P('section'), may hold values from -0.21875 to 0.21875
- w_out: bfloat16 [2, 400, 800], P('section'), may hold values from -0.625 to 0.625
- conv_taps: bfloat16 [2, 5, 400, 400], P('section'), may hold values from -0.125 to 0.125
Outputs:
- block_out: bfloat16 [2, 2, 16384, 800], P('section', None, 'dp')
- input_grad: bfloat16 [2, 2, 16384, 800], P('section', None, 'dp')
- grad_gains_in: float32 [2, 800], P('section')
- grad_biases_in: float32 [2, 800], P('section')
- grad_gains_mid: float32 [2, 2, 400], P('section')
- grad_biases_mid: float32 [2, 2, 400], P('section')
- grad_out_bias: float32 [2, 800], P('section')
- grad_w_in: float32 [2, 800, 400], P('section')
- grad_w_out: float32 [2, 400, 800], P('section')
- grad_conv_taps: float32 [2, 5, 400, 400], P('section')
The draws below stay inside these ranges and needn't reach their ends.
Inputs may be any that keep to these rules, and one draw needn't show every extreme that they name: `seq_lengths`: each index of dp holds, in each micro-batch, 1024 tokens made of whole sequences of 128, 256, 512 or 1024 tokens, each beginning at a multiple of its own length within those tokens; an entry is the length of the sequence that begins at that unit, 0 where none begins; some index holds one sequence of 1024 tokens. `dilations`: powers of two; one of the two is 16.
All inputs are finite; a program needn't handle non-finite values.
Results may differ from the reference program's by a relative error of at most 0.012.
Values may be sent and summed in bfloat16 or wider, within the bound.
No kernel may reach another device: no remote copies, remote signals or barrier semaphores. Data moves between devices by JAX's collectives and lax.ppermute only.
A program may use at most 192 MiB of HBM per device.

```python
import jax
import jax.numpy as jnp
from jax import lax

D = 800
INNER = 400
TAPS = 5
DEC_TAPS = 3
UNIT = 128
MB = 2
TOK_MB = 1024
TOKENS = 16384


def draw_seq_lengths(key, part):
    key = jax.random.fold_in(key, 11)
    key_top, key_half, key_quarter, key_whole = jax.random.split(key, 4)
    blocks = MB * (TOKENS // TOK_MB)
    split_top = jax.random.randint(key_top, (blocks, 1), 0, 10) < 7
    whole_block = jax.random.randint(key_whole, (), 0, blocks)
    split_top = split_top & (jnp.arange(blocks)[:, None] != whole_block)
    split_half = jax.random.randint(key_half, (blocks, 2), 0, 10) < 6
    split_quarter = jax.random.randint(key_quarter, (blocks, 4), 0, 10) < 5
    unit_index = jnp.arange(8)
    size_units = jnp.where(jnp.logical_not(split_top), 8, jnp.where(jnp.logical_not(split_half[:, unit_index // 4]), 4, jnp.where(jnp.logical_not(split_quarter[:, unit_index // 2]), 2, 1)))
    begins = unit_index[None, :] % size_units == 0
    lengths = jnp.where(begins, size_units * UNIT, 0).astype(jnp.int32)
    return lengths.reshape(MB, TOKENS // UNIT)


def draw_dilations(key, part):
    key = jax.random.fold_in(key, 23)
    key_power, key_pick = jax.random.split(key)
    powers = jax.random.randint(key_power, (2,), 0, 5)
    picked = jax.random.randint(key_pick, (), 0, 2)
    powers = jnp.where(jnp.arange(2) == picked, 4, powers)
    return jnp.left_shift(jnp.ones((2,), jnp.int32), powers.astype(jnp.int32))


def level_of(own_key, shape, cuts, least, high):
    def one(dim, blocks):
        heights = jax.random.uniform(jax.random.fold_in(jax.random.fold_in(own_key, 6), dim), (blocks,), jnp.float32, least / len(cuts), high / len(cuts))
        return jnp.repeat(jnp.exp(heights), shape[dim] // blocks).reshape((-1,) + (1,) * (len(shape) - dim - 1))

    factor_of = one(*cuts[0])
    for cut in cuts[1:]:
        factor_of = factor_of * one(*cut)
    return factor_of


def gaussian(key, extent, spread, reach, cuts=(), held_as=jnp.bfloat16):
    gain = level_of(key, extent, cuts, -0.22, 0.18) if cuts else 1.0
    values = jax.random.normal(key, extent, jnp.float32) * spread * gain
    return jnp.minimum(jnp.maximum(values, -reach), reach).astype(held_as)


def setup_inputs(seed: int = 0) -> dict:
    streams_of = jax.random.split(jax.random.key(seed), 12)
    section_inputs = gaussian(streams_of[0], (2, MB, TOKENS, D), 1.0, 6.0, ((0, 2), (2, 16)))
    seq_lengths = draw_seq_lengths(jax.random.fold_in(streams_of[11], 71), 0)
    dilations = draw_dilations(jax.random.fold_in(streams_of[11], 71), 0)
    gains_in = jnp.clip(1.0 + 0.1 * jax.random.normal(streams_of[3], (2, D), jnp.float32), 0.5, 1.5)
    biases_in = gaussian(streams_of[4], (2, D), 0.3, 1.5, ((0, 2),), jnp.float32)
    gains_mid = jnp.clip(1.0 + 0.1 * jax.random.normal(streams_of[5], (2, 2, INNER), jnp.float32), 0.5, 1.5)
    biases_mid = gaussian(streams_of[6], (2, 2, INNER), 0.3, 1.5, ((0, 2),), jnp.float32)
    out_bias = gaussian(streams_of[7], (2, D), 0.3, 1.5, ((0, 2),), jnp.float32)
    w_in = gaussian(streams_of[8], (2, D, INNER), D ** -0.5, 0.21875, ((0, 2),))
    w_out = gaussian(streams_of[9], (2, INNER, D), (INNER // 4) ** -0.5, 0.625, ((0, 2),))
    conv_taps = gaussian(streams_of[10], (2, TAPS, INNER, INNER), (TAPS * INNER) ** -0.5, 0.125, ((0, 2),))
    return dict(section_inputs=section_inputs, seq_lengths=seq_lengths, dilations=dilations, gains_in=gains_in, biases_in=biases_in, gains_mid=gains_mid, biases_mid=biases_mid, out_bias=out_bias, w_in=w_in, w_out=w_out, conv_taps=conv_taps)


EPS = 1e-05

@jax.custom_vjp
def low(v):
    return lax.optimization_barrier(v.astype(jnp.bfloat16)).astype(jnp.float32)

@jax.custom_vjp
def low_back(v):
    return v

def low_keep(v):
    return (low(v), None)

def low_pass(kept, grad):
    return (grad,)

def back_keep(v):
    return (v, None)

def back_low(kept, grad):
    return (low(grad),)
low.defvjp(low_keep, low_pass)
low_back.defvjp(back_keep, back_low)

def matmul(left_matrix, right_matrix):
    return jnp.dot(left_matrix, right_matrix, precision=lax.Precision.HIGHEST)

def normalize(values, gain_vec, bias_vec):
    average = lax.optimization_barrier(jnp.mean(values, axis=-1, keepdims=True))
    centered = values - average
    return centered * lax.rsqrt(lax.optimization_barrier(jnp.mean(centered * centered, axis=-1, keepdims=True)) + EPS) * gain_vec + bias_vec

def shift_rows(token_rows, segment, offset):
    length_rows = token_rows.shape[0]
    padded = jnp.pad(token_rows, ((length_rows, length_rows), (0, 0)))
    shifted = lax.dynamic_slice_in_dim(padded, length_rows + offset, length_rows, 0)
    labels = jnp.pad(segment, (length_rows, length_rows), constant_values=-1)
    shifted_labels = lax.dynamic_slice_in_dim(labels, length_rows + offset, length_rows, 0)
    return jnp.where((shifted_labels == segment)[:, None], shifted, jnp.zeros_like(shifted))

def block(token_rows, segment, dilation, tap_count, params, section):
    gain_in = params[0][section]
    bias_in = params[1][section]
    gain_mid = params[2][section]
    bias_mid = params[3][section]
    bias_out = params[4][section]
    weight_in = params[5][section]
    weight_out = params[6][section]
    kernel = params[7][section][:tap_count]
    hidden_in = low(jax.nn.silu(normalize(token_rows, gain_in, bias_in)))
    projected = low_back(matmul(hidden_in, weight_in))
    hidden_mid = low(jax.nn.silu(normalize(projected, gain_mid[0], bias_mid[0])))
    shifted = jnp.stack([shift_rows(hidden_mid, segment, (position - 2) * dilation) for position in range(tap_count)], axis=1)
    mixed = low_back(jnp.einsum('tki,kij->tj', shifted, kernel, precision=lax.Precision.HIGHEST))
    hidden_out = low(jax.nn.silu(normalize(mixed, gain_mid[1], bias_mid[1])))
    return token_rows + matmul(hidden_out, weight_out) + bias_out

def reference(section_inputs, seq_lengths, dilations, gains_in, biases_in, gains_mid, biases_mid, out_bias, w_in, w_out, conv_taps):
    micro = section_inputs.shape[1]
    tokens = section_inputs.shape[2]
    width = section_inputs.shape[3]
    starts = (seq_lengths > 0).astype(jnp.int32)
    labels = jnp.cumsum(starts.reshape(-1)).astype(jnp.int32).reshape(starts.shape)
    group_len = 4 * TOK_MB
    groups = micro * tokens // group_len
    segments = jnp.repeat(labels, UNIT, axis=1).reshape(groups, group_len)
    inputs = section_inputs[0].astype(jnp.float32).reshape(groups, group_len, width)
    cotangent = section_inputs[1].astype(jnp.float32).reshape(groups, group_len, width)
    probes = jnp.zeros_like(inputs)
    params = tuple((member.astype(jnp.float32) for member in (gains_in, biases_in, gains_mid, biases_mid, out_bias, w_in, w_out, conv_taps)))

    def forward(params, inputs, probes):

        def one_group(items):
            token_rows, segment, probe = items
            encoded = low(block(token_rows, segment, dilations[0], TAPS, params, 0))
            decoded = block(low_back(encoded + probe), segment, dilations[1], DEC_TAPS, params, 1)
            return (encoded, decoded)
        return lax.map(jax.checkpoint(one_group), (inputs, segments, probes))
    (encoded, decoded), pull_back = jax.vjp(forward, params, inputs, probes)
    grad_params, grad_inputs, grad_probes = pull_back((jnp.zeros_like(encoded), cotangent))
    block_out = jnp.stack([encoded, decoded]).reshape(2, micro, tokens, width).astype(jnp.bfloat16)
    input_grad = jnp.stack([grad_inputs, grad_probes]).reshape(2, micro, tokens, width).astype(jnp.bfloat16)
    return (block_out, input_grad, grad_params[0], grad_params[1], grad_params[2], grad_params[3], grad_params[4], grad_params[5], grad_params[6], grad_params[7])
```

```python
import functools

import jax
import jax.numpy as jnp
from jax import lax
from jax.experimental import pallas as pl
from jax.experimental.pallas import tpu as pltpu
from jax.sharding import PartitionSpec as P

DEC_TAPS = 3
EPS = 1e-05
LANES = 128
VEC_ROWS = 48
BF = jnp.bfloat16
F32 = jnp.float32
VMEM_LIMIT = 62 * 2**20


def nn(left, right):
    return jnp.dot(left, right, preferred_element_type=F32)


def nt(left, right):
    return lax.dot_general(left, right, (((1,), (1,)), ((), ())), preferred_element_type=F32)


def column(vector):
    return jnp.broadcast_to(vector, (LANES, vector.shape[1])).T


def lane_block(index):
    return pl.ds(pl.multiple_of(index * LANES, LANES), LANES)


def normalize(values):
    scale = 1.0 / values.shape[0]
    centered = values - jnp.sum(values, 0, keepdims=True) * scale
    inverse_dev = lax.rsqrt(jnp.sum(centered * centered, 0, keepdims=True) * scale + EPS)
    return centered * inverse_dev, inverse_dev


def activate(normed, gain, bias):
    pre = normed * gain + bias
    sig = 0.5 * jnp.tanh(0.5 * pre) + 0.5
    out = pre * sig
    return out, (sig + out - out * sig) * gain


def norm_back(gradient, slope, normed, inverse_dev):
    scale = 1.0 / gradient.shape[0]
    scaled = gradient * slope
    weighted = scaled * normed
    first = jnp.sum(scaled, 0, keepdims=True) * scale
    second = jnp.sum(weighted, 0, keepdims=True) * scale
    return inverse_dev * (scaled - first - normed * second), scaled, weighted


def write_shifts(source, target, begins, offsets):
    feats, tokens = source.shape
    units = tokens // LANES
    lane = lax.broadcasted_iota(jnp.int32, (feats, LANES), 1)

    def one_unit(unit, _):
        here = lane_block(unit)
        ahead_unit = jnp.minimum(unit + 1, units - 1)
        joined_behind = ((unit > 0) & (begins[unit] == 0)).astype(F32)
        joined_ahead = ((unit < units - 1) & (begins[ahead_unit] == 0)).astype(F32)
        current = source[:, here]
        behind = source[:, lane_block(jnp.maximum(unit - 1, 0))] * joined_behind
        ahead = source[:, lane_block(ahead_unit)] * joined_ahead
        for position, (sign, step) in enumerate(offsets):
            if sign == 0:
                moved = current
            elif sign < 0:
                moved = pltpu.roll(jnp.where(lane < LANES - step, current, behind), step, 1)
            else:
                moved = pltpu.roll(jnp.where(lane >= step, current, ahead), LANES - step, 1)
            target[feats * position : feats * (position + 1), here] = moved.astype(BF)
        return 0

    lax.fori_loop(0, units, one_unit, 0)


def tap_offsets(taps, dilation, flip):
    result = []
    for position in range(taps):
        factor = (position - 2) * (-1 if flip else 1)
        result.append(((factor > 0) - (factor < 0), abs(factor) * dilation))
    return result


def forward_kernel(
    taps,
    begins, dilation, x, g1, b1, g2, b2, g3, b3, ob, w_in_t, w_out, conv,
    y, n1, s1, r, n2, s2, n3, s3, hin, shifted, hout,
    hmid, prod, cg1, cb1, cg2, cb2, cg3, cb3, cob, w_out_t, conv_t,
):
    tokens = x.shape[1]
    inner = w_out.shape[0]
    for col, vec in ((cg1, g1), (cb1, b1), (cg2, g2), (cb2, b2), (cg3, g3), (cb3, b3), (cob, ob)):
        col[...] = column(vec[...])
    w_out_t[...] = w_out[...].T
    for k in range(taps):
        conv_t[:, inner * k : inner * (k + 1)] = conv[k].T

    def first(i, _):
        c = lane_block(i)
        normed, dev = normalize(x[:, c].astype(F32))
        hidden, slope = activate(normed, cg1[...], cb1[...])
        n1[:, c] = normed
        s1[:, c] = slope
        r[0:1, c] = dev
        hin[:, c] = hidden.astype(BF)
        return 0

    lax.fori_loop(0, tokens // LANES, first, 0, unroll=2)
    prod[...] = nn(w_in_t[...], hin[...])

    def second(i, _):
        c = lane_block(i)
        normed, dev = normalize(prod[:, c])
        hidden, slope = activate(normed, cg2[...], cb2[...])
        n2[:, c] = normed
        s2[:, c] = slope
        r[1:2, c] = dev
        hmid[:, c] = hidden
        return 0

    lax.fori_loop(0, tokens // LANES, second, 0, unroll=2)
    write_shifts(hmid, shifted, begins, tap_offsets(taps, dilation[0], False))
    prod[...] = nn(conv_t[...], shifted[...])

    def third(i, _):
        c = lane_block(i)
        normed, dev = normalize(prod[:, c])
        hidden, slope = activate(normed, cg3[...], cb3[...])
        n3[:, c] = normed
        s3[:, c] = slope
        r[2:3, c] = dev
        hout[:, c] = hidden.astype(BF)
        return 0

    lax.fori_loop(0, tokens // LANES, third, 0, unroll=2)
    bias = jnp.concatenate([cob[...]] * (tokens // LANES), 1)
    y[...] = (x[...].astype(F32) + nn(w_out_t[...], hout[...]) + bias).astype(BF)


def forward(taps, begins, dilation, x, vecs, w_in_t, w_out, conv):
    width, tokens = x.shape
    inner = w_out.shape[0]
    smem = pl.BlockSpec(memory_space=pltpu.SMEM)
    vmem = pl.BlockSpec(memory_space=pltpu.VMEM)
    of = jax.ShapeDtypeStruct
    return pl.pallas_call(
        functools.partial(forward_kernel, taps),
        in_specs=[smem, smem] + [vmem] * 11,
        out_specs=[vmem] * 11,
        out_shape=[
            of((width, tokens), BF),
            of((width, tokens), F32),
            of((width, tokens), F32),
            of((8, tokens), F32),
            of((inner, tokens), F32),
            of((inner, tokens), F32),
            of((inner, tokens), F32),
            of((inner, tokens), F32),
            of((width, tokens), BF),
            of((inner * taps, tokens), BF),
            of((inner, tokens), BF),
        ],
        scratch_shapes=[pltpu.VMEM((inner, tokens), F32)] * 2
        + [pltpu.VMEM((width, LANES), F32)] * 2
        + [pltpu.VMEM((inner, LANES), F32)] * 4
        + [
            pltpu.VMEM((width, LANES), F32),
            pltpu.VMEM((width, inner), BF),
            pltpu.VMEM((inner, inner * taps), BF),
        ],
        compiler_params=pltpu.CompilerParams(vmem_limit_bytes=VMEM_LIMIT),
        name="forward_%d" % taps,
    )(begins, dilation, x, *vecs, w_in_t, w_out, conv)


def put_slabs(buf, row, matrix):
    rows, cols = matrix.shape
    for q in range(pl.cdiv(cols, LANES)):
        part = matrix[:, LANES * q : min(cols, LANES * (q + 1))]
        if part.shape[1] < LANES:
            part = jnp.concatenate([part, jnp.zeros((rows, LANES - part.shape[1]), F32)], 1)
        buf[row + q * rows : row + (q + 1) * rows, :] = part.astype(BF)


def row_sums(acc):
    return lax.dot_general(
        jnp.ones((8, LANES), F32), acc, (((1,), (1,)), ((), ())),
        precision=lax.Precision.HIGHEST, preferred_element_type=F32,
    )[0:1]


def layout(taps, width, inner):
    wide = pl.cdiv(width, LANES) * inner
    whole = inner // LANES
    taps_at = wide
    tails_at = taps_at + taps * whole * inner
    w_in_at = tails_at + inner
    vec_at = w_in_at + wide
    return taps_at, tails_at, w_in_at, vec_at, vec_at + VEC_ROWS


def backward_kernel(
    taps,
    begins, dilation, gy, n1, s1, r, n2, s2, n3, s3, hin, shifted, hout, g1, g2, g3, w_in_t, w_out, conv,
    gx, buf,
    prod, prod_wide, gm, gm_b, gp, moved, conv_w, w_in, ag1, ab1, ag2, ab2, ag3, ab3, vec,
):
    width, tokens = gy.shape
    inner = w_out.shape[0]
    taps_at, tails_at, w_in_at, vec_at, _ = layout(taps, width, inner)
    whole = inner // LANES
    tail = inner - whole * LANES
    w_in[...] = w_in_t[...].T
    for k in range(taps):
        conv_w[:, inner * k : inner * (k + 1)] = conv[k]
    for acc in (ag1, ab1, ag2, ab2, ag3, ab3):
        acc[...] = jnp.zeros_like(acc)

    prod[...] = nn(w_out[...], gy[...])

    def third(i, _):
        c = lane_block(i)
        value, scaled, weighted = norm_back(prod[:, c], s3[:, c], n3[:, c], r[2:3, c])
        ab3[...] += scaled
        ag3[...] += weighted
        gm[:, c] = value
        gm_b[:, c] = value.astype(BF)
        return 0

    lax.fori_loop(0, tokens // LANES, third, 0, unroll=2)
    put_slabs(buf, 0, nt(hout[...], gy[...]))
    write_shifts(gm, moved, begins, tap_offsets(taps, dilation[0], True))
    prod[...] = nn(conv_w[...], moved[...])
    for k in range(taps):
        grad = nt(shifted[inner * k : inner * (k + 1), :], gm_b[...])
        for q in range(whole):
            at = taps_at + inner * (whole * k + q)
            buf[at : at + inner, :] = grad[:, LANES * q : LANES * (q + 1)].astype(BF)
        buf[tails_at : tails_at + inner, tail * k : tail * (k + 1)] = grad[:, LANES * whole :].astype(BF)
    buf[tails_at : tails_at + inner, tail * taps :] = jnp.zeros((inner, LANES - tail * taps), BF)

    def second(i, _):
        c = lane_block(i)
        value, scaled, weighted = norm_back(prod[:, c], s2[:, c], n2[:, c], r[1:2, c])
        ab2[...] += scaled
        ag2[...] += weighted
        gp[:, c] = value.astype(BF)
        return 0

    lax.fori_loop(0, tokens // LANES, second, 0, unroll=2)
    put_slabs(buf, w_in_at, nt(gp[...], hin[...]))
    prod_wide[...] = nn(w_in[...], gp[...])

    def first(i, _):
        c = lane_block(i)
        value, scaled, weighted = norm_back(prod_wide[:, c], s1[:, c], n1[:, c], r[0:1, c])
        ab1[...] += scaled
        ag1[...] += weighted
        gx[:, c] = (gy[:, c].astype(F32) + value).astype(BF)
        return 0

    lax.fori_loop(0, tokens // LANES, first, 0, unroll=2)

    vec[...] = jnp.zeros_like(vec)
    sums = [
        row_sums(ag1[...]) / g1[...],
        row_sums(ab1[...]) / g1[...],
        row_sums(ag2[...]) / g2[...],
        row_sums(ag3[...]) / g3[...],
        row_sums(ab2[...]) / g2[...],
        row_sums(ab3[...]) / g3[...],
        nt(jnp.ones((16, tokens), BF), gy[...])[0:1],
    ]
    row = 0
    for total in sums:
        for at in range(0, total.shape[1], LANES):
            part = total[:, at : at + LANES]
            vec[row : row + 1, 0 : part.shape[1]] = part
            row += 1
    buf[vec_at : vec_at + VEC_ROWS, :] = vec[...].astype(BF)


def backward(taps, begins, dilation, gy, kept, gains, w_in_t, w_out, conv):
    width, tokens = gy.shape
    inner = w_out.shape[0]
    smem = pl.BlockSpec(memory_space=pltpu.SMEM)
    vmem = pl.BlockSpec(memory_space=pltpu.VMEM)
    of = jax.ShapeDtypeStruct
    return pl.pallas_call(
        functools.partial(backward_kernel, taps),
        in_specs=[smem, smem] + [vmem] * 17,
        out_specs=[vmem] * 2,
        out_shape=[of((width, tokens), BF), of((layout(taps, width, inner)[-1], LANES), BF)],
        scratch_shapes=[
            pltpu.VMEM((inner, tokens), F32),
            pltpu.VMEM((width, tokens), F32),
            pltpu.VMEM((inner, tokens), F32),
            pltpu.VMEM((inner, tokens), BF),
            pltpu.VMEM((inner, tokens), BF),
            pltpu.VMEM((inner * taps, tokens), BF),
            pltpu.VMEM((inner, inner * taps), BF),
            pltpu.VMEM((width, inner), BF),
            pltpu.VMEM((width, LANES), F32),
            pltpu.VMEM((width, LANES), F32),
        ]
        + [pltpu.VMEM((inner, LANES), F32)] * 4
        + [pltpu.VMEM((VEC_ROWS, LANES), F32)],
        compiler_params=pltpu.CompilerParams(vmem_limit_bytes=VMEM_LIMIT),
        name="backward_%d" % taps,
    )(begins, dilation, gy, *kept, *gains, w_in_t, w_out, conv)


def swap_sections(value):
    return lax.ppermute(value, "section", [(0, 1), (1, 0)])


def swap_dp(value, mask):
    count = lax.axis_size("dp")
    return lax.ppermute(value, "dp", [(i, i ^ mask) for i in range(count)])


def add_rounded(*parts):
    total = parts[0].astype(F32)
    for part in parts[1:]:
        total = total + part.astype(F32)
    return total.astype(BF)


def piece(array, index, count):
    size = array.shape[0] // count
    return lax.dynamic_slice_in_dim(array, index * size, size, 0)


def scatter_step(array, index, bits):
    own = (index >> bits[0]) & (2 ** len(bits) - 1)
    count = 2 ** len(bits)
    parts = [piece(array, own, count)]
    for other in range(1, count):
        parts.append(swap_dp(piece(array, own ^ other, count), other << bits[0]))
    return add_rounded(*parts)


def gather_step(array, index, bits):
    own = (index >> bits[0]) & (2 ** len(bits) - 1)
    count = 2 ** len(bits)
    size = array.shape[0]
    whole = jnp.zeros((size * count,) + array.shape[1:], array.dtype)
    whole = lax.dynamic_update_slice_in_dim(whole, array, own * size, 0)
    for other in range(1, count):
        whole = lax.dynamic_update_slice_in_dim(whole, swap_dp(array, other << bits[0]), (own ^ other) * size, 0)
    return whole


def step_orders(count):
    total = count.bit_length() - 1
    rest = []
    at = 2
    while at < total:
        rest.append(list(range(at, min(at + 2, total))))
        at += 2
    return ([[0], [1]] + rest, [[1], [0]] + rest)


def all_reduce_dp(array):
    count = lax.axis_size("dp")
    index = lax.axis_index("dp")
    orders = step_orders(count)
    half = array.shape[0] // 2
    parts = [array[:half], array[half:]]
    for steps in zip(*orders):
        parts = [scatter_step(part, index, bits) for part, bits in zip(parts, steps)]
    for steps in reversed(list(zip(*orders))):
        parts = [gather_step(part, index, bits) for part, bits in zip(parts, steps)]
    return jnp.concatenate(parts, 0)


def reduce_block(buf, section):
    rows = buf.shape[0]
    unit = 2 * 2 * 16 * lax.axis_size("dp")
    padded = jnp.pad(buf, ((0, -rows % unit), (0, 0)))
    mine = add_rounded(piece(padded, section, 2), swap_sections(piece(padded, 1 - section, 2)))
    return all_reduce_dp(mine)


def unpack_kernel(taps_of, index, own0, got0, own1, got1, w_in_t, w_out, conv, gin, bin_, gmid, bmid, out_bias, buf, sem):
    inner, width = w_out.shape
    whole = inner // LANES
    tail = inner - whole * LANES
    slots = conv.shape[0]

    def write(taps, first, second):
        half = first.shape[0]
        copies = [
            pltpu.make_async_copy(first, buf.at[pl.ds(0, half)], sem.at[0]),
            pltpu.make_async_copy(second, buf.at[pl.ds(half, half)], sem.at[1]),
        ]
        for copy in copies:
            copy.start()
        for copy in copies:
            copy.wait()
        taps_at, tails_at, w_in_at, vec_at, _ = layout(taps, width, inner)

        def wide(target, row):
            for at in range(0, width, LANES):
                q = at // LANES
                size = min(LANES, width - at)
                target[:, at : at + size] = buf[row + q * inner : row + (q + 1) * inner, 0:size].astype(F32)

        wide(w_out, 0)
        wide(w_in_t, w_in_at)
        tails = buf[tails_at : tails_at + inner, :].astype(F32)
        for k in range(slots):
            if k >= taps:
                conv[k] = jnp.zeros((inner, inner), F32)
                continue
            for q in range(whole):
                at = taps_at + inner * (whole * k + q)
                conv[k, :, LANES * q : LANES * (q + 1)] = buf[at : at + inner, :].astype(F32)
            conv[k, :, LANES * whole :] = tails[:, tail * k : tail * (k + 1)]
        vec = buf[vec_at : vec_at + VEC_ROWS, :].astype(F32)
        row = 0
        for target, member in ((gin, 0), (bin_, 0), (gmid, 0), (gmid, 1), (bmid, 0), (bmid, 1), (out_bias, 0)):
            for at in range(0, target.shape[1], LANES):
                size = min(LANES, target.shape[1] - at)
                target[member : member + 1, at : at + size] = vec[row : row + 1, 0:size]
                row += 1

    pl.when(index[0] == 0)(lambda: write(taps_of[0], own0, got0))
    pl.when(index[0] != 0)(lambda: write(taps_of[1], got1, own1))


def unpack(taps_of, section, halves, got, width, inner):
    smem = pl.BlockSpec(memory_space=pltpu.SMEM)
    vmem = pl.BlockSpec(memory_space=pltpu.VMEM)
    hbm = pl.BlockSpec(memory_space=pl.ANY)
    of = jax.ShapeDtypeStruct
    rows = max(2 * half.shape[0] for half in halves)
    return pl.pallas_call(
        functools.partial(unpack_kernel, taps_of),
        in_specs=[smem] + [hbm] * 4,
        out_specs=[vmem] * 8,
        out_shape=[
            of((inner, width), F32),
            of((inner, width), F32),
            of((taps_of[0], inner, inner), F32),
            of((1, width), F32),
            of((1, width), F32),
            of((2, inner), F32),
            of((2, inner), F32),
            of((1, width), F32),
        ],
        scratch_shapes=[pltpu.VMEM((rows, LANES), BF), pltpu.SemaphoreType.DMA((2,))],
        compiler_params=pltpu.CompilerParams(vmem_limit_bytes=VMEM_LIMIT),
        name="unpack",
    )(jnp.reshape(section, (1,)), halves[0], got[0], halves[1], got[1])


def shards(
    section_inputs,
    seq_lengths,
    dilations,
    gains_in,
    biases_in,
    gains_mid,
    biases_mid,
    out_bias,
    w_in,
    w_out,
    conv_taps,
):
    section = lax.axis_index("section")
    leading = section == 0
    rows = jnp.swapaxes(section_inputs[0], 1, 2)
    width = rows.shape[1]
    inner = w_out.shape[1]
    taps_of = (conv_taps.shape[1], DEC_TAPS)

    def pick(stacked, index):
        return lax.dynamic_index_in_dim(stacked, index, 0, keepdims=False)

    def both(mine):
        theirs = swap_sections(mine)
        return jnp.where(leading, mine, theirs), jnp.where(leading, theirs, mine)

    own_rows = pick(rows, section)
    got_rows = swap_sections(pick(rows, 1 - section))
    x = jnp.where(leading, own_rows, got_rows)
    cotangent = jnp.where(leading, got_rows, own_rows)
    w_in_t = both(jnp.swapaxes(w_in[0], 0, 1))
    small = both(
        jnp.concatenate(
            [
                gains_in[0], biases_in[0], gains_mid[0, 0], biases_mid[0, 0], gains_mid[0, 1], biases_mid[0, 1],
                out_bias[0], dilations.astype(F32),
            ]
        )
    )
    conv = both(conv_taps[0])
    w_out_both = both(w_out[0])

    vecs_of, dil_of = [], []
    for member in small:
        vecs, at = [], 0
        for size in (width, width, inner, inner, inner, inner, width):
            vecs.append(member[at : at + size][None])
            at += size
        vecs_of.append(vecs)
        dil_of.append(member[at : at + 1].astype(jnp.int32))
    begins = pick(seq_lengths, section)

    encoded = forward(taps_of[0], begins, dil_of[0], x, vecs_of[0], w_in_t[0], w_out_both[0], conv[0])
    decoded = forward(taps_of[1], begins, dil_of[1], encoded[0], vecs_of[1], w_in_t[1], w_out_both[1], conv[1])
    grad_dec, buf_dec = backward(
        taps_of[1], begins, dil_of[1], cotangent, decoded[1:], vecs_of[1][0:5:2], w_in_t[1], w_out_both[1], conv[1]
    )
    half_dec = reduce_block(buf_dec, section)
    got_dec = lax.ppermute(half_dec, "section", [(0, 1)])
    grad_enc, buf_enc = backward(
        taps_of[0], begins, dil_of[0], grad_dec, encoded[1:], vecs_of[0][0:5:2], w_in_t[0], w_out_both[0], conv[0]
    )
    half_enc = reduce_block(buf_enc, section)
    got_enc = lax.ppermute(half_enc, "section", [(1, 0)])

    def own_section(enc, dec):
        keep = jnp.where(leading, enc, dec)
        got = swap_sections(jnp.where(leading, dec, enc))
        pair = jnp.where(leading, jnp.stack([keep, got]), jnp.stack([got, keep]))
        return jnp.swapaxes(pair, 1, 2)[None]

    outputs = own_section(encoded[0], decoded[0])
    input_grads = own_section(grad_enc, grad_dec)
    grads = unpack(taps_of, section, (half_enc, half_dec), (got_enc, got_dec), width, inner)
    return (
        outputs,
        input_grads,
        grads[3],
        grads[4],
        grads[5][None],
        grads[6][None],
        grads[7],
        jnp.swapaxes(grads[0], 0, 1)[None],
        grads[1][None],
        grads[2][None],
    )


def solution(mesh):
    in_specs = (
        P("section", None, "dp", None),
        P(None, "dp"),
        P("section"),
        P("section", None),
        P("section", None),
        P("section", None, None),
        P("section", None, None),
        P("section", None),
        P("section", None, None),
        P("section", None, None),
        P("section", None, None, None),
    )
    out_specs = (
        P("section", None, "dp", None),
        P("section", None, "dp", None),
        P("section", None),
        P("section", None),
        P("section", None, None),
        P("section", None, None),
        P("section", None),
        P("section", None, None),
        P("section", None, None),
        P("section", None, None, None),
    )
    return jax.shard_map(shards, mesh=mesh, in_specs=in_specs, out_specs=out_specs, check_vma=False)
```

```python
import functools

import jax
import jax.numpy as jnp
from jax import lax
from jax.experimental import pallas as pl
from jax.experimental.pallas import tpu as pltpu
from jax.sharding import PartitionSpec as P

DEC_TAPS = 3
EPS = 1e-05
LANES = 128
CHUNK = 80
VEC_ROWS = 48
SMALL_ROWS = 8
BF = jnp.bfloat16
F32 = jnp.float32
VMEM_LIMIT = 62 * 2**20
ANY = pl.BlockSpec(memory_space=pl.ANY)
SMEM = pl.BlockSpec(memory_space=pltpu.SMEM)
VMEM = pl.BlockSpec(memory_space=pltpu.VMEM)


def shape(dims, dtype):
    return jax.ShapeDtypeStruct(tuple(dims), dtype)


def nn(left, right):
    return jnp.dot(left, right, preferred_element_type=F32)


def nt(left, right):
    return lax.dot_general(left, right, (((1,), (1,)), ((), ())), preferred_element_type=F32)


def lane_block(index):
    return pl.ds(pl.multiple_of(index * LANES, LANES), LANES)


def chunks(rows):
    size = CHUNK if rows % CHUNK == 0 else 16
    return [slice(at, at + size) for at in range(0, rows, size)]


def folded(values):
    return jnp.sum(values.reshape(values.shape[0] // 8, 8, values.shape[1]), 0)


def column(vector):
    return jnp.broadcast_to(vector, (LANES, vector.shape[1])).T


def norm_forward(source, half_gain, half_bias, normed, slope, hidden, devs, row):
    feats, tokens = source.shape
    scale = 1.0 / feats

    def stats(unit):
        here = lane_block(unit)
        base = source[0:1, here].astype(F32)
        total = jnp.zeros((8, LANES), F32)
        squares = jnp.zeros((8, LANES), F32)
        for part in chunks(feats):
            moved = source[part, here].astype(F32) - base
            total = total + folded(moved)
            squares = squares + folded(moved * moved)
        average = jnp.sum(total, 0, keepdims=True) * scale
        variance = jnp.sum(squares, 0, keepdims=True) * scale - average * average
        inverse_dev = lax.rsqrt(jnp.maximum(variance, 0.0) + EPS)
        return (average + base) * inverse_dev, inverse_dev

    def body(unit, carry):
        following = stats(jnp.minimum(unit + 1, tokens // LANES - 1))
        offset, inverse_dev = carry
        here = lane_block(unit)
        devs[row : row + 1, here] = inverse_dev
        for part in chunks(feats):
            values = source[part, here].astype(F32) * inverse_dev - offset
            gain = half_gain[part, :]
            half = values * gain + half_bias[part, :]
            tan = jnp.tanh(half)
            weight = 1.0 + tan
            out = half * weight
            normed[part, here] = values.astype(BF)
            slope[part, here] = ((weight + out * (1.0 - tan)) * gain).astype(BF)
            hidden[part, here] = out.astype(hidden.dtype)
        return following

    lax.fori_loop(0, tokens // LANES, body, stats(0))


def norm_backward(gradient, slope, normed, devs, row, gain_sums, bias_sums, emit):
    feats, tokens = gradient.shape
    scale = 1.0 / feats
    for part in chunks(feats):
        gain_sums[part, :] = jnp.zeros_like(gain_sums[part, :])
        bias_sums[part, :] = jnp.zeros_like(bias_sums[part, :])

    def means(unit):
        here = lane_block(unit)
        first = jnp.zeros((8, LANES), F32)
        second = jnp.zeros((8, LANES), F32)
        for part in chunks(feats):
            scaled = gradient[part, here] * slope[part, here].astype(F32)
            weighted = scaled * normed[part, here].astype(F32)
            gain_sums[part, :] += weighted
            bias_sums[part, :] += scaled
            first = first + folded(scaled)
            second = second + folded(weighted)
        return jnp.sum(first, 0, keepdims=True) * scale, jnp.sum(second, 0, keepdims=True) * scale

    def finish(unit, first, second):
        here = lane_block(unit)
        inverse_dev = devs[row : row + 1, here]
        first = first * inverse_dev
        second = second * inverse_dev
        for part in chunks(feats):
            scaled = gradient[part, here] * slope[part, here].astype(F32)
            emit(part, here, scaled * inverse_dev - first - normed[part, here].astype(F32) * second)

    def body(unit, carry):
        following = means(unit + 1)
        finish(unit, *carry)
        return following

    last = tokens // LANES - 1
    finish(last, *lax.fori_loop(0, last, body, means(0)))


def write_shifts(source, target, begins, offsets):
    feats, tokens = source.shape
    units = tokens // LANES

    def body(unit, _):
        here = lane_block(unit)
        behind_unit = jnp.maximum(unit - 1, 0)
        ahead_unit = jnp.minimum(unit + 1, units - 1)
        joined_behind = ((unit > 0) & (begins(unit) == 0)).astype(F32)
        joined_ahead = ((unit < units - 1) & (begins(ahead_unit) == 0)).astype(F32)
        for part in chunks(feats):
            size = part.stop - part.start
            lane = lax.broadcasted_iota(jnp.int32, (size, LANES), 1)
            current = source[part, here].astype(F32)
            behind = source[part, lane_block(behind_unit)].astype(F32) * joined_behind
            ahead = source[part, lane_block(ahead_unit)].astype(F32) * joined_ahead
            for position, (sign, step) in enumerate(offsets):
                if sign == 0:
                    moved = current
                elif sign < 0:
                    moved = pltpu.roll(jnp.where(lane < LANES - step, current, behind), step, 1)
                else:
                    moved = pltpu.roll(jnp.where(lane >= step, current, ahead), LANES - step, 1)
                target[feats * position + part.start : feats * position + part.stop, here] = moved.astype(BF)
        return 0

    lax.fori_loop(0, units, body, 0, unroll=2)


def tap_offsets(taps, dilation, flip):
    result = []
    for position in range(taps):
        factor = (position - 2) * (-1 if flip else 1)
        result.append(((factor > 0) - (factor < 0), abs(factor) * dilation))
    return result


def layout(taps, width, inner):
    wide = pl.cdiv(width, LANES) * inner
    taps_at = wide
    tails_at = taps_at + taps * (inner // LANES) * inner
    w_in_at = tails_at + inner
    vec_at = w_in_at + wide
    return taps_at, tails_at, w_in_at, vec_at, vec_at + VEC_ROWS


def scatter_groups(count, full):
    total = count.bit_length() - 1
    rest = [list(range(2, min(4, total)))] if full and total > 2 else []
    return [[[bit] for bit in bits if bit < total] + rest for bits in ((0, 1), (1, 0))]


def share_count(groups):
    return 2 ** sum(len(bits) for bits in groups)


def padded_rows(taps, width, inner, groups):
    unit = 2 * 16 * share_count(groups[0])
    return pl.cdiv(layout(taps, width, inner)[-1], unit) * unit


def put_slabs(buf, row, matrix):
    rows, cols = matrix.shape
    for q in range(pl.cdiv(cols, LANES)):
        part = matrix[:, LANES * q : min(cols, LANES * (q + 1))]
        if part.shape[1] < LANES:
            part = jnp.concatenate([part, jnp.zeros((rows, LANES - part.shape[1]), F32)], 1)
        buf[row + q * rows : row + (q + 1) * rows, :] = part.astype(BF)


def put_taps(buf, taps, width, shifted, grad_mixed):
    inner = grad_mixed.shape[0]
    taps_at, tails_at, _, _, _ = layout(taps, width, inner)
    whole = inner // LANES
    tail = inner - whole * LANES
    for k in range(taps):
        grad = nt(shifted[inner * k : inner * (k + 1), :], grad_mixed[...])
        for q in range(whole):
            at = taps_at + inner * (whole * k + q)
            buf[at : at + inner, :] = grad[:, LANES * q : LANES * (q + 1)].astype(BF)
        buf[tails_at : tails_at + inner, tail * k : tail * (k + 1)] = grad[:, LANES * whole :].astype(BF)
    buf[tails_at : tails_at + inner, tail * taps :] = jnp.zeros((inner, LANES - tail * taps), BF)


def row_sums(acc):
    return lax.dot_general(
        jnp.ones((8, LANES), F32), acc, (((1,), (1,)), ((), ())),
        precision=lax.Precision.HIGHEST, preferred_element_type=F32,
    )[0:1]


def put_vectors(buf, at, vec, sums):
    vec[...] = jnp.zeros_like(vec)
    row = 0
    for total in sums:
        for lane in range(0, total.shape[1], LANES):
            part = total[:, lane : lane + LANES]
            vec[row : row + 1, 0 : part.shape[1]] = part
            row += 1
    buf[at : at + VEC_ROWS, :] = vec[...].astype(BF)


def relative_index(position, groups):
    result = 0
    for bits in reversed(groups):
        size = 2 ** len(bits)
        result = result + (position & (size - 1)) * 2 ** bits[0]
        position = position >> len(bits)
    return result


def owner_of(position, side, groups, index):
    both = [relative_index(position, order) for order in groups]
    mask = sum(2**bit for bits in groups[0] for bit in bits)
    return jnp.where(side == 0, both[0], both[1]) ^ (index & mask)


def send_out(buf, keep, send, section, index, groups, sems):
    half = keep.shape[0]
    count = share_count(groups[0])
    share = half // count

    def body(position, _):
        for slot, (target, side) in enumerate(((keep, section), (send, 1 - section))):
            start = side * half + owner_of(position, side, groups, index) * share
            pltpu.make_async_copy(
                buf.at[pl.ds(pl.multiple_of(start, 16), share)],
                target.at[pl.ds(pl.multiple_of(position * share, 16), share)],
                sems.at[slot],
            ).start()
        return 0

    lax.fori_loop(0, count, body, 0)


def send_wait(buf, keep, send, sems):
    half = keep.shape[0]
    pltpu.make_async_copy(buf.at[pl.ds(0, half)], keep, sems.at[0]).wait()
    pltpu.make_async_copy(buf.at[pl.ds(half, half)], send, sems.at[1]).wait()


def forward_block(taps, begins, dilation, x, y, weights, cols, kept, hmid, prod):
    w_in_t, w_out_t, conv_t = weights
    g1, b1, g2, b2, g3, b3, ob = cols
    n1, s1, r, n2, s2, n3, s3, hin, shifted, hout = kept
    inner = hmid.shape[0]
    tokens = x.shape[1]
    narrow = prod.at[0:inner]
    norm_forward(x, g1, b1, n1, s1, hin, r, 0)
    narrow[...] = nn(w_in_t[...], hin[...])
    norm_forward(narrow, g2, b2, n2, s2, hmid, r, 1)
    write_shifts(hmid, shifted, begins, tap_offsets(taps, dilation, False))
    narrow[...] = nn(conv_t[:, 0 : inner * taps], shifted[...])
    norm_forward(narrow, g3, b3, n3, s3, hout, r, 2)
    prod[...] = nn(w_out_t[...], hout[...])

    def body(unit, _):
        here = lane_block(unit)
        for part in chunks(x.shape[0]):
            y[part, here] = (x[part, here].astype(F32) + prod[part, here] + ob[part, :]).astype(BF)
        return 0

    lax.fori_loop(0, tokens // LANES, body, 0)


def fill_columns(small, cols):
    g1, b1, g2, b2, g3, b3, ob = cols
    width, inner = g1.shape[0], g2.shape[0]
    for target, row, scale in ((g1, 0, 0.5), (b1, 1, 0.5), (ob, 2, 1.0)):
        target[...] = column(small[row : row + 1, 0:width] * scale)
    for target, row in ((g2, 3), (b2, 4), (g3, 5), (b3, 6)):
        target[...] = column(small[row : row + 1, 0:inner] * 0.5)


def back_third(gy, w_out, kept, prod, grad_mixed, gain_sums, bias_sums):
    n3, s3, r = kept
    inner = w_out.shape[0]
    narrow = prod.at[0:inner]
    narrow[...] = nn(w_out[...], gy[...])

    def emit(part, here, value):
        grad_mixed[part, here] = value.astype(BF)

    norm_backward(narrow, s3, n3, r, 2, gain_sums, bias_sums, emit)


def back_second(taps, begins, dilation, conv_w, kept, prod, grad_mixed, moved, grad_projected, gain_sums, bias_sums):
    n2, s2, r = kept
    inner = grad_mixed.shape[0]
    narrow = prod.at[0:inner]
    write_shifts(grad_mixed, moved, begins, tap_offsets(taps, dilation, True))
    narrow[...] = nn(conv_w[...], moved[...])

    def emit(part, here, value):
        grad_projected[part, here] = value.astype(BF)

    norm_backward(narrow, s2, n2, r, 1, gain_sums, bias_sums, emit)


def back_first(gy, w_in, kept, prod, grad_projected, gx, gain_sums, bias_sums):
    n1, s1, r = kept
    prod[...] = nn(w_in[...], grad_projected[...])

    def emit(part, here, value):
        gx[part, here] = (gy[part, here].astype(F32) + value).astype(BF)

    norm_backward(prod, s1, n1, r, 0, gain_sums, bias_sums, emit)


def vector_sums(small, sums, gy):
    ag1, ab1, ag2, ab2, ag3, ab3 = sums
    width, inner = ag1.shape[0], ag2.shape[0]
    g1, g2, g3 = small[0:1, 0:width], small[3:4, 0:inner], small[5:6, 0:inner]
    bias = nt(jnp.ones((16, gy.shape[1]), BF), gy[...])[0:1]
    pairs = ((ag1, g1), (ab1, g1), (ag2, g2), (ag3, g3), (ab2, g2), (ab3, g3))
    return [row_sums(acc[...]) / gain for acc, gain in pairs] + [bias]


def start_all(copies):
    for copy in copies:
        copy.start()


def prepare_kernel(rows, gin, bin_, gmid, bmid, out_bias, dilation, send, small, sem):
    section = lax.axis_index("section")
    copy = pltpu.make_async_copy(rows.at[1 - section], send, sem)
    copy.start()
    width, inner = gin.shape[1], gmid.shape[1]
    small[...] = jnp.zeros_like(small)
    for row, ref in ((0, gin), (1, bin_), (2, out_bias)):
        small[row : row + 1, 0:width] = ref[...]
    for row, ref, which in ((3, gmid, 0), (4, bmid, 0), (5, gmid, 1), (6, bmid, 1)):
        small[row : row + 1, 0:inner] = ref[which : which + 1, :]
    small[7:8, :] = jnp.full((1, small.shape[1]), dilation[0].astype(F32), F32)
    copy.wait()


def prepare(rows, gin, bin_, gmid, bmid, out_bias, dilation):
    return pl.pallas_call(
        prepare_kernel,
        in_specs=[ANY] + [VMEM] * 5 + [SMEM],
        out_specs=[VMEM, VMEM],
        out_shape=[shape(rows.shape[1:], BF), shape((SMALL_ROWS, rows.shape[1]), F32)],
        scratch_shapes=[pltpu.SemaphoreType.DMA],
        name="prepare",
    )(rows, gin, bin_, gmid, bmid, out_bias, dilation)


def kept_shapes(taps, width, inner, tokens):
    wide, narrow = (width, tokens), (inner, tokens)
    return [
        (wide, BF), (wide, BF), ((8, tokens), F32), (narrow, BF), (narrow, BF), (narrow, BF), (narrow, BF),
        (wide, BF), ((inner * taps, tokens), BF), (narrow, BF),
    ]


def column_shapes(width, inner):
    return [(width, LANES)] * 2 + [(inner, LANES)] * 4 + [(width, LANES)]


def sum_shapes(width, inner):
    return [(width, LANES)] * 2 + [(inner, LANES)] * 4


def main_kernel(taps_of, groups, *refs):
    refs = list(refs)

    def take(number):
        taken = refs[:number]
        del refs[:number]
        return taken

    seq, rows, got, small_own, small_got = take(5)
    own_w, got_w = take(3), take(3)
    outs, send_y, grad_out, keep_buf, send_buf = take(5)
    kept_out = take(10)
    x, cot = take(2)
    enc_w, dec_w = take(3), take(3)
    small = take(2)
    enc_kept, dec_kept = take(10), take(10)
    cols = take(7)
    hmid, prod, y_enc, gx, w_out_t, conv_t, w_in, conv_w, grad_mixed, grad_projected, moved, buf = take(12)
    sums = take(6)
    vec, sem = take(2)

    section = lax.axis_index("section")
    index = lax.axis_index("dp")
    leading = section == 0
    width, tokens = x.shape
    inner = hmid.shape[0]
    flag = leading.astype(F32)
    small[0][...] = small_own[...] * flag + small_got[...] * (1.0 - flag)
    small[1][...] = small_own[...] * (1.0 - flag) + small_got[...] * flag
    dilation = [jnp.max(member[7:8, 0:LANES]).astype(jnp.int32) for member in small]

    def begins(unit):
        return seq[section, unit]

    loads = [(x, rows.at[0], got), (enc_w[0], own_w[0], got_w[0]), (enc_w[2], own_w[2], got_w[2])]
    loads += [(enc_w[1], own_w[1], got_w[1]), (dec_w[0], got_w[0], own_w[0]), (dec_w[1], got_w[1], own_w[1])]
    loads += [(dec_w[2], got_w[2].at[0 : taps_of[1]], own_w[2].at[0 : taps_of[1]]), (cot, got, rows.at[1])]

    def load(at):
        target, first, second = loads[at]
        pl.when(leading)(pltpu.make_async_copy(first, target, sem.at[at]).start)
        pl.when(jnp.logical_not(leading))(pltpu.make_async_copy(second, target, sem.at[at]).start)

    for at in range(4):
        load(at)

    def ready(at):
        pltpu.make_async_copy(loads[at][1], loads[at][0], sem.at[at]).wait()

    fill_columns(small[0], cols)
    ready(0)
    ready(1)
    ready(2)
    for k in range(taps_of[0]):
        conv_t[:, inner * k : inner * (k + 1)] = enc_w[2][k].T
    ready(3)
    w_out_t[...] = enc_w[1][...].T
    for at in range(4, 8):
        load(at)
    forward_block(
        taps_of[0], begins, dilation[0], x, y_enc, (enc_w[0], w_out_t, conv_t), cols, enc_kept, hmid, prod
    )
    saves = [pltpu.make_async_copy(a, b, sem.at[8 + i]) for i, (a, b) in enumerate(zip(enc_kept, kept_out))]
    start_all(saves)

    fill_columns(small[1], cols)
    for at in range(4, 8):
        ready(at)
    for k in range(taps_of[1]):
        conv_t[:, inner * k : inner * (k + 1)] = dec_w[2][k].T
        conv_w[:, inner * k : inner * (k + 1)] = dec_w[2][k]
    w_out_t[...] = dec_w[1][...].T
    w_in[...] = dec_w[0][...].T
    y_dec = x
    forward_block(
        taps_of[1], begins, dilation[1], y_enc, y_dec, (dec_w[0], w_out_t, conv_t), cols, dec_kept, hmid, prod
    )
    pl.when(leading)(pltpu.make_async_copy(y_enc, outs.at[0], sem.at[18]).start)
    pl.when(leading)(pltpu.make_async_copy(y_dec, send_y, sem.at[19]).start)
    pl.when(jnp.logical_not(leading))(pltpu.make_async_copy(y_dec, outs.at[1], sem.at[18]).start)
    pl.when(jnp.logical_not(leading))(pltpu.make_async_copy(y_enc, send_y, sem.at[19]).start)

    n1, s1, r, n2, s2, n3, s3, hin, shifted, hout = dec_kept
    ag1, ab1, ag2, ab2, ag3, ab3 = sums
    w_in_at, vec_at, end = layout(taps_of[1], width, inner)[2:]
    back_third(cot, dec_w[1], (n3, s3, r), prod, grad_mixed, ag3, ab3)
    put_slabs(buf, 0, nt(hout[...], cot[...]))
    put_taps(buf, taps_of[1], width, shifted, grad_mixed)
    back_second(
        taps_of[1], begins, dilation[1], conv_w, (n2, s2, r), prod, grad_mixed, moved, grad_projected, ag2, ab2
    )
    put_slabs(buf, w_in_at, nt(grad_projected[...], hin[...]))
    back_first(cot, w_in, (n1, s1, r), prod, grad_projected, gx, ag1, ab1)
    put_vectors(buf, vec_at, vec, vector_sums(small[1], sums, cot))
    if buf.shape[0] > end:
        buf[end:, :] = jnp.zeros((buf.shape[0] - end, LANES), BF)
    send_out(buf, keep_buf, send_buf, section, index, groups, sem.at[21:23])
    last = pltpu.make_async_copy(gx, grad_out, sem.at[20])
    last.start()
    send_wait(buf, keep_buf, send_buf, sem.at[21:23])
    for copy in saves + [last]:
        copy.wait()
    pltpu.make_async_copy(y_enc, outs.at[0], sem.at[18]).wait()
    pltpu.make_async_copy(y_dec, send_y, sem.at[19]).wait()


def main_call(taps_of, groups, seq, rows, got, small_own, small_got, own_w, got_w):
    _, width, tokens = rows.shape
    inner = own_w[1].shape[0]
    half = padded_rows(taps_of[1], width, inner, groups) // 2
    wide, narrow = (width, tokens), (inner, tokens)
    weight_shapes = [(inner, width), (inner, width)]
    scratch = [(wide, BF)] * 2
    for taps in taps_of:
        scratch += [(dims, BF) for dims in weight_shapes + [(taps, inner, inner)]]
    scratch += [((SMALL_ROWS, width), F32)] * 2
    scratch += kept_shapes(taps_of[0], width, inner, tokens) + kept_shapes(taps_of[1], width, inner, tokens)
    scratch += [(dims, F32) for dims in column_shapes(width, inner)]
    scratch += [
        (narrow, BF), (wide, F32), (wide, BF), (wide, BF), ((width, inner), BF), ((inner, inner * taps_of[0]), BF),
        ((width, inner), BF), ((inner, inner * taps_of[1]), BF), (narrow, BF), (narrow, BF),
        ((inner * taps_of[1], tokens), BF), ((2 * half, LANES), BF),
    ]
    scratch += [(dims, F32) for dims in sum_shapes(width, inner)]
    scratch += [((VEC_ROWS, LANES), F32)]
    outs = [shape((2,) + wide, BF), shape(wide, BF), shape(wide, BF), shape((half, LANES), BF), shape((half, LANES), BF)]
    outs += [shape(dims, dtype) for dims, dtype in kept_shapes(taps_of[0], width, inner, tokens)]
    flops = 2 * tokens * inner * (2 * width + taps_of[0] * inner + 3 * (2 * width + taps_of[1] * inner))
    return pl.pallas_call(
        functools.partial(main_kernel, taps_of, groups),
        in_specs=[SMEM, ANY, ANY, VMEM, VMEM] + [ANY] * 6,
        out_specs=[ANY] * len(outs),
        out_shape=outs,
        scratch_shapes=[pltpu.VMEM(dims, dtype) for dims, dtype in scratch] + [pltpu.SemaphoreType.DMA((23,))],
        compiler_params=pltpu.CompilerParams(vmem_limit_bytes=VMEM_LIMIT),
        cost_estimate=pl.CostEstimate(flops=4 * flops, bytes_accessed=60 * 2**20, transcendentals=0),
        name="main_blocks",
    )(seq, rows, got, small_own, small_got, *own_w, *got_w)


def upper_kernel(
    taps,
    gy_in, n3_in, s3_in, r_in, shifted_in, hout_in, own_w, got_w,
    part, grad_mixed_out, ag3, ab3,
    gy, n3, s3, r, shifted, hout, w_out, prod, grad_mixed, buf, sem,
):
    leading = lax.axis_index("section") == 0
    width = gy.shape[0]
    pl.when(leading)(pltpu.make_async_copy(own_w, w_out, sem.at[0]).start)
    pl.when(jnp.logical_not(leading))(pltpu.make_async_copy(got_w, w_out, sem.at[0]).start)
    pairs = ((gy_in, gy), (s3_in, s3), (n3_in, n3), (r_in, r), (hout_in, hout), (shifted_in, shifted))
    loads = [pltpu.make_async_copy(a, b, sem.at[1 + i]) for i, (a, b) in enumerate(pairs)]
    start_all(loads)
    pltpu.make_async_copy(own_w, w_out, sem.at[0]).wait()
    for copy in loads[:4]:
        copy.wait()
    back_third(gy, w_out, (n3, s3, r), prod, grad_mixed, ag3, ab3)
    out = pltpu.make_async_copy(grad_mixed, grad_mixed_out, sem.at[7])
    out.start()
    loads[4].wait()
    put_slabs(buf, 0, nt(hout[...], gy[...]))
    loads[5].wait()
    put_taps(buf, taps, width, shifted, grad_mixed)
    save = pltpu.make_async_copy(buf, part, sem.at[8])
    save.start()
    save.wait()
    out.wait()


def upper_call(taps, gy, kept, own_w, got_w):
    width, tokens = gy.shape
    inner = own_w.shape[0]
    n1, s1, r, n2, s2, n3, s3, hin, shifted, hout = kept
    rows = layout(taps, width, inner)[2]
    wide, narrow = (width, tokens), (inner, tokens)
    scratch = [
        (wide, BF), (narrow, BF), (narrow, BF), ((8, tokens), F32), ((inner * taps, tokens), BF), (narrow, BF),
        ((inner, width), BF), (narrow, F32), (narrow, BF), ((rows, LANES), BF),
    ]
    flops = 2 * tokens * inner * (2 * width + taps * inner)
    return pl.pallas_call(
        functools.partial(upper_kernel, taps),
        in_specs=[ANY] * 8,
        out_specs=[ANY, ANY, VMEM, VMEM],
        out_shape=[shape((rows, LANES), BF), shape(narrow, BF), shape((inner, LANES), F32), shape((inner, LANES), F32)],
        scratch_shapes=[pltpu.VMEM(dims, dtype) for dims, dtype in scratch] + [pltpu.SemaphoreType.DMA((9,))],
        compiler_params=pltpu.CompilerParams(vmem_limit_bytes=VMEM_LIMIT),
        cost_estimate=pl.CostEstimate(flops=4 * flops, bytes_accessed=20 * 2**20, transcendentals=0),
        name="upper_encoder",
    )(gy, n3, s3, r, shifted, hout, own_w, got_w)


def lower_kernel(
    taps, groups,
    seq, gy_in, grad_mixed_in, part, ag3, ab3, small_own, small_got, n1_in, s1_in, r_in, n2_in, s2_in, hin_in,
    own_in, own_conv, got_in, got_conv,
    outs, send_gx, keep_buf, send_buf,
    gy, grad_mixed, n1, s1, r, n2, s2, hin, w_in_t, conv, w_in, conv_w, prod, moved, grad_projected, gx, buf,
    ag1, ab1, ag2, ab2, vec, sem,
):
    section = lax.axis_index("section")
    index = lax.axis_index("dp")
    leading = section == 0
    other = jnp.logical_not(leading)
    width, tokens = gy.shape
    inner = grad_mixed.shape[0]
    for at, (first, second, target) in enumerate(((own_conv, got_conv, conv), (own_in, got_in, w_in_t))):
        pl.when(leading)(pltpu.make_async_copy(first, target, sem.at[at]).start)
        pl.when(other)(pltpu.make_async_copy(second, target, sem.at[at]).start)
    w_in_at, vec_at, end = layout(taps, width, inner)[2:]
    pairs = (
        (grad_mixed_in, grad_mixed), (n2_in, n2), (s2_in, s2), (r_in, r), (hin_in, hin), (n1_in, n1), (s1_in, s1),
        (gy_in, gy), (part, buf.at[0:w_in_at]),
    )
    loads = [pltpu.make_async_copy(a, b, sem.at[2 + i]) for i, (a, b) in enumerate(pairs)]
    start_all(loads)
    flag = leading.astype(F32)
    small = small_own[...] * flag + small_got[...] * (1.0 - flag)
    dilation = jnp.max(small[7:8, 0:LANES]).astype(jnp.int32)
    pltpu.make_async_copy(own_conv, conv, sem.at[0]).wait()
    for k in range(taps):
        conv_w[:, inner * k : inner * (k + 1)] = conv[k]
    for copy in loads[:4]:
        copy.wait()

    def begins(unit):
        return seq[section, unit]

    back_second(taps, begins, dilation, conv_w, (n2, s2, r), prod, grad_mixed, moved, grad_projected, ag2, ab2)
    loads[4].wait()
    put_slabs(buf, w_in_at, nt(grad_projected[...], hin[...]))
    pltpu.make_async_copy(own_in, w_in_t, sem.at[1]).wait()
    w_in[...] = w_in_t[...].T
    for copy in loads[5:]:
        copy.wait()
    back_first(gy, w_in, (n1, s1, r), prod, grad_projected, gx, ag1, ab1)
    put_vectors(buf, vec_at, vec, vector_sums(small, (ag1, ab1, ag2, ab2, ag3, ab3), gy))
    if buf.shape[0] > end:
        buf[end:, :] = jnp.zeros((buf.shape[0] - end, LANES), BF)
    send_out(buf, keep_buf, send_buf, section, index, groups, sem.at[13:15])
    pl.when(leading)(pltpu.make_async_copy(gx, outs.at[0], sem.at[11]).start)
    pl.when(leading)(pltpu.make_async_copy(gy, send_gx, sem.at[12]).start)
    pl.when(other)(pltpu.make_async_copy(gy, outs.at[1], sem.at[11]).start)
    pl.when(other)(pltpu.make_async_copy(gx, send_gx, sem.at[12]).start)
    send_wait(buf, keep_buf, send_buf, sem.at[13:15])
    pltpu.make_async_copy(gx, outs.at[0], sem.at[11]).wait()
    pltpu.make_async_copy(gy, send_gx, sem.at[12]).wait()


def lower_call(taps, groups, seq, gy, upper, kept, small_own, small_got, own_w, got_w):
    width, tokens = gy.shape
    part, grad_mixed, ag3, ab3 = upper
    n1, s1, r, n2, s2, n3, s3, hin, shifted, hout = kept
    inner = grad_mixed.shape[0]
    half = padded_rows(taps, width, inner, groups) // 2
    wide, narrow = (width, tokens), (inner, tokens)
    scratch = [
        (wide, BF), (narrow, BF), (wide, BF), (wide, BF), ((8, tokens), F32), (narrow, BF), (narrow, BF), (wide, BF),
        ((inner, width), BF), ((taps, inner, inner), BF), ((width, inner), BF), ((inner, inner * taps), BF),
        (wide, F32), ((inner * taps, tokens), BF), (narrow, BF), (wide, BF), ((2 * half, LANES), BF),
    ]
    scratch += [(dims, F32) for dims in sum_shapes(width, inner)[:4]]
    scratch += [((VEC_ROWS, LANES), F32)]
    outs = [shape((2,) + wide, BF), shape(wide, BF), shape((half, LANES), BF), shape((half, LANES), BF)]
    flops = 2 * tokens * inner * (2 * width + taps * inner)
    return pl.pallas_call(
        functools.partial(lower_kernel, taps, groups),
        in_specs=[SMEM, ANY, ANY, ANY, VMEM, VMEM, VMEM, VMEM] + [ANY] * 10,
        out_specs=[ANY] * 4,
        out_shape=outs,
        scratch_shapes=[pltpu.VMEM(dims, dtype) for dims, dtype in scratch] + [pltpu.SemaphoreType.DMA((15,))],
        compiler_params=pltpu.CompilerParams(vmem_limit_bytes=VMEM_LIMIT),
        cost_estimate=pl.CostEstimate(flops=4 * flops, bytes_accessed=20 * 2**20, transcendentals=0),
        name="lower_encoder",
    )(
        seq, gy, grad_mixed, part, ag3, ab3, small_own, small_got, n1, s1, r, n2, s2, hin,
        own_w[0], own_w[2], got_w[0], got_w[2],
    )


def unpack_kernel(taps_of, groups_of, *refs):
    refs = list(refs)

    def take(number):
        taken = refs[:number]
        del refs[:number]
        return taken

    own_of, got_of = [], []
    for _ in range(2):
        own_of.append(take(2))
        got_of.append(take(2))
    w_in_t, w_out, conv, gin, bin_, gmid, bmid, out_bias, buf, sem = refs
    inner, width = w_out.shape
    whole = inner // LANES
    tail = inner - whole * LANES
    slots = conv.shape[0]
    section = lax.axis_index("section")
    index = lax.axis_index("dp")

    def write(taps, groups, own, got):
        rows = own[0].shape[0]
        count = share_count(groups[0])
        share = 2 * rows // count

        def body(position, _):
            for which, (pieces, side) in enumerate(((own, section), (got, 1 - section))):
                for at, ref in enumerate(pieces):
                    owner = owner_of(position + at * (count // 2), side, groups, index)
                    start = side * (2 * rows) + owner * share
                    pltpu.make_async_copy(
                        ref.at[pl.ds(pl.multiple_of(position * share, 16), share)],
                        buf.at[pl.ds(pl.multiple_of(start, 16), share)],
                        sem.at[2 * which + at],
                    ).start()
            return 0

        lax.fori_loop(0, count // 2, body, 0)
        for which, pieces in enumerate((own, got)):
            for at, ref in enumerate(pieces):
                pltpu.make_async_copy(ref, buf.at[pl.ds(0, rows)], sem.at[2 * which + at]).wait()
        taps_at, tails_at, w_in_at, vec_at, _ = layout(taps, width, inner)

        def wide(target, row):
            for at in range(0, width, LANES):
                q = at // LANES
                size = min(LANES, width - at)
                target[:, at : at + size] = buf[row + q * inner : row + (q + 1) * inner, 0:size].astype(F32)

        wide(w_out, 0)
        wide(w_in_t, w_in_at)
        tails = buf[tails_at : tails_at + inner, :].astype(F32)
        for k in range(slots):
            if k >= taps:
                conv[k] = jnp.zeros((inner, inner), F32)
                continue
            for q in range(whole):
                at = taps_at + inner * (whole * k + q)
                conv[k, :, LANES * q : LANES * (q + 1)] = buf[at : at + inner, :].astype(F32)
            conv[k, :, LANES * whole :] = tails[:, tail * k : tail * (k + 1)]
        vec = buf[vec_at : vec_at + VEC_ROWS, :].astype(F32)
        row = 0
        for target, member in ((gin, 0), (bin_, 0), (gmid, 0), (gmid, 1), (bmid, 0), (bmid, 1), (out_bias, 0)):
            for at in range(0, target.shape[1], LANES):
                size = min(LANES, target.shape[1] - at)
                target[member : member + 1, at : at + size] = vec[row : row + 1, 0:size]
                row += 1

    pl.when(section == 0)(lambda: write(taps_of[0], groups_of[0], own_of[0], got_of[0]))
    pl.when(section != 0)(lambda: write(taps_of[1], groups_of[1], own_of[1], got_of[1]))


def unpack(taps_of, groups_of, enc, dec, width, inner):
    pieces = enc[0] + enc[1] + dec[0] + dec[1]
    rows = max(4 * part[0].shape[0] for part in (enc[0], dec[0]))
    return pl.pallas_call(
        functools.partial(unpack_kernel, taps_of, groups_of),
        in_specs=[ANY] * len(pieces),
        out_specs=[VMEM] * 8,
        out_shape=[
            shape((inner, width), F32), shape((inner, width), F32), shape((taps_of[0], inner, inner), F32),
            shape((1, width), F32), shape((1, width), F32), shape((2, inner), F32), shape((2, inner), F32),
            shape((1, width), F32),
        ],
        scratch_shapes=[pltpu.VMEM((rows, LANES), BF), pltpu.SemaphoreType.DMA((4,))],
        compiler_params=pltpu.CompilerParams(vmem_limit_bytes=VMEM_LIMIT),
        name="unpack",
    )(*pieces)


def swap_sections(value):
    return lax.ppermute(value, "section", [(0, 1), (1, 0)])


def swap_dp(value, masks):
    count = lax.axis_size("dp")
    pairs = [(s * count + i, s * count + (i ^ masks[s])) for s in range(2) for i in range(count)]
    return lax.ppermute(value, ("section", "dp"), pairs)


def rounded_sum(terms, rows):
    total = terms[0][rows].astype(F32)
    for term in terms[1:]:
        total = total + term[rows].astype(F32)
    return total.astype(BF)


def masks_of(bits, other):
    return [other << own[0] for own in bits]


def reduce_all(keep, send, groups, receiver):
    count = lax.axis_size("dp")
    steps = list(zip(*groups))
    terms = [keep, swap_sections(send)]
    for bits in steps:
        size = terms[0].shape[0] >> len(bits[0])
        came = []
        for other in range(1, 2 ** len(bits[0])):
            part = rounded_sum(terms, slice(other * size, (other + 1) * size))
            came.append(swap_dp(part, masks_of(bits, other)))
        terms = [term[:size] for term in terms] + came
    value = rounded_sum(terms, slice(None))
    for bit in range(sum(len(bits) for bits in groups[0]), count.bit_length() - 1):
        value = rounded_sum([value, swap_dp(value, [1 << bit] * 2)], slice(None))
    pieces = [value]
    for bits in reversed(steps):
        if len(pieces) > 1:
            value = jnp.concatenate(pieces, 0)
        pieces = [value] + [swap_dp(value, masks_of(bits, other)) for other in range(1, 2 ** len(bits[0]))]
    pairs = [(1 - receiver, receiver)]
    return pieces, [lax.ppermute(piece, "section", pairs) for piece in pieces]


def shards(
    section_inputs,
    seq_lengths,
    dilations,
    gains_in,
    biases_in,
    gains_mid,
    biases_mid,
    out_bias,
    w_in,
    w_out,
    conv_taps,
):
    section = lax.axis_index("section")
    count = lax.axis_size("dp")
    groups_of = (scatter_groups(count, True), scatter_groups(count, False))
    rows = jnp.swapaxes(section_inputs[0], 1, 2)
    width = rows.shape[1]
    inner = w_out.shape[1]
    taps_of = (conv_taps.shape[1], DEC_TAPS)

    own_w = (jnp.swapaxes(w_in[0], 0, 1), w_out[0], conv_taps[0])
    send_rows, small = prepare(rows, gains_in, biases_in, gains_mid[0], biases_mid[0], out_bias, dilations)
    got_rows = swap_sections(send_rows)
    got_small = swap_sections(small)
    got_w = tuple(swap_sections(member) for member in own_w)

    outs, send_y, grad_dec, keep_dec, send_dec, *kept = main_call(
        taps_of, groups_of[1], seq_lengths, rows, got_rows, small, got_small, own_w, got_w
    )
    got_y = swap_sections(send_y)
    dec = reduce_all(keep_dec, send_dec, groups_of[1], 1)
    upper = upper_call(taps_of[0], grad_dec, kept, own_w[1], got_w[1])
    grads_x, send_gx, keep_enc, send_enc = lower_call(
        taps_of[0], groups_of[0], seq_lengths, grad_dec, upper, kept, small, got_small, own_w, got_w
    )
    enc = reduce_all(keep_enc, send_enc, groups_of[0], 0)
    got_gx = swap_sections(send_gx)

    def joined(pair, got):
        pair = lax.dynamic_update_slice_in_dim(pair, got[None], 1 - section, 0)
        return jnp.swapaxes(pair, 1, 2)[None]

    grads = unpack(taps_of, groups_of, enc, dec, width, inner)
    return (
        joined(outs, got_y),
        joined(grads_x, got_gx),
        grads[3],
        grads[4],
        grads[5][None],
        grads[6][None],
        grads[7],
        jnp.swapaxes(grads[0], 0, 1)[None],
        grads[1][None],
        grads[2][None],
    )


def solution(mesh):
    in_specs = (
        P("section", None, "dp", None),
        P(None, "dp"),
        P("section"),
        P("section", None),
        P("section", None),
        P("section", None, None),
        P("section", None, None),
        P("section", None),
        P("section", None, None),
        P("section", None, None),
        P("section", None, None, None),
    )
    out_specs = (
        P("section", None, "dp", None),
        P("section", None, "dp", None),
        P("section", None),
        P("section", None),
        P("section", None, None),
        P("section", None, None),
        P("section", None),
        P("section", None, None),
        P("section", None, None),
        P("section", None, None, None),
    )
    return jax.shard_map(shards, mesh=mesh, in_specs=in_specs, out_specs=out_specs, check_vma=False)
```

```python
import functools

import jax
import jax.numpy as jnp
from jax import lax
from jax.experimental import pallas as pl
from jax.experimental.pallas import tpu as pltpu
from jax.sharding import PartitionSpec as P

DEC_TAPS = 3
EPS = 1e-05
LANES = 128
CHUNK = 80
VEC_ROWS = 48
SMALL_ROWS = 8
PIECES = 5
BF = jnp.bfloat16
F32 = jnp.float32
VMEM_LIMIT = 62 * 2**20
SMALL_LIMIT = 62 * 2**20
SEQ = "ddedeydexdede"
ANY = pl.BlockSpec(memory_space=pl.ANY)
SMEM = pl.BlockSpec(memory_space=pltpu.SMEM)
VMEM = pl.BlockSpec(memory_space=pltpu.VMEM)


def shape(dims, dtype):
    return jax.ShapeDtypeStruct(tuple(dims), dtype)


def nn(left, right):
    return jnp.dot(left, right, preferred_element_type=F32)


def nt(left, right):
    return lax.dot_general(left, right, (((1,), (1,)), ((), ())), preferred_element_type=F32)


def tn(left, right):
    return lax.dot_general(left, right, (((0,), (0,)), ((), ())), preferred_element_type=F32)


def lane_block(index):
    return pl.ds(pl.multiple_of(index * LANES, LANES), LANES)


def chunks(rows):
    size = CHUNK if rows % CHUNK == 0 else 16
    return [slice(at, at + size) for at in range(0, rows, size)]


def folded(values):
    return jnp.sum(values.reshape(values.shape[0] // 8, 8, values.shape[1]), 0)


def column(vector):
    return jnp.broadcast_to(vector, (LANES, vector.shape[1])).T


def norm_forward(source, half_gain, half_bias, normed, slope, hidden, devs, row):
    feats, tokens = source.shape
    scale = 1.0 / feats

    def stats(unit):
        here = lane_block(unit)
        base = source[0:1, here].astype(F32)
        total = jnp.zeros((8, LANES), F32)
        squares = jnp.zeros((8, LANES), F32)
        for part in chunks(feats):
            moved = source[part, here].astype(F32) - base
            total = total + folded(moved)
            squares = squares + folded(moved * moved)
        average = jnp.sum(total, 0, keepdims=True) * scale
        variance = jnp.sum(squares, 0, keepdims=True) * scale - average * average
        inverse_dev = lax.rsqrt(jnp.maximum(variance, 0.0) + EPS)
        return (average + base) * inverse_dev, inverse_dev

    def body(unit, carry):
        following = stats(jnp.minimum(unit + 1, tokens // LANES - 1))
        offset, inverse_dev = carry
        here = lane_block(unit)
        devs[row : row + 1, here] = inverse_dev
        for part in chunks(feats):
            values = source[part, here].astype(F32) * inverse_dev - offset
            gain = half_gain[part, :]
            half = values * gain + half_bias[part, :]
            tan = jnp.tanh(half)
            weight = 1.0 + tan
            out = half * weight
            normed[part, here] = values.astype(BF)
            slope[part, here] = ((weight + out * (1.0 - tan)) * gain).astype(BF)
            hidden[part, here] = out.astype(hidden.dtype)
        return following

    lax.fori_loop(0, tokens // LANES, body, stats(0))


def norm_backward(gradient, slope, normed, devs, row, gain_sums, bias_sums, means, emit):
    feats, tokens = gradient.shape
    units = tokens // LANES
    scale = 1.0 / feats
    size = CHUNK if feats % CHUNK == 0 else 16
    means[...] = jnp.zeros_like(means)

    def collect(index, _):
        rows = pl.ds(pl.multiple_of(index * size, 16), size)
        gain_sum = jnp.zeros((size, LANES), F32)
        bias_sum = jnp.zeros((size, LANES), F32)
        for unit in range(units):
            here = slice(unit * LANES, (unit + 1) * LANES)
            scaled = gradient[rows, here] * slope[rows, here].astype(F32)
            weighted = scaled * normed[rows, here].astype(F32)
            gain_sum = gain_sum + weighted
            bias_sum = bias_sum + scaled
            means[0:8, here] += folded(scaled)
            means[8:16, here] += folded(weighted)
        gain_sums[rows, :] = gain_sum
        bias_sums[rows, :] = bias_sum
        return 0

    lax.fori_loop(0, feats // size, collect, 0)

    def finish(unit, _):
        here = lane_block(unit)
        inverse_dev = devs[row : row + 1, here]
        first = jnp.sum(means[0:8, here], 0, keepdims=True) * (scale * inverse_dev)
        second = jnp.sum(means[8:16, here], 0, keepdims=True) * (scale * inverse_dev)
        for part in chunks(feats):
            scaled = gradient[part, here] * slope[part, here].astype(F32)
            emit(part, here, scaled * inverse_dev - first - normed[part, here].astype(F32) * second)
        return 0

    lax.fori_loop(0, units, finish, 0, unroll=2)


def write_shifts(source, target, begins, offsets):
    feats, tokens = source.shape
    units = tokens // LANES

    def body(unit, _):
        here = lane_block(unit)
        behind_unit = jnp.maximum(unit - 1, 0)
        ahead_unit = jnp.minimum(unit + 1, units - 1)
        joined_behind = ((unit > 0) & (begins(unit) == 0)).astype(F32)
        joined_ahead = ((unit < units - 1) & (begins(ahead_unit) == 0)).astype(F32)
        for part in chunks(feats):
            size = part.stop - part.start
            lane = lax.broadcasted_iota(jnp.int32, (size, LANES), 1)
            current = source[part, here].astype(F32)
            behind = source[part, lane_block(behind_unit)].astype(F32) * joined_behind
            ahead = source[part, lane_block(ahead_unit)].astype(F32) * joined_ahead
            for position, (sign, step) in enumerate(offsets):
                if sign == 0:
                    moved = current
                elif sign < 0:
                    moved = pltpu.roll(jnp.where(lane < LANES - step, current, behind), step, 1)
                else:
                    moved = pltpu.roll(jnp.where(lane >= step, current, ahead), LANES - step, 1)
                target[feats * position + part.start : feats * position + part.stop, here] = moved.astype(BF)
        return 0

    lax.fori_loop(0, units, body, 0, unroll=2)


def tap_offsets(taps, dilation, flip):
    result = []
    for position in range(taps):
        factor = (position - 2) * (-1 if flip else 1)
        result.append(((factor > 0) - (factor < 0), abs(factor) * dilation))
    return result


def layout(taps, width, inner):
    wide = pl.cdiv(width, LANES) * inner
    taps_at = wide
    tails_at = taps_at + taps * (inner // LANES) * inner
    w_in_at = tails_at + inner
    vec_at = w_in_at + wide
    return taps_at, tails_at, w_in_at, vec_at, vec_at + VEC_ROWS


def scatter_groups(count, full):
    total = count.bit_length() - 1
    rest = [list(range(2, min(4, total)))] if full and total > 2 else []
    return [[[bit] for bit in bits if bit < total] + rest for bits in ((0, 1), (1, 0))]


def share_count(groups):
    return 2 ** sum(len(bits) for bits in groups)


def padded_rows(rows, groups):
    unit = 2 * 16 * share_count(groups[0])
    return pl.cdiv(rows, unit) * unit


def put_slabs(buf, row, matrix):
    rows, cols = matrix.shape
    for q in range(pl.cdiv(cols, LANES)):
        part = matrix[:, LANES * q : min(cols, LANES * (q + 1))]
        if part.shape[1] < LANES:
            part = jnp.concatenate([part, jnp.zeros((rows, LANES - part.shape[1]), F32)], 1)
        buf[row + q * rows : row + (q + 1) * rows, :] = part.astype(BF)


def put_taps(buf, taps, width, shifted, grad_mixed, ready):
    inner = grad_mixed.shape[0]
    taps_at, tails_at, _, _, _ = layout(taps, width, inner)
    whole = inner // LANES
    tail = inner - whole * LANES
    for k in range(taps):
        grad = nt(shifted[inner * k : inner * (k + 1), :], grad_mixed[...])
        for q in range(whole):
            at = taps_at + inner * (whole * k + q)
            buf[at : at + inner, :] = grad[:, LANES * q : LANES * (q + 1)].astype(BF)
        buf[tails_at : tails_at + inner, tail * k : tail * (k + 1)] = grad[:, LANES * whole :].astype(BF)
        if k == taps - 2:
            ready(taps_at, taps_at + inner * whole * (taps - 1))
    buf[tails_at : tails_at + inner, tail * taps :] = jnp.zeros((inner, LANES - tail * taps), BF)
    ready(taps_at + inner * whole * (taps - 1), tails_at + inner)


def row_sums(acc):
    return jnp.sum(acc.T, 0, keepdims=True)


def put_vectors(buf, at, vec, sums):
    vec[...] = jnp.zeros_like(vec)
    row = 0
    for total in sums:
        for lane in range(0, total.shape[1], LANES):
            part = total[:, lane : lane + LANES]
            vec[row : row + 1, 0 : part.shape[1]] = part
            row += 1
    buf[at : at + VEC_ROWS, :] = vec[...].astype(BF)


def relative_index(position, groups):
    result = 0
    for bits in reversed(groups):
        size = 2 ** len(bits)
        result = result + (position & (size - 1)) * 2 ** bits[0]
        position = position >> len(bits)
    return result


def owner_of(position, side, groups, index):
    both = [relative_index(position, order) for order in groups]
    mask = sum(2**bit for bits in groups[0] for bit in bits)
    return jnp.where(side == 0, both[0], both[1]) ^ (index & mask)


def position_of(owner, side, groups, index):
    distance = owner ^ index
    position = 0
    for bits in groups[side]:
        position = position * 2 ** len(bits) + ((distance >> bits[0]) & (2 ** len(bits) - 1))
    return position


class RowsOut:
    def __init__(self, buf, keep, send, section, index, groups, sems):
        self.buf, self.keep, self.send, self.sems = buf, keep, send, sems
        self.section, self.index, self.groups = section, index, groups
        self.count = share_count(groups[0])
        self.share = keep.shape[0] // self.count
        self.sizes = []

    def start(self, first, last):
        for number in range(2 * self.count):
            low, high = max(first, number * self.share), min(last, (number + 1) * self.share)
            if low >= high:
                continue
            side, owner = divmod(number, self.count)
            place = position_of(owner, side, self.groups, self.index) * self.share + (low - number * self.share)
            target = pl.ds(pl.multiple_of(place, 16), high - low)
            source = self.buf.at[low:high]
            sem = self.sems.at[len(self.sizes)]
            pl.when(self.section == side)(pltpu.make_async_copy(source, self.keep.at[target], sem).start)
            pl.when(self.section != side)(pltpu.make_async_copy(source, self.send.at[target], sem).start)
            self.sizes.append(high - low)

    def wait(self):
        for number, size in enumerate(self.sizes):
            source, target = self.buf.at[0:size], self.keep.at[0:size]
            pltpu.make_async_copy(source, target, self.sems.at[number]).wait()


def forward_block(taps, begins, dilation, x, y, weights, cols, kept, hmid, prod):
    w_in_t, w_out, conv = weights
    g1, b1, g2, b2, g3, b3, ob = cols
    n1, s1, r, n2, s2, n3, s3, hin, shifted, hout = kept
    inner, tokens = hmid.shape
    narrow = prod.at[0:inner]
    norm_forward(x, g1, b1, n1, s1, hin, r, 0)
    narrow[...] = nn(w_in_t[...], hin[...])
    norm_forward(narrow, g2, b2, n2, s2, hmid, r, 1)
    write_shifts(hmid, shifted, begins, tap_offsets(taps, dilation, False))
    narrow[...] = tn(conv[...].reshape(taps * inner, inner), shifted[...])
    norm_forward(narrow, g3, b3, n3, s3, hout, r, 2)
    bias = jnp.concatenate([ob[...]] * (tokens // LANES), 1)
    y[...] = (x[...].astype(F32) + tn(w_out[...], hout[...]) + bias).astype(BF)


def fill_columns(small, cols):
    g1, b1, g2, b2, g3, b3, ob = cols
    width, inner = g1.shape[0], g2.shape[0]
    for target, row, scale in ((g1, 0, 0.5), (b1, 1, 0.5), (ob, 2, 1.0)):
        target[...] = column(small[row : row + 1, 0:width] * scale)
    for target, row in ((g2, 3), (b2, 4), (g3, 5), (b3, 6)):
        target[...] = column(small[row : row + 1, 0:inner] * 0.5)


def back_third(gy, w_out, kept, prod, means, grad_mixed, gain_sums, bias_sums, ready):
    n3, s3, r = kept
    inner = w_out.shape[0]
    narrow = prod.at[0:inner]
    narrow[...] = nn(w_out[...], gy[...])
    ready()

    def emit(part, here, value):
        grad_mixed[part, here] = value.astype(BF)

    norm_backward(narrow, s3, n3, r, 2, gain_sums, bias_sums, means, emit)


def back_second(
    taps, begins, dilation, conv_w, kept, prod, means, grad_mixed, moved, grad_projected, gain_sums, bias_sums, ready,
    weights=None,
):
    n2, s2, r = kept
    inner = grad_mixed.shape[0]
    narrow = prod.at[0:inner]
    write_shifts(grad_mixed, moved, begins, tap_offsets(taps, dilation, True))
    if weights is not None:
        weights()
    narrow[...] = nn(conv_w[...], moved[...])
    ready()

    def emit(part, here, value):
        grad_projected[part, here] = value.astype(BF)

    norm_backward(narrow, s2, n2, r, 1, gain_sums, bias_sums, means, emit)


def back_first(gy, w_in_t, kept, prod, means, grad_projected, gx, gain_sums, bias_sums, ready):
    n1, s1, r = kept
    prod[...] = tn(w_in_t[...], grad_projected[...])
    ready()

    def emit(part, here, value):
        gx[part, here] = (gy[part, here].astype(F32) + value).astype(BF)

    norm_backward(prod, s1, n1, r, 0, gain_sums, bias_sums, means, emit)


def put_w_out(buf, hout_ones, gy):
    grad = nt(hout_ones[...], gy[...])
    inner = hout_ones.shape[0] - 16
    put_slabs(buf, 0, grad[0:inner])
    return grad[inner : inner + 1]


def gain_and_bias(gain, sums):
    return [row_sums(acc[...]) / gain for acc in sums]


def put_rows(target, rows):
    target[...] = jnp.zeros_like(target)
    for at, row in enumerate(rows):
        target[at : at + 1, 0 : row.shape[1]] = row


def gains_of(small, width, inner):
    return small[0:1, 0:width], small[3:4, 0:inner], small[5:6, 0:inner]


def pick_small(leading, own, got):
    flag = leading.astype(F32)
    return own[...] * flag + got[...] * (1.0 - flag)


def start_all(copies):
    for copy in copies:
        copy.start()


def prepare_kernel(rows, gin, bin_, gmid, bmid, out_bias, dilation, send, small, hold, sem):
    section = lax.axis_index("section")
    size = send.shape[0] // PIECES
    arrive = [pltpu.make_async_copy(rows.at[1 - section, size * i : size * (i + 1)], hold.at[i], sem.at[i]) for i in range(PIECES)]
    leave = [pltpu.make_async_copy(hold.at[i], send.at[size * i : size * (i + 1)], sem.at[PIECES + i]) for i in range(PIECES)]
    start_all(arrive)
    width, inner = gin.shape[1], gmid.shape[1]
    small[...] = jnp.zeros_like(small)
    for row, ref in ((0, gin), (1, bin_), (2, out_bias)):
        small[row : row + 1, 0:width] = ref[...]
    for row, ref, which in ((3, gmid, 0), (4, bmid, 0), (5, gmid, 1), (6, bmid, 1)):
        small[row : row + 1, 0:inner] = ref[which : which + 1, :]
    small[7:8, :] = jnp.full((1, small.shape[1]), dilation[0].astype(F32), F32)
    for come, go in zip(arrive, leave):
        come.wait()
        go.start()
    for go in leave:
        go.wait()


def prepare(rows, gin, bin_, gmid, bmid, out_bias, dilation):
    return pl.pallas_call(
        prepare_kernel,
        in_specs=[ANY] + [VMEM] * 5 + [SMEM],
        out_specs=[ANY, VMEM],
        out_shape=[shape(rows.shape[1:], BF), shape((SMALL_ROWS, rows.shape[1]), F32)],
        scratch_shapes=[
            pltpu.VMEM((PIECES, rows.shape[1] // PIECES, rows.shape[2]), BF), pltpu.SemaphoreType.DMA((2 * PIECES,))
        ],
        compiler_params=pltpu.CompilerParams(vmem_limit_bytes=VMEM_LIMIT),
        name="prepare",
    )(rows, gin, bin_, gmid, bmid, out_bias, dilation)


def kept_shapes(taps, width, inner, tokens):
    wide, narrow = (width, tokens), (inner, tokens)
    return [
        (wide, BF), (wide, BF), ((8, tokens), F32), (narrow, BF), (narrow, BF), (narrow, BF), (narrow, BF),
        (wide, BF), ((inner * taps, tokens), BF), (narrow, BF),
    ]


def column_shapes(width, inner):
    return [(width, LANES)] * 2 + [(inner, LANES)] * 4 + [(width, LANES)]


def main_kernel(taps_of, groups, *refs):
    refs = list(refs)

    def take(number):
        taken = refs[:number]
        del refs[:number]
        return taken

    seq, rows, got, small_own, small_got = take(5)
    own_w, got_w = take(3), take(3)
    outs, send_y, grad_out, keep_buf, send_buf, vec_out = take(6)
    kept_out = take(10)
    x, cot = take(2)
    enc_w, dec_w = take(3), take(3)
    small = take(2)
    enc_kept, dec_kept = take(10), take(10)
    cols = take(7)
    hmid, prod, means, y_enc, gx, conv_w, grad_mixed, grad_projected, moved, buf = take(10)
    ag1, ab1, ag2, ab2, ag3, ab3, vec, sem, row_sems = take(9)

    section = lax.axis_index("section")
    index = lax.axis_index("dp")
    leading = section == 0
    width, tokens = x.shape
    inner = hmid.shape[0]
    small[0][...] = pick_small(leading, small_own, small_got)
    small[1][...] = pick_small(leading, small_got, small_own)
    dilation = [jnp.max(member[7:8, 0:LANES]).astype(jnp.int32) for member in small]

    def begins(unit):
        return seq[section, unit]

    loads = [(x, rows.at[0], got), (enc_w[0], own_w[0], got_w[0]), (enc_w[2], own_w[2], got_w[2])]
    loads += [(enc_w[1], own_w[1], got_w[1]), (dec_w[0], got_w[0], own_w[0]), (dec_w[1], got_w[1], own_w[1])]
    loads += [(dec_w[2], got_w[2].at[0 : taps_of[1]], own_w[2].at[0 : taps_of[1]]), (cot, got, rows.at[1])]

    def load(at):
        target, first, second = loads[at]
        pl.when(leading)(pltpu.make_async_copy(first, target, sem.at[at]).start)
        pl.when(jnp.logical_not(leading))(pltpu.make_async_copy(second, target, sem.at[at]).start)

    for at in range(4):
        load(at)

    def ready(at):
        pltpu.make_async_copy(loads[at][1], loads[at][0], sem.at[at]).wait()

    fill_columns(small[0], cols)
    hout_ones = dec_kept[9]
    dec_kept[9] = hout_ones.at[0:inner]
    hout_ones[inner:, :] = jnp.ones((16, tokens), BF)
    for at in range(4):
        ready(at)
    for at in range(4, 8):
        load(at)
    forward_block(taps_of[0], begins, dilation[0], x, y_enc, enc_w, cols, enc_kept, hmid, prod)
    saves = [pltpu.make_async_copy(a, b, sem.at[8 + i]) for i, (a, b) in enumerate(zip(enc_kept, kept_out))]
    start_all(saves)

    fill_columns(small[1], cols)
    for at in range(4, 8):
        ready(at)
    for k in range(taps_of[1]):
        conv_w[:, inner * k : inner * (k + 1)] = dec_w[2][k]
    y_dec = x
    forward_block(taps_of[1], begins, dilation[1], y_enc, y_dec, dec_w, cols, dec_kept, hmid, prod)
    pl.when(leading)(pltpu.make_async_copy(y_enc, outs.at[0], sem.at[18]).start)
    pl.when(leading)(pltpu.make_async_copy(y_dec, send_y, sem.at[19]).start)
    pl.when(jnp.logical_not(leading))(pltpu.make_async_copy(y_dec, outs.at[1], sem.at[18]).start)
    pl.when(jnp.logical_not(leading))(pltpu.make_async_copy(y_enc, send_y, sem.at[19]).start)

    n1, s1, r, n2, s2, n3, s3, hin, shifted, hout = dec_kept
    rows_out = RowsOut(buf, keep_buf, send_buf, section, index, groups, row_sems)
    w_in_at, end = layout(taps_of[1], width, inner)[2:4]

    def nothing():
        pass

    back_third(cot, dec_w[1], (n3, s3, r), prod, means, grad_mixed, ag3, ab3, nothing)
    bias = put_w_out(buf, hout_ones, cot)
    rows_out.start(0, layout(taps_of[1], width, inner)[0])
    put_taps(buf, taps_of[1], width, shifted, grad_mixed, rows_out.start)
    back_second(
        taps_of[1], begins, dilation[1], conv_w, (n2, s2, r), prod, means, grad_mixed, moved, grad_projected, ag2, ab2,
        nothing,
    )
    put_slabs(buf, w_in_at, nt(grad_projected[...], hin[...]))
    rows_out.start(w_in_at, end)
    back_first(cot, dec_w[0], (n1, s1, r), prod, means, grad_projected, gx, ag1, ab1, nothing)
    last = pltpu.make_async_copy(gx, grad_out, sem.at[20])
    last.start()
    g1, g2, g3 = gains_of(small[1], width, inner)
    first, second, third = gain_and_bias(g1, (ag1, ab1)), gain_and_bias(g2, (ag2, ab2)), gain_and_bias(g3, (ag3, ab3))
    put_vectors(vec_out, 0, vec, first + [second[0], third[0], second[1], third[1], bias])
    rows_out.wait()
    wait_all(saves + [last])
    pltpu.make_async_copy(y_enc, outs.at[0], sem.at[18]).wait()
    pltpu.make_async_copy(y_dec, send_y, sem.at[19]).wait()


def main_call(taps_of, groups, seq, rows, got, small_own, small_got, own_w, got_w):
    _, width, tokens = rows.shape
    inner = own_w[1].shape[0]
    half = padded_rows(layout(taps_of[1], width, inner)[3], groups) // 2
    wide, narrow = (width, tokens), (inner, tokens)
    weight_shapes = [(inner, width), (inner, width)]
    scratch = [(wide, BF)] * 2
    for taps in taps_of:
        scratch += [(dims, BF) for dims in weight_shapes + [(taps, inner, inner)]]
    scratch += [((SMALL_ROWS, width), F32)] * 2
    scratch += kept_shapes(taps_of[0], width, inner, tokens) + kept_shapes(taps_of[1], width, inner, tokens)[:-1]
    scratch += [((inner + 16, tokens), BF)]
    scratch += [(dims, F32) for dims in column_shapes(width, inner)]
    scratch += [
        (narrow, BF), (wide, F32), ((16, tokens), F32), (wide, BF), (wide, BF), ((inner, inner * taps_of[1]), BF),
        (narrow, BF), (narrow, BF), ((inner * taps_of[1], tokens), BF), ((2 * half, LANES), BF),
    ]
    scratch += [((width, LANES), F32)] * 2 + [((inner, LANES), F32)] * 4 + [((VEC_ROWS, LANES), F32)]
    block = shape((half, LANES), BF)
    outs = [shape((2,) + wide, BF), shape(wide, BF), shape(wide, BF), block, block, shape((VEC_ROWS, LANES), BF)]
    outs += [shape(dims, dtype) for dims, dtype in kept_shapes(taps_of[0], width, inner, tokens)]
    flops = 2 * tokens * inner * (2 * width + taps_of[0] * inner + 3 * (2 * width + taps_of[1] * inner))
    return pl.pallas_call(
        functools.partial(main_kernel, taps_of, groups),
        in_specs=[SMEM, ANY, ANY, VMEM, VMEM] + [ANY] * 6,
        out_specs=[ANY] * 5 + [VMEM] + [ANY] * 10,
        out_shape=outs,
        scratch_shapes=[pltpu.VMEM(dims, dtype) for dims, dtype in scratch]
        + [pltpu.SemaphoreType.DMA((24,)), pltpu.SemaphoreType.DMA((8 * share_count(groups[0]),))],
        compiler_params=pltpu.CompilerParams(vmem_limit_bytes=VMEM_LIMIT),
        cost_estimate=pl.CostEstimate(flops=4 * flops, bytes_accessed=60 * 2**20, transcendentals=0),
        name="main_blocks",
    )(seq, rows, got, small_own, small_got, *own_w, *got_w)


def load_weight(leading, own, got, target, sem):
    pl.when(leading)(pltpu.make_async_copy(own, target, sem).start)
    pl.when(jnp.logical_not(leading))(pltpu.make_async_copy(got, target, sem).start)
    return pltpu.make_async_copy(own, target, sem)


def wait_all(copies):
    for copy in copies:
        copy.wait()


def encoder_kernel(
    taps, groups,
    seq, gy_in, small_own, small_got, n3_in, s3_in, r_in, shifted_in, hout_in, n2_in, s2_in, hin_in, own_out, got_out,
    own_conv, got_conv,
    grad_projected_out, vec_out, keep_buf, send_buf,
    gy, n3, s3, r, shifted, hout_ones, n2, s2, hin, w_out, conv, conv_w, prod, means, grad_mixed, moved, grad_projected,
    buf, ag3, ab3, ag2, ab2, sem, row_sems,
):
    section = lax.axis_index("section")
    leading = section == 0
    width, tokens = gy.shape
    inner = w_out.shape[0]
    w_in_at, end = layout(taps, width, inner)[2:4]
    hout = hout_ones.at[0:inner]
    pairs = (
        (gy_in, gy), (s3_in, s3), (n3_in, n3), (r_in, r), (hout_in, hout), (shifted_in, shifted), (n2_in, n2), (s2_in, s2),
        (hin_in, hin),
    )
    loads = [pltpu.make_async_copy(a, b, sem.at[2 + i]) for i, (a, b) in enumerate(pairs)]
    loads[0].start()
    weight = load_weight(leading, own_out, got_out, w_out, sem.at[0])
    start_all(loads[1:5])
    conv_weight = load_weight(leading, own_conv, got_conv, conv, sem.at[1])
    start_all(loads[5:])
    hout_ones[inner:, :] = jnp.ones((16, tokens), BF)
    small = pick_small(leading, small_own, small_got)
    dilation = jnp.max(small[7:8, 0:LANES]).astype(jnp.int32)

    def begins(unit):
        return seq[section, unit]

    def weights():
        conv_weight.wait()
        for k in range(taps):
            conv_w[:, inner * k : inner * (k + 1)] = conv[k]

    wait_all([weight, loads[0]])
    back_third(gy, w_out, (n3, s3, r), prod, means, grad_mixed, ag3, ab3, lambda: wait_all(loads[1:4]))
    back_second(
        taps, begins, dilation, conv_w, (n2, s2, r), prod, means, grad_mixed, moved, grad_projected, ag2, ab2,
        lambda: wait_all(loads[6:8]), weights,
    )
    out = pltpu.make_async_copy(grad_projected, grad_projected_out, sem.at[11])
    out.start()
    rows_out = RowsOut(buf, keep_buf, send_buf, section, lax.axis_index("dp"), groups, row_sems)
    loads[8].wait()
    put_slabs(buf, w_in_at, nt(grad_projected[...], hin[...]))
    rows_out.start(w_in_at, end)
    loads[4].wait()
    bias = put_w_out(buf, hout_ones, gy)
    rows_out.start(0, layout(taps, width, inner)[0])
    loads[5].wait()
    put_taps(buf, taps, width, shifted, grad_mixed, rows_out.start)
    _, g2, g3 = gains_of(small, width, inner)
    second, third = gain_and_bias(g2, (ag2, ab2)), gain_and_bias(g3, (ag3, ab3))
    put_rows(vec_out, [second[0], third[0], second[1], third[1], bias])
    out.wait()
    rows_out.wait()


def encoder_call(taps, groups, seq, gy, small_own, small_got, kept, own_out, got_out, own_conv, got_conv):
    width, tokens = gy.shape
    inner = own_out.shape[0]
    n1, s1, r, n2, s2, n3, s3, hin, shifted, hout = kept
    rows = layout(taps, width, inner)[3]
    half = padded_rows(rows, groups) // 2
    wide, narrow = (width, tokens), (inner, tokens)
    scratch = [
        (wide, BF), (narrow, BF), (narrow, BF), ((8, tokens), F32), ((inner * taps, tokens), BF),
        ((inner + 16, tokens), BF), (narrow, BF), (narrow, BF), (wide, BF), ((inner, width), BF),
        ((taps, inner, inner), BF), ((inner, inner * taps), BF), (narrow, F32), ((16, tokens), F32), (narrow, BF),
        ((inner * taps, tokens), BF), (narrow, BF), ((rows, LANES), BF),
    ]
    scratch += [((inner, LANES), F32)] * 4
    flops = 2 * tokens * inner * (3 * width + 2 * taps * inner)
    block = shape((half, LANES), BF)
    return pl.pallas_call(
        functools.partial(encoder_kernel, taps, groups),
        in_specs=[SMEM, ANY, VMEM, VMEM] + [ANY] * 12,
        out_specs=[ANY, VMEM, ANY, ANY],
        out_shape=[shape(narrow, BF), shape((SMALL_ROWS, width), F32), block, block],
        scratch_shapes=[pltpu.VMEM(dims, dtype) for dims, dtype in scratch]
        + [pltpu.SemaphoreType.DMA((12,)), pltpu.SemaphoreType.DMA((8 * share_count(groups[0]),))],
        compiler_params=pltpu.CompilerParams(vmem_limit_bytes=SMALL_LIMIT),
        cost_estimate=pl.CostEstimate(flops=4 * flops, bytes_accessed=20 * 2**20, transcendentals=0),
        name="encoder_back",
    )(
        seq, gy, small_own, small_got, n3, s3, r, shifted, hout, n2, s2, hin, own_out, got_out, own_conv, got_conv
    )


def first_kernel(
    block, gy_first, gy_second, grad_projected_in, small_own, small_got, vecs, n1_in, s1_in, r_in, own_in, got_in,
    *refs,
):
    outs_of, refs = refs[: 2 - block], refs[2 - block :]
    vec_out, gy, grad_projected, n1, s1, r, w_in_t, prod, means, gx, ag1, ab1, vec, sem = refs
    leading = lax.axis_index("section") == 0
    mine = leading if block == 0 else jnp.logical_not(leading)
    width, inner = gy.shape[0], grad_projected.shape[0]
    pairs = ((grad_projected_in, grad_projected), (s1_in, s1), (n1_in, n1), (r_in, r))
    loads = [pltpu.make_async_copy(a, b, sem.at[2 + i]) for i, (a, b) in enumerate(pairs)]
    loads[0].start()
    weight = load_weight(mine, own_in, got_in, w_in_t, sem.at[0])
    start_all(loads[1:])
    loads.append(load_weight(leading, gy_first, gy_second, gy, sem.at[1]))
    small = pick_small(mine, small_own, small_got)
    wait_all([loads[0], weight])

    def save(value, at_home, away, sem):
        pl.when(leading)(pltpu.make_async_copy(value, at_home, sem).start)
        pl.when(jnp.logical_not(leading))(pltpu.make_async_copy(value, away, sem).start)
        return pltpu.make_async_copy(value, away, sem)

    waits = []

    def ready():
        wait_all(loads[1:])
        if block == 0:
            outs, send = outs_of
            waits.append(save(gy, send, outs.at[1], sem.at[6]))

    back_first(gy, w_in_t, (n1, s1, r), prod, means, grad_projected, gx, ag1, ab1, ready)
    if block == 0:
        outs, send = outs_of
        waits.append(save(gx, outs.at[0], send, sem.at[7]))
    else:
        waits.append(pltpu.make_async_copy(gx, outs_of[0], sem.at[7]))
        waits[-1].start()
    sums = gain_and_bias(gains_of(small, width, inner)[0], (ag1, ab1))
    sums += [vecs[row : row + 1, 0:size] for row, size in enumerate((inner, inner, inner, inner, width))]
    put_vectors(vec_out, 0, vec, sums)
    wait_all(waits)


def first_call(block, gy_first, gy_second, grad_projected, vecs, kept, small_own, small_got, own_in, got_in):
    n1, s1, r = kept
    width, tokens = n1.shape
    inner = grad_projected.shape[0]
    wide, narrow = (width, tokens), (inner, tokens)
    scratch = [
        (wide, BF), (narrow, BF), (wide, BF), (wide, BF), ((8, tokens), F32), ((inner, width), BF), (wide, F32),
        ((16, tokens), F32), (wide, BF), ((width, LANES), F32), ((width, LANES), F32), ((VEC_ROWS, LANES), F32),
    ]
    outs = [shape((2,) + wide, BF), shape(wide, BF)] if block == 0 else [shape(wide, BF)]
    flops = 2 * tokens * inner * width
    return pl.pallas_call(
        functools.partial(first_kernel, block),
        in_specs=[ANY] * 3 + [VMEM] * 3 + [ANY] * 5,
        out_specs=[ANY] * len(outs) + [VMEM],
        out_shape=outs + [shape((VEC_ROWS, LANES), BF)],
        scratch_shapes=[pltpu.VMEM(dims, dtype) for dims, dtype in scratch] + [pltpu.SemaphoreType.DMA((8,))],
        compiler_params=pltpu.CompilerParams(vmem_limit_bytes=SMALL_LIMIT),
        cost_estimate=pl.CostEstimate(flops=8 * flops, bytes_accessed=20 * 2**20, transcendentals=0),
        name="first_%d" % block,
    )(gy_first, gy_second, grad_projected, small_own, small_got, vecs, n1, s1, r, own_in, got_in)


def load_weight(first, one, other, target, sem):
    pl.when(first)(pltpu.make_async_copy(one, target, sem).start)
    pl.when(jnp.logical_not(first))(pltpu.make_async_copy(other, target, sem).start)
    return pltpu.make_async_copy(one, target, sem)


def wait_all(copies):
    for copy in copies:
        copy.wait()


def unpack_kernel(taps_of, groups_of, *refs):
    refs = list(refs)

    def take(number):
        taken = refs[:number]
        del refs[:number]
        return taken

    own_of, got_of = [], []
    for _ in range(2):
        own_of.append(take(2))
        got_of.append(take(2))
    w_in_t_out, w_out_out, conv_out, gin, bin_, gmid, bmid, out_bias, w_in_t, w_out, conv, buf, extra, sem = refs
    inner, width = w_out.shape
    whole = inner // LANES
    tail = inner - whole * LANES
    slots = conv.shape[0]
    section = lax.axis_index("section")
    index = lax.axis_index("dp")

    def write(taps, groups, own, got):
        rows = own[0].shape[0] - VEC_ROWS
        count = share_count(groups[0])
        share = 2 * rows // count

        def body(position, _):
            for which, (pieces, side) in enumerate(((own, section), (got, 1 - section))):
                for at, ref in enumerate(pieces):
                    owner = owner_of(position + at * (count // 2), side, groups, index)
                    start = side * (2 * rows) + owner * share
                    pltpu.make_async_copy(
                        ref.at[pl.ds(pl.multiple_of(position * share, 16), share)],
                        buf.at[pl.ds(pl.multiple_of(start, 16), share)],
                        sem.at[2 * which + at],
                    ).start()
            return 0

        lax.fori_loop(0, count // 2, body, 0)
        pieces = list(own) + list(got)
        vectors = [
            pltpu.make_async_copy(ref.at[pl.ds(rows, VEC_ROWS)], extra.at[at], sem.at[4 + at])
            for at, ref in enumerate(pieces)
        ]
        start_all(vectors)
        for at, ref in enumerate(pieces):
            pltpu.make_async_copy(ref.at[pl.ds(0, rows)], buf.at[pl.ds(0, rows)], sem.at[at]).wait()
        wait_all(vectors)
        taps_at, tails_at, w_in_at, _, _ = layout(taps, width, inner)

        def wide(target, row):
            for at in range(0, width, LANES):
                q = at // LANES
                size = min(LANES, width - at)
                target[:, at : at + size] = buf[row + q * inner : row + (q + 1) * inner, 0:size].astype(F32)

        copies = []

        def leave(source, target):
            copies.append(pltpu.make_async_copy(source, target, sem.at[8 + len(copies)]))
            copies[-1].start()

        wide(w_out, 0)
        leave(w_out, w_out_out)
        tails = buf[tails_at : tails_at + inner, :].astype(F32)
        for k in range(slots):
            if k >= taps:
                conv[k] = jnp.zeros((inner, inner), F32)
            else:
                for q in range(whole):
                    at = taps_at + inner * (whole * k + q)
                    conv[k, :, LANES * q : LANES * (q + 1)] = buf[at : at + inner, :].astype(F32)
                conv[k, :, LANES * whole :] = tails[:, tail * k : tail * (k + 1)]
            leave(conv.at[k], conv_out.at[k])
        wide(w_in_t, w_in_at)
        leave(w_in_t, w_in_t_out)
        vec = sum(extra[at].astype(F32) for at in range(4))
        row = 0
        for target, member in ((gin, 0), (bin_, 0), (gmid, 0), (gmid, 1), (bmid, 0), (bmid, 1), (out_bias, 0)):
            for at in range(0, target.shape[1], LANES):
                size = min(LANES, target.shape[1] - at)
                target[member : member + 1, at : at + size] = vec[row : row + 1, 0:size]
                row += 1
        for copy in copies:
            copy.wait()

    pl.when(section == 0)(lambda: write(taps_of[0], groups_of[0], own_of[0], got_of[0]))
    pl.when(section != 0)(lambda: write(taps_of[1], groups_of[1], own_of[1], got_of[1]))


def unpack(taps_of, groups_of, enc, dec, width, inner):
    pieces = enc[0] + enc[1] + dec[0] + dec[1]
    rows = max(4 * part[0].shape[0] for part in (enc[0], dec[0]))
    return pl.pallas_call(
        functools.partial(unpack_kernel, taps_of, groups_of),
        in_specs=[ANY] * len(pieces),
        out_specs=[ANY] * 3 + [VMEM] * 5,
        out_shape=[
            shape((inner, width), F32), shape((inner, width), F32), shape((taps_of[0], inner, inner), F32),
            shape((1, width), F32), shape((1, width), F32), shape((2, inner), F32), shape((2, inner), F32),
            shape((1, width), F32),
        ],
        scratch_shapes=[
            pltpu.VMEM((inner, width), F32), pltpu.VMEM((inner, width), F32), pltpu.VMEM((taps_of[0], inner, inner), F32),
            pltpu.VMEM((rows, LANES), BF), pltpu.VMEM((4, VEC_ROWS, LANES), BF),
            pltpu.SemaphoreType.DMA((10 + taps_of[0],)),
        ],
        compiler_params=pltpu.CompilerParams(vmem_limit_bytes=SMALL_LIMIT),
        name="unpack",
    )(*pieces)


def swap_sections(value):
    return lax.ppermute(value, "section", [(0, 1), (1, 0)])


def swap_dp(value, masks):
    count = lax.axis_size("dp")
    pairs = [(s * count + i, s * count + (i ^ masks[s])) for s in range(2) for i in range(count)]
    return lax.ppermute(value, ("section", "dp"), pairs)


def rounded_sum(terms, rows):
    total = terms[0][rows].astype(F32)
    for term in terms[1:]:
        total = total + term[rows].astype(F32)
    return total.astype(BF)


def masks_of(bits, other):
    return [other << own[0] for own in bits]


def reduce_steps(keep, got, groups, receiver, vec=None):
    count = lax.axis_size("dp")
    steps = list(zip(*groups))
    terms = [keep, got]

    def loaded(part, riding):
        return part if vec is None or not riding else jnp.concatenate([part, vec], 0)

    for number, bits in enumerate(steps):
        size = terms[0].shape[0] >> len(bits[0])
        others = range(1, 2 ** len(bits[0]))
        parts = [rounded_sum(terms, slice(other * size, (other + 1) * size)) for other in others]
        parts = [loaded(part, number > 0) for part in parts]
        gate = yield parts
        came = after([swap_dp(part, masks_of(bits, other)) for part, other in zip(parts, others)], gate)
        terms = [term[:size] for term in terms] + [part[:size] for part in came]
        if vec is not None and number > 0:
            vec = rounded_sum([vec] + [part[size:] for part in came], slice(None))
    value = rounded_sum(terms, slice(None))
    rest = list(range(sum(len(bits) for bits in groups[0]), count.bit_length() - 1))
    for bits in zip(rest, rest[1:] + rest[:1]):
        size = value.shape[0]
        whole = loaded(value, True)
        gate = yield [whole]
        whole = rounded_sum([whole, after(swap_dp(whole, [1 << bit for bit in bits]), gate)], slice(None))
        value, vec = whole[:size], (None if vec is None else whole[size:])
    pieces = [value]
    for bits in reversed(steps[1:]):
        if len(pieces) > 1:
            value = jnp.concatenate(pieces, 0)
        gate = yield [value]
        came = [swap_dp(value, masks_of(bits, other)) for other in range(1, 2 ** len(bits[0]))]
        pieces = [value] + after(came, gate)
    if vec is not None:
        pieces = pieces + [vec]
    if len(pieces) > 1:
        value = jnp.concatenate(pieces, 0)
    gate = yield [value]
    sender = 1 - receiver
    masks = masks_of(steps[0], 1)
    ways = ((receiver, masks[receiver]), (sender, 0), (sender, masks[sender]))
    came = []
    for source, mask in ways:
        pairs = [(source * count + i, receiver * count + (i ^ mask)) for i in range(count)]
        came.append(lax.ppermute(value, ("section", "dp"), pairs))
    yield [value] + after(came, gate)


class Steps:
    def __init__(self, *args):
        self.steps = reduce_steps(*args)
        self.ready = next(self.steps)

    def step(self, gate=()):
        self.ready = self.steps.send(gate)
        return self.ready

    def finish(self):
        while len(self.ready) != 4:
            self.step()
        return self.ready[:2], self.ready[2:]


def after(values, earlier):
    return lax.optimization_barrier((values, earlier))[0] if earlier else values


def shards(
    section_inputs,
    seq_lengths,
    dilations,
    gains_in,
    biases_in,
    gains_mid,
    biases_mid,
    out_bias,
    w_in,
    w_out,
    conv_taps,
):
    section = lax.axis_index("section")
    count = lax.axis_size("dp")
    groups_of = (scatter_groups(count, False), scatter_groups(count, False))
    rows = jnp.swapaxes(section_inputs[0], 1, 2)
    width = rows.shape[1]
    inner = w_out.shape[1]
    taps_of = (conv_taps.shape[1], DEC_TAPS)

    own_w = (jnp.swapaxes(w_in[0], 0, 1), w_out[0], conv_taps[0])
    send_rows, small = prepare(rows, gains_in, biases_in, gains_mid[0], biases_mid[0], out_bias, dilations)
    got_rows = swap_sections(send_rows)
    got_small = swap_sections(small)
    got_w = tuple(swap_sections(member) for member in own_w)

    outs, send_y, grad_dec, keep_dec, send_dec, vec, *kept = main_call(
        taps_of, groups_of[1], seq_lengths, rows, got_rows, small, got_small, own_w, got_w
    )
    dec = Steps(keep_dec, swap_sections(send_dec), groups_of[1], 1, vec)
    grad_projected, vec, keep_enc, send_enc = encoder_call(
        taps_of[0], groups_of[0], seq_lengths, grad_dec, small, got_small, kept, own_w[1], got_w[1], own_w[2], got_w[2]
    )
    got_y = swap_sections(send_y)
    enc_early = swap_sections(send_enc)
    grad_projected = after(grad_projected, dec.ready)
    grads_x, send_gx, vec = first_call(
        0, grad_dec, grad_dec, grad_projected, vec, kept[0:3], small, got_small, own_w[0], got_w[0]
    )

    def joined(pair, got):
        pair = lax.dynamic_update_slice_in_dim(pair, got[None], 1 - section, 0)
        return jnp.swapaxes(pair, 1, 2)[None]

    enc = Steps(keep_enc, enc_early, groups_of[0], 0, vec)
    got_gx = swap_sections(send_gx)
    outputs = joined(outs, got_y)
    input_grads = joined(grads_x, got_gx)
    named = {"d": dec, "e": enc}
    last = ()
    for name in SEQ:
        if name in named:
            if len(named[name].ready) != 4:
                last = named[name].step(last)
        else:
            last = [*last, outputs if name == "y" else input_grads]
    enc = enc.finish()
    dec = dec.finish()
    grads = unpack(taps_of, groups_of, enc, dec, width, inner)
    return (
        outputs,
        input_grads,
        grads[3],
        grads[4],
        grads[5][None],
        grads[6][None],
        grads[7],
        jnp.swapaxes(grads[0], 0, 1)[None],
        grads[1][None],
        grads[2][None],
    )


def solution(mesh):
    in_specs = (
        P("section", None, "dp", None),
        P(None, "dp"),
        P("section"),
        P("section", None),
        P("section", None),
        P("section", None, None),
        P("section", None, None),
        P("section", None),
        P("section", None, None),
        P("section", None, None),
        P("section", None, None, None),
    )
    out_specs = (
        P("section", None, "dp", None),
        P("section", None, "dp", None),
        P("section", None),
        P("section", None),
        P("section", None, None),
        P("section", None, None),
        P("section", None),
        P("section", None, None),
        P("section", None, None),
        P("section", None, None, None),
    )
    return jax.shard_map(shards, mesh=mesh, in_specs=in_specs, out_specs=out_specs, check_vma=False)
```

```python
import functools

import jax
import jax.numpy as jnp
from jax import lax
from jax.experimental import pallas as pl
from jax.experimental.pallas import tpu as pltpu
from jax.sharding import PartitionSpec as P

DEC_TAPS = 3
EPS = 1e-05
LANES = 128
CHUNK = 80
VEC_ROWS = 48
SMALL_ROWS = 8
PIECES = 5
BF = jnp.bfloat16
F32 = jnp.float32
VMEM_LIMIT = 62 * 2**20
SMALL_LIMIT = 62 * 2**20
SEQ = "ddeedeydexde"
ANY = pl.BlockSpec(memory_space=pl.ANY)
SMEM = pl.BlockSpec(memory_space=pltpu.SMEM)
VMEM = pl.BlockSpec(memory_space=pltpu.VMEM)


def shape(dims, dtype):
    return jax.ShapeDtypeStruct(tuple(dims), dtype)


def nn(left, right):
    return jnp.dot(left, right, preferred_element_type=F32)


def nt(left, right):
    return lax.dot_general(left, right, (((1,), (1,)), ((), ())), preferred_element_type=F32)


def tn(left, right):
    return lax.dot_general(left, right, (((0,), (0,)), ((), ())), preferred_element_type=F32)


def lane_block(index):
    return pl.ds(pl.multiple_of(index * LANES, LANES), LANES)


def chunks(rows):
    size = CHUNK if rows % CHUNK == 0 else 16
    return [slice(at, at + size) for at in range(0, rows, size)]


def folded(values):
    return jnp.sum(values.reshape(values.shape[0] // 8, 8, values.shape[1]), 0)


def column(vector):
    return jnp.broadcast_to(vector, (LANES, vector.shape[1])).T


def norm_forward(source, half_gain, half_bias, normed, slope, hidden, devs, row, units):
    feats, tokens = source.shape
    scale = 1.0 / feats

    def stats(here):
        base = source[0:1, here].astype(F32)
        total = jnp.zeros((8, LANES), F32)
        squares = jnp.zeros((8, LANES), F32)
        for part in chunks(feats):
            moved = source[part, here].astype(F32) - base
            total = total + folded(moved)
            squares = squares + folded(moved * moved)
        average = jnp.sum(total, 0, keepdims=True) * scale
        variance = jnp.sum(squares, 0, keepdims=True) * scale - average * average
        inverse_dev = lax.rsqrt(jnp.maximum(variance, 0.0) + EPS)
        return (average + base) * inverse_dev, inverse_dev

    for unit in units:
        here = slice(unit * LANES, (unit + 1) * LANES)
        offset, inverse_dev = stats(here)
        devs[row : row + 1, here] = inverse_dev
        for part in chunks(feats):
            values = source[part, here].astype(F32) * inverse_dev - offset
            gain = half_gain[part, :]
            half = values * gain + half_bias[part, :]
            tan = jnp.tanh(half)
            weight = 1.0 + tan
            out = half * weight
            normed[part, here] = values.astype(BF)
            slope[part, here] = ((weight + out * (1.0 - tan)) * gain).astype(BF)
            hidden[part, here] = out.astype(hidden.dtype)


def norm_backward(gradient, slope, normed, devs, row, gain_sums, bias_sums, means, emit):
    feats, tokens = gradient.shape
    units = tokens // LANES
    scale = 1.0 / feats
    means[...] = jnp.zeros_like(means)

    for part in chunks(feats):
        size = part.stop - part.start
        gain_sum = jnp.zeros((size, LANES), F32)
        bias_sum = jnp.zeros((size, LANES), F32)
        for unit in range(units):
            here = slice(unit * LANES, (unit + 1) * LANES)
            scaled = gradient[part, here] * slope[part, here].astype(F32)
            weighted = scaled * normed[part, here].astype(F32)
            gain_sum = gain_sum + weighted
            bias_sum = bias_sum + scaled
            means[0:8, here] += folded(scaled)
            means[8:16, here] += folded(weighted)
        gain_sums[part, :] = gain_sum
        bias_sums[part, :] = bias_sum

    for unit in range(units):
        here = slice(unit * LANES, (unit + 1) * LANES)
        inverse_dev = devs[row : row + 1, here]
        first = jnp.sum(means[0:8, here], 0, keepdims=True) * (scale * inverse_dev)
        second = jnp.sum(means[8:16, here], 0, keepdims=True) * (scale * inverse_dev)
        for part in chunks(feats):
            scaled = gradient[part, here] * slope[part, here].astype(F32)
            emit(part, here, scaled * inverse_dev - first - normed[part, here].astype(F32) * second)


def write_shifts(source, target, begins, offsets, units):
    feats, tokens = source.shape
    count = tokens // LANES
    block = lambda unit: slice(unit * LANES, (unit + 1) * LANES)
    for unit in units:
        joined_behind = (begins(unit) == 0).astype(F32) if unit > 0 else None
        joined_ahead = (begins(unit + 1) == 0).astype(F32) if unit < count - 1 else None
        for part in chunks(feats):
            size = part.stop - part.start
            lane = lax.broadcasted_iota(jnp.int32, (size, LANES), 1)
            zero = jnp.zeros((size, LANES), F32)
            current = source[part, block(unit)].astype(F32)
            behind = zero if unit == 0 else source[part, block(unit - 1)].astype(F32) * joined_behind
            ahead = zero if unit == count - 1 else source[part, block(unit + 1)].astype(F32) * joined_ahead
            for position, (sign, step) in enumerate(offsets):
                if sign == 0:
                    moved = current
                elif sign < 0:
                    moved = pltpu.roll(jnp.where(lane < LANES - step, current, behind), step, 1)
                else:
                    moved = pltpu.roll(jnp.where(lane >= step, current, ahead), LANES - step, 1)
                rows = slice(feats * position + part.start, feats * position + part.stop)
                target[rows, block(unit)] = moved.astype(BF)


def tap_offsets(taps, dilation, flip):
    result = []
    for position in range(taps):
        factor = (position - 2) * (-1 if flip else 1)
        result.append(((factor > 0) - (factor < 0), abs(factor) * dilation))
    return result


def layout(taps, width, inner):
    wide = pl.cdiv(width, LANES) * inner
    taps_at = wide
    tails_at = taps_at + taps * (inner // LANES) * inner
    w_in_at = tails_at + inner
    vec_at = w_in_at + wide
    return taps_at, tails_at, w_in_at, vec_at, vec_at + VEC_ROWS


def scatter_groups(count, full):
    total = count.bit_length() - 1
    rest = [list(range(2, min(4, total)))] if full and total > 2 else []
    return [[[bit] for bit in bits if bit < total] + rest for bits in ((0, 1), (1, 0))]


def share_count(groups):
    return 2 ** sum(len(bits) for bits in groups)


def padded_rows(rows, groups):
    unit = 2 * 16 * share_count(groups[0])
    return pl.cdiv(rows, unit) * unit


def put_slabs(buf, row, matrix):
    rows, cols = matrix.shape
    for q in range(pl.cdiv(cols, LANES)):
        part = matrix[:, LANES * q : min(cols, LANES * (q + 1))]
        if part.shape[1] < LANES:
            part = jnp.concatenate([part, jnp.zeros((rows, LANES - part.shape[1]), F32)], 1)
        buf[row + q * rows : row + (q + 1) * rows, :] = part.astype(BF)


def put_taps(buf, taps, width, shifted, grad_mixed):
    inner = grad_mixed.shape[0]
    taps_at, tails_at, _, _, _ = layout(taps, width, inner)
    whole = inner // LANES
    tail = inner - whole * LANES
    for k in range(taps):
        grad = nt(shifted[inner * k : inner * (k + 1), :], grad_mixed[...])
        for q in range(whole):
            at = taps_at + inner * (whole * k + q)
            buf[at : at + inner, :] = grad[:, LANES * q : LANES * (q + 1)].astype(BF)
        buf[tails_at : tails_at + inner, tail * k : tail * (k + 1)] = grad[:, LANES * whole :].astype(BF)
    buf[tails_at : tails_at + inner, tail * taps :] = jnp.zeros((inner, LANES - tail * taps), BF)


def row_sums(acc):
    return jnp.sum(acc.T, 0, keepdims=True)


def put_vectors(buf, at, vec, sums):
    vec[...] = jnp.zeros_like(vec)
    row = 0
    for total in sums:
        for lane in range(0, total.shape[1], LANES):
            part = total[:, lane : lane + LANES]
            vec[row : row + 1, 0 : part.shape[1]] = part
            row += 1
    buf[at : at + VEC_ROWS, :] = vec[...].astype(BF)


def relative_index(position, groups):
    result = 0
    for bits in reversed(groups):
        size = 2 ** len(bits)
        result = result + (position & (size - 1)) * 2 ** bits[0]
        position = position >> len(bits)
    return result


def owner_of(position, side, groups, index):
    both = [relative_index(position, order) for order in groups]
    mask = sum(2**bit for bits in groups[0] for bit in bits)
    return jnp.where(side == 0, both[0], both[1]) ^ (index & mask)


def position_of(owner, side, groups, index):
    distance = owner ^ index
    position = 0
    for bits in groups[side]:
        position = position * 2 ** len(bits) + ((distance >> bits[0]) & (2 ** len(bits) - 1))
    return position


class RowsOut:
    def __init__(self, buf, keep, send, section, index, groups, sems):
        self.buf, self.keep, self.send, self.sems = buf, keep, send, sems
        self.section, self.index, self.groups = section, index, groups
        self.count = share_count(groups[0])
        self.share = keep.shape[0] // self.count
        self.sizes = []

    def start(self, first, last):
        for number in range(2 * self.count):
            low, high = max(first, number * self.share), min(last, (number + 1) * self.share)
            if low >= high:
                continue
            side, owner = divmod(number, self.count)
            place = position_of(owner, side, self.groups, self.index) * self.share + (low - number * self.share)
            target = pl.ds(pl.multiple_of(place, 16), high - low)
            source = self.buf.at[low:high]
            sem = self.sems.at[len(self.sizes)]
            pl.when(self.section == side)(pltpu.make_async_copy(source, self.keep.at[target], sem).start)
            pl.when(self.section != side)(pltpu.make_async_copy(source, self.send.at[target], sem).start)
            self.sizes.append(high - low)

    def wait(self):
        for number, size in enumerate(self.sizes):
            source, target = self.buf.at[0:size], self.keep.at[0:size]
            pltpu.make_async_copy(source, target, self.sems.at[number]).wait()


def forward_block(taps, begins, dilation, x, y, weights, turned, cols, kept, hmid, prod, ready):
    w_in_t, w_out, conv = weights
    w_out_t, conv_t = turned
    g1, b1, g2, b2, g3, b3, ob = cols
    n1, s1, r, n2, s2, n3, s3, hin, shifted, hout = kept
    inner, tokens = hmid.shape
    units = tokens // LANES
    narrow = prod.at[0:inner]
    parts = [range(at, min(at + units // 2, units)) for at in range(0, units, units // 2)]
    columns = [slice(part.start * LANES, part.stop * LANES) for part in parts]
    offsets = tap_offsets(taps, dilation, False)

    def project(part):
        narrow[:, columns[part]] = nn(w_in_t[...], hin[:, columns[part]])

    def mix(part):
        narrow[:, columns[part]] = nn(conv_t[:, 0 : taps * inner], shifted[:, columns[part]])

    def leave(part):
        here = columns[part]
        bias = jnp.concatenate([ob[...]] * len(parts[part]), 1)
        y[:, here] = (x[:, here].astype(F32) + nn(w_out_t[...], hout[:, here]) + bias).astype(BF)

    norm_forward(x, g1, b1, n1, s1, hin, r, 0, parts[0])
    ready(0)
    project(0)
    norm_forward(x, g1, b1, n1, s1, hin, r, 0, parts[1])
    ready(1)
    project(1)
    norm_forward(narrow, g2, b2, n2, s2, hmid, r, 1, parts[0])
    for k in range(taps):
        conv_t[:, inner * k : inner * (k + 1)] = conv[k].T
    w_out_t[...] = w_out[...].T
    norm_forward(narrow, g2, b2, n2, s2, hmid, r, 1, parts[1])
    write_shifts(hmid, shifted, begins, offsets, parts[0])
    mix(0)
    write_shifts(hmid, shifted, begins, offsets, parts[1])
    mix(1)
    norm_forward(narrow, g3, b3, n3, s3, hout, r, 2, parts[0])
    leave(0)
    norm_forward(narrow, g3, b3, n3, s3, hout, r, 2, parts[1])
    leave(1)


def fill_columns(small, cols):
    g1, b1, g2, b2, g3, b3, ob = cols
    width, inner = g1.shape[0], g2.shape[0]
    for target, row, scale in ((g1, 0, 0.5), (b1, 1, 0.5), (ob, 2, 1.0)):
        target[...] = column(small[row : row + 1, 0:width] * scale)
    for target, row in ((g2, 3), (b2, 4), (g3, 5), (b3, 6)):
        target[...] = column(small[row : row + 1, 0:inner] * 0.5)


def back_third(gy, w_out, kept, prod, means, grad_mixed, gain_sums, bias_sums, beside):
    n3, s3, r = kept
    inner = w_out.shape[0]
    narrow = prod.at[0:inner]
    narrow[...] = nn(w_out[...], gy[...])
    beside()

    def emit(part, here, value):
        grad_mixed[part, here] = value.astype(BF)

    norm_backward(narrow, s3, n3, r, 2, gain_sums, bias_sums, means, emit)


def back_second(
    taps, begins, dilation, conv_w, kept, prod, means, grad_mixed, moved, grad_projected, gain_sums, bias_sums, ready,
    weights=None,
):
    n2, s2, r = kept
    inner = grad_mixed.shape[0]
    narrow = prod.at[0:inner]
    write_shifts(grad_mixed, moved, begins, tap_offsets(taps, dilation, True), range(grad_mixed.shape[1] // LANES))
    if weights is not None:
        weights()
    narrow[...] = nn(conv_w[...], moved[...])
    ready()

    def emit(part, here, value):
        grad_projected[part, here] = value.astype(BF)

    norm_backward(narrow, s2, n2, r, 1, gain_sums, bias_sums, means, emit)


def back_first(gy, w_in_t, kept, prod, means, grad_projected, gx, gain_sums, bias_sums, ready):
    n1, s1, r = kept
    prod[...] = tn(w_in_t[...], grad_projected[...])
    ready()

    def emit(part, here, value):
        gx[part, here] = (gy[part, here].astype(F32) + value).astype(BF)

    norm_backward(prod, s1, n1, r, 0, gain_sums, bias_sums, means, emit)


def put_w_out(buf, hout_ones, gy):
    grad = nt(hout_ones[...], gy[...])
    inner = hout_ones.shape[0] - 16
    put_slabs(buf, 0, grad[0:inner])
    return grad[inner : inner + 1]


def gain_and_bias(gain, sums):
    return [row_sums(acc[...]) / gain for acc in sums]


def put_rows(target, rows):
    target[...] = jnp.zeros_like(target)
    for at, row in enumerate(rows):
        target[at : at + 1, 0 : row.shape[1]] = row


def gains_of(small, width, inner):
    return small[0:1, 0:width], small[3:4, 0:inner], small[5:6, 0:inner]


def pick_small(leading, own, got):
    flag = leading.astype(F32)
    return own[...] * flag + got[...] * (1.0 - flag)


def start_all(copies):
    for copy in copies:
        copy.start()


def pick_rows_kernel(rows, send, hold, sem):
    section = lax.axis_index("section")
    size = send.shape[0] // PIECES
    parts = [slice(size * i, size * (i + 1)) for i in range(PIECES)]
    arrive = [
        pltpu.make_async_copy(rows.at[1 - section, part], hold.at[part], sem.at[i]) for i, part in enumerate(parts)
    ]
    leave = [pltpu.make_async_copy(hold.at[part], send.at[part], sem.at[PIECES + i]) for i, part in enumerate(parts)]
    start_all(arrive)
    for come, go in zip(arrive, leave):
        come.wait()
        go.start()
    for go in leave:
        go.wait()


def pick_rows(rows):
    return pl.pallas_call(
        pick_rows_kernel,
        in_specs=[ANY],
        out_specs=ANY,
        out_shape=shape(rows.shape[1:], BF),
        scratch_shapes=[pltpu.VMEM(rows.shape[1:], BF), pltpu.SemaphoreType.DMA((2 * PIECES,))],
        compiler_params=pltpu.CompilerParams(vmem_limit_bytes=VMEM_LIMIT),
        cost_estimate=pl.CostEstimate(flops=0, bytes_accessed=8 * 2**20, transcendentals=0),
        name="pick_rows",
    )(rows)


def pack_small_kernel(gin, bin_, gmid, bmid, out_bias, dilation, small):
    width, inner = gin.shape[1], gmid.shape[1]
    small[...] = jnp.zeros_like(small)
    for row, ref in ((0, gin), (1, bin_), (2, out_bias)):
        small[row : row + 1, 0:width] = ref[...]
    for row, ref, which in ((3, gmid, 0), (4, bmid, 0), (5, gmid, 1), (6, bmid, 1)):
        small[row : row + 1, 0:inner] = ref[which : which + 1, :]
    small[7:8, :] = jnp.full((1, small.shape[1]), dilation[0].astype(F32), F32)


def pack_small(gin, bin_, gmid, bmid, out_bias, dilation):
    return pl.pallas_call(
        pack_small_kernel,
        in_specs=[VMEM] * 5 + [SMEM],
        out_specs=VMEM,
        out_shape=shape((SMALL_ROWS, gin.shape[1]), F32),
        compiler_params=pltpu.CompilerParams(vmem_limit_bytes=VMEM_LIMIT),
        name="pack_small",
    )(gin, bin_, gmid, bmid, out_bias, dilation)


def kept_shapes(taps, width, inner, tokens):
    wide, narrow = (width, tokens), (inner, tokens)
    return [
        (wide, BF), (wide, BF), ((8, tokens), F32), (narrow, BF), (narrow, BF), (narrow, BF), (narrow, BF),
        (wide, BF), ((inner * taps, tokens), BF), (narrow, BF),
    ]


def column_shapes(width, inner):
    return [(width, LANES)] * 2 + [(inner, LANES)] * 4 + [(width, LANES)]


def main_kernel(taps_of, groups, *refs):
    refs = list(refs)

    def take(number):
        taken = refs[:number]
        del refs[:number]
        return taken

    seq, rows, got, small_own, small_got = take(5)
    own_w, got_w = take(3), take(3)
    outs, send_y, grad_out, keep_buf, send_buf, vec_out = take(6)
    kept_out = take(10)
    x, cot = take(2)
    enc_w, dec_w = take(3), take(3)
    small = take(2)
    enc_kept, dec_kept = take(10), take(10)
    cols = take(7)
    hmid, prod, means, y_enc, gx, w_out_t, conv_t, conv_w, grad_mixed, grad_projected, moved, buf = take(12)
    ag1, ab1, ag2, ab2, ag3, ab3, vec, sem, row_sems = take(9)

    section = lax.axis_index("section")
    index = lax.axis_index("dp")
    leading = section == 0
    width, tokens = x.shape
    inner = hmid.shape[0]
    small[0][...] = pick_small(leading, small_own, small_got)
    small[1][...] = pick_small(leading, small_got, small_own)
    dilation = [jnp.max(member[7:8, 0:LANES]).astype(jnp.int32) for member in small]

    def begins(unit):
        return seq[section, unit]

    loads = [(x, rows.at[0], got), (enc_w[0], own_w[0], got_w[0]), (enc_w[2], own_w[2], got_w[2])]
    loads += [(enc_w[1], own_w[1], got_w[1]), (dec_w[0], got_w[0], own_w[0]), (dec_w[1], got_w[1], own_w[1])]
    loads += [(dec_w[2], got_w[2].at[0 : taps_of[1]], own_w[2].at[0 : taps_of[1]]), (cot, got, rows.at[1])]

    def load(at):
        target, first, second = loads[at]
        pl.when(leading)(pltpu.make_async_copy(first, target, sem.at[at]).start)
        pl.when(jnp.logical_not(leading))(pltpu.make_async_copy(second, target, sem.at[at]).start)

    for at in range(4):
        load(at)

    def ready(at):
        pltpu.make_async_copy(loads[at][1], loads[at][0], sem.at[at]).wait()

    fill_columns(small[0], cols)
    hout_ones = dec_kept[9]
    dec_kept[9] = hout_ones.at[0:inner]
    hout_ones[inner:, :] = jnp.ones((16, tokens), BF)
    ready(0)

    def enc_ready(which):
        for at in ((1,), (2, 3))[which]:
            ready(at)
        if which:
            for at in range(4, 8):
                load(at)

    turned = (w_out_t, conv_t)
    forward_block(taps_of[0], begins, dilation[0], x, y_enc, enc_w, turned, cols, enc_kept, hmid, prod, enc_ready)
    saves = [pltpu.make_async_copy(a, b, sem.at[8 + i]) for i, (a, b) in enumerate(zip(enc_kept, kept_out))]
    start_all(saves)

    fill_columns(small[1], cols)
    for at in range(4, 8):
        ready(at)
    for k in range(taps_of[1]):
        conv_w[:, inner * k : inner * (k + 1)] = dec_w[2][k]
    y_dec = x
    forward_block(
        taps_of[1], begins, dilation[1], y_enc, y_dec, dec_w, turned, cols, dec_kept, hmid, prod, lambda which: None
    )
    pl.when(leading)(pltpu.make_async_copy(y_enc, outs.at[0], sem.at[18]).start)
    pl.when(leading)(pltpu.make_async_copy(y_dec, send_y, sem.at[19]).start)
    pl.when(jnp.logical_not(leading))(pltpu.make_async_copy(y_dec, outs.at[1], sem.at[18]).start)
    pl.when(jnp.logical_not(leading))(pltpu.make_async_copy(y_enc, send_y, sem.at[19]).start)

    n1, s1, r, n2, s2, n3, s3, hin, shifted, hout = dec_kept
    rows_out = RowsOut(buf, keep_buf, send_buf, section, index, groups, row_sems)
    w_in_at, end = layout(taps_of[1], width, inner)[2:4]

    bias = []

    def third_beside():
        bias.append(put_w_out(buf, hout_ones, cot))

    def first_beside():
        put_slabs(buf, w_in_at, nt(grad_projected[...], hin[...]))

    back_third(cot, dec_w[1], (n3, s3, r), prod, means, grad_mixed, ag3, ab3, third_beside)
    put_taps(buf, taps_of[1], width, shifted, grad_mixed)
    back_second(
        taps_of[1], begins, dilation[1], conv_w, (n2, s2, r), prod, means, grad_mixed, moved, grad_projected, ag2, ab2,
        lambda: None,
    )
    rows_out.start(0, w_in_at)
    back_first(cot, dec_w[0], (n1, s1, r), prod, means, grad_projected, gx, ag1, ab1, first_beside)
    rows_out.start(w_in_at, end)
    last = pltpu.make_async_copy(gx, grad_out, sem.at[20])
    last.start()
    g1, g2, g3 = gains_of(small[1], width, inner)
    first, second, third = gain_and_bias(g1, (ag1, ab1)), gain_and_bias(g2, (ag2, ab2)), gain_and_bias(g3, (ag3, ab3))
    put_vectors(vec_out, 0, vec, first + [second[0], third[0], second[1], third[1]] + bias)
    rows_out.wait()
    wait_all(saves + [last])
    pltpu.make_async_copy(y_enc, outs.at[0], sem.at[18]).wait()
    pltpu.make_async_copy(y_dec, send_y, sem.at[19]).wait()


def main_call(taps_of, groups, seq, rows, got, small_own, small_got, own_w, got_w):
    _, width, tokens = rows.shape
    inner = own_w[1].shape[0]
    half = padded_rows(layout(taps_of[1], width, inner)[3], groups) // 2
    wide, narrow = (width, tokens), (inner, tokens)
    weight_shapes = [(inner, width), (inner, width)]
    scratch = [(wide, BF)] * 2
    for taps in taps_of:
        scratch += [(dims, BF) for dims in weight_shapes + [(taps, inner, inner)]]
    scratch += [((SMALL_ROWS, width), F32)] * 2
    scratch += kept_shapes(taps_of[0], width, inner, tokens) + kept_shapes(taps_of[1], width, inner, tokens)[:-1]
    scratch += [((inner + 16, tokens), BF)]
    scratch += [(dims, F32) for dims in column_shapes(width, inner)]
    scratch += [
        (narrow, BF), (wide, F32), ((16, tokens), F32), (wide, BF), (wide, BF), ((width, inner), BF),
        ((inner, inner * taps_of[0]), BF), ((inner, inner * taps_of[1]), BF),
        (narrow, BF), (narrow, BF), ((inner * taps_of[1], tokens), BF), ((2 * half, LANES), BF),
    ]
    scratch += [((width, LANES), F32)] * 2 + [((inner, LANES), F32)] * 4 + [((VEC_ROWS, LANES), F32)]
    block = shape((half, LANES), BF)
    outs = [shape((2,) + wide, BF), shape(wide, BF), shape(wide, BF), block, block, shape((VEC_ROWS, LANES), BF)]
    outs += [shape(dims, dtype) for dims, dtype in kept_shapes(taps_of[0], width, inner, tokens)]
    flops = 2 * tokens * inner * (2 * width + taps_of[0] * inner + 3 * (2 * width + taps_of[1] * inner))
    return pl.pallas_call(
        functools.partial(main_kernel, taps_of, groups),
        in_specs=[SMEM, ANY, ANY, VMEM, VMEM] + [ANY] * 6,
        out_specs=[ANY] * 5 + [VMEM] + [ANY] * 10,
        out_shape=outs,
        scratch_shapes=[pltpu.VMEM(dims, dtype) for dims, dtype in scratch]
        + [pltpu.SemaphoreType.DMA((24,)), pltpu.SemaphoreType.DMA((8 * share_count(groups[0]),))],
        compiler_params=pltpu.CompilerParams(vmem_limit_bytes=VMEM_LIMIT),
        cost_estimate=pl.CostEstimate(flops=4 * flops, bytes_accessed=60 * 2**20, transcendentals=0),
        name="main_blocks",
    )(seq, rows, got, small_own, small_got, *own_w, *got_w)


def load_weight(leading, own, got, target, sem):
    pl.when(leading)(pltpu.make_async_copy(own, target, sem).start)
    pl.when(jnp.logical_not(leading))(pltpu.make_async_copy(got, target, sem).start)
    return pltpu.make_async_copy(own, target, sem)


def wait_all(copies):
    for copy in copies:
        copy.wait()


def encoder_kernel(
    taps, groups,
    seq, gy_in, small_own, small_got, n3_in, s3_in, r_in, shifted_in, hout_in, n2_in, s2_in, hin_in, own_out, got_out,
    own_conv, got_conv,
    grad_projected_out, vec_out, keep_buf, send_buf,
    gy, n3, s3, r, shifted, hout_ones, n2, s2, hin, w_out, conv, conv_w, prod, means, grad_mixed, moved, grad_projected,
    buf, ag3, ab3, ag2, ab2, sem, row_sems,
):
    section = lax.axis_index("section")
    leading = section == 0
    width, tokens = gy.shape
    inner = w_out.shape[0]
    w_in_at, end = layout(taps, width, inner)[2:4]
    hout = hout_ones.at[0:inner]
    pairs = (
        (gy_in, gy), (s3_in, s3), (n3_in, n3), (r_in, r), (hout_in, hout), (shifted_in, shifted), (n2_in, n2), (s2_in, s2),
        (hin_in, hin),
    )
    loads = [pltpu.make_async_copy(a, b, sem.at[2 + i]) for i, (a, b) in enumerate(pairs)]
    loads[0].start()
    weight = load_weight(leading, own_out, got_out, w_out, sem.at[0])
    start_all(loads[1:5])
    conv_weight = load_weight(leading, own_conv, got_conv, conv, sem.at[1])
    start_all(loads[5:])
    hout_ones[inner:, :] = jnp.ones((16, tokens), BF)
    small = pick_small(leading, small_own, small_got)
    dilation = jnp.max(small[7:8, 0:LANES]).astype(jnp.int32)

    def begins(unit):
        return seq[section, unit]

    def weights():
        conv_weight.wait()
        for k in range(taps):
            conv_w[:, inner * k : inner * (k + 1)] = conv[k]

    wait_all([weight, loads[0]])
    bias = []

    def third_beside():
        wait_all(loads[1:5])
        bias.append(put_w_out(buf, hout_ones, gy))

    back_third(gy, w_out, (n3, s3, r), prod, means, grad_mixed, ag3, ab3, third_beside)
    wait_all([loads[5]])
    put_taps(buf, taps, width, shifted, grad_mixed)
    back_second(
        taps, begins, dilation, conv_w, (n2, s2, r), prod, means, grad_mixed, moved, grad_projected, ag2, ab2,
        lambda: wait_all(loads[6:8]), weights,
    )
    out = pltpu.make_async_copy(grad_projected, grad_projected_out, sem.at[11])
    out.start()
    rows_out = RowsOut(buf, keep_buf, send_buf, section, lax.axis_index("dp"), groups, row_sems)
    rows_out.start(0, w_in_at)
    loads[8].wait()
    put_slabs(buf, w_in_at, nt(grad_projected[...], hin[...]))
    rows_out.start(w_in_at, end)
    _, g2, g3 = gains_of(small, width, inner)
    second, third = gain_and_bias(g2, (ag2, ab2)), gain_and_bias(g3, (ag3, ab3))
    put_rows(vec_out, [second[0], third[0], second[1], third[1]] + bias)
    out.wait()
    rows_out.wait()


def encoder_call(taps, groups, seq, gy, small_own, small_got, kept, own_out, got_out, own_conv, got_conv):
    width, tokens = gy.shape
    inner = own_out.shape[0]
    n1, s1, r, n2, s2, n3, s3, hin, shifted, hout = kept
    rows = layout(taps, width, inner)[3]
    half = padded_rows(rows, groups) // 2
    wide, narrow = (width, tokens), (inner, tokens)
    scratch = [
        (wide, BF), (narrow, BF), (narrow, BF), ((8, tokens), F32), ((inner * taps, tokens), BF),
        ((inner + 16, tokens), BF), (narrow, BF), (narrow, BF), (wide, BF), ((inner, width), BF),
        ((taps, inner, inner), BF), ((inner, inner * taps), BF), (narrow, F32), ((16, tokens), F32), (narrow, BF),
        ((inner * taps, tokens), BF), (narrow, BF), ((rows, LANES), BF),
    ]
    scratch += [((inner, LANES), F32)] * 4
    flops = 2 * tokens * inner * (3 * width + 2 * taps * inner)
    block = shape((half, LANES), BF)
    return pl.pallas_call(
        functools.partial(encoder_kernel, taps, groups),
        in_specs=[SMEM, ANY, VMEM, VMEM] + [ANY] * 12,
        out_specs=[ANY, VMEM, ANY, ANY],
        out_shape=[shape(narrow, BF), shape((SMALL_ROWS, width), F32), block, block],
        scratch_shapes=[pltpu.VMEM(dims, dtype) for dims, dtype in scratch]
        + [pltpu.SemaphoreType.DMA((12,)), pltpu.SemaphoreType.DMA((8 * share_count(groups[0]),))],
        compiler_params=pltpu.CompilerParams(vmem_limit_bytes=SMALL_LIMIT),
        cost_estimate=pl.CostEstimate(flops=4 * flops, bytes_accessed=20 * 2**20, transcendentals=0),
        name="encoder_back",
    )(
        seq, gy, small_own, small_got, n3, s3, r, shifted, hout, n2, s2, hin, own_out, got_out, own_conv, got_conv
    )


def first_kernel(
    block, gy_first, gy_second, grad_projected_in, small_own, small_got, vecs, n1_in, s1_in, r_in, own_in, got_in,
    *refs,
):
    outs_of, refs = refs[: 2 - block], refs[2 - block :]
    vec_out, gy, grad_projected, n1, s1, r, w_in_t, prod, means, gx, ag1, ab1, vec, sem = refs
    leading = lax.axis_index("section") == 0
    mine = leading if block == 0 else jnp.logical_not(leading)
    width, inner = gy.shape[0], grad_projected.shape[0]
    pairs = ((grad_projected_in, grad_projected), (s1_in, s1), (n1_in, n1), (r_in, r))
    loads = [pltpu.make_async_copy(a, b, sem.at[2 + i]) for i, (a, b) in enumerate(pairs)]
    loads[0].start()
    weight = load_weight(mine, own_in, got_in, w_in_t, sem.at[0])
    start_all(loads[1:])
    loads.append(load_weight(leading, gy_first, gy_second, gy, sem.at[1]))
    small = pick_small(mine, small_own, small_got)
    wait_all([loads[0], weight])

    def save(value, at_home, away, sem):
        pl.when(leading)(pltpu.make_async_copy(value, at_home, sem).start)
        pl.when(jnp.logical_not(leading))(pltpu.make_async_copy(value, away, sem).start)
        return pltpu.make_async_copy(value, away, sem)

    waits = []

    def ready():
        wait_all(loads[1:])
        if block == 0:
            outs, send = outs_of
            waits.append(save(gy, send, outs.at[1], sem.at[6]))

    back_first(gy, w_in_t, (n1, s1, r), prod, means, grad_projected, gx, ag1, ab1, ready)
    if block == 0:
        outs, send = outs_of
        waits.append(save(gx, outs.at[0], send, sem.at[7]))
    else:
        waits.append(pltpu.make_async_copy(gx, outs_of[0], sem.at[7]))
        waits[-1].start()
    sums = gain_and_bias(gains_of(small, width, inner)[0], (ag1, ab1))
    sums += [vecs[row : row + 1, 0:size] for row, size in enumerate((inner, inner, inner, inner, width))]
    put_vectors(vec_out, 0, vec, sums)
    wait_all(waits)


def first_call(block, gy_first, gy_second, grad_projected, vecs, kept, small_own, small_got, own_in, got_in):
    n1, s1, r = kept
    width, tokens = n1.shape
    inner = grad_projected.shape[0]
    wide, narrow = (width, tokens), (inner, tokens)
    scratch = [
        (wide, BF), (narrow, BF), (wide, BF), (wide, BF), ((8, tokens), F32), ((inner, width), BF), (wide, F32),
        ((16, tokens), F32), (wide, BF), ((width, LANES), F32), ((width, LANES), F32), ((VEC_ROWS, LANES), F32),
    ]
    outs = [shape((2,) + wide, BF), shape(wide, BF)] if block == 0 else [shape(wide, BF)]
    flops = 2 * tokens * inner * width
    return pl.pallas_call(
        functools.partial(first_kernel, block),
        in_specs=[ANY] * 3 + [VMEM] * 3 + [ANY] * 5,
        out_specs=[ANY] * len(outs) + [VMEM],
        out_shape=outs + [shape((VEC_ROWS, LANES), BF)],
        scratch_shapes=[pltpu.VMEM(dims, dtype) for dims, dtype in scratch] + [pltpu.SemaphoreType.DMA((8,))],
        compiler_params=pltpu.CompilerParams(vmem_limit_bytes=SMALL_LIMIT),
        cost_estimate=pl.CostEstimate(flops=8 * flops, bytes_accessed=20 * 2**20, transcendentals=0),
        name="first_%d" % block,
    )(gy_first, gy_second, grad_projected, small_own, small_got, vecs, n1, s1, r, own_in, got_in)


def load_weight(first, one, other, target, sem):
    pl.when(first)(pltpu.make_async_copy(one, target, sem).start)
    pl.when(jnp.logical_not(first))(pltpu.make_async_copy(other, target, sem).start)
    return pltpu.make_async_copy(one, target, sem)


def wait_all(copies):
    for copy in copies:
        copy.wait()


def unpack_kernel(taps_of, groups_of, *refs):
    refs = list(refs)

    def take(number):
        taken = refs[:number]
        del refs[:number]
        return taken

    own_of, got_of = [], []
    for _ in range(2):
        own_of.append(take(2))
        got_of.append(take(2))
    w_in_t_out, w_out_out, conv_out, gin, bin_, gmid, bmid, out_bias, w_in_t, w_out, conv, buf, extra, sem = refs
    inner, width = w_out.shape
    whole = inner // LANES
    tail = inner - whole * LANES
    slots = conv.shape[0]
    section = lax.axis_index("section")
    index = lax.axis_index("dp")

    def write(taps, groups, own, got):
        rows = own[0].shape[0] - VEC_ROWS
        count = share_count(groups[0])
        share = 2 * rows // count

        def body(position, _):
            for which, (pieces, side) in enumerate(((own, section), (got, 1 - section))):
                for at, ref in enumerate(pieces):
                    owner = owner_of(position + at * (count // 2), side, groups, index)
                    start = side * (2 * rows) + owner * share
                    pltpu.make_async_copy(
                        ref.at[pl.ds(pl.multiple_of(position * share, 16), share)],
                        buf.at[pl.ds(pl.multiple_of(start, 16), share)],
                        sem.at[2 * which + at],
                    ).start()
            return 0

        lax.fori_loop(0, count // 2, body, 0)
        pieces = list(own) + list(got)
        vectors = [
            pltpu.make_async_copy(ref.at[pl.ds(rows, VEC_ROWS)], extra.at[at], sem.at[4 + at])
            for at, ref in enumerate(pieces)
        ]
        start_all(vectors)
        for at, ref in enumerate(pieces):
            pltpu.make_async_copy(ref.at[pl.ds(0, rows)], buf.at[pl.ds(0, rows)], sem.at[at]).wait()
        wait_all(vectors)
        taps_at, tails_at, w_in_at, _, _ = layout(taps, width, inner)

        def wide(target, row):
            for at in range(0, width, LANES):
                q = at // LANES
                size = min(LANES, width - at)
                target[:, at : at + size] = buf[row + q * inner : row + (q + 1) * inner, 0:size].astype(F32)

        copies = []

        def leave(source, target):
            copies.append(pltpu.make_async_copy(source, target, sem.at[8 + len(copies)]))
            copies[-1].start()

        wide(w_out, 0)
        leave(w_out, w_out_out)
        tails = buf[tails_at : tails_at + inner, :].astype(F32)
        for k in range(slots):
            if k >= taps:
                conv[k] = jnp.zeros((inner, inner), F32)
            else:
                for q in range(whole):
                    at = taps_at + inner * (whole * k + q)
                    conv[k, :, LANES * q : LANES * (q + 1)] = buf[at : at + inner, :].astype(F32)
                conv[k, :, LANES * whole :] = tails[:, tail * k : tail * (k + 1)]
            leave(conv.at[k], conv_out.at[k])
        wide(w_in_t, w_in_at)
        leave(w_in_t, w_in_t_out)
        vec = sum(extra[at].astype(F32) for at in range(4))
        row = 0
        for target, member in ((gin, 0), (bin_, 0), (gmid, 0), (gmid, 1), (bmid, 0), (bmid, 1), (out_bias, 0)):
            for at in range(0, target.shape[1], LANES):
                size = min(LANES, target.shape[1] - at)
                target[member : member + 1, at : at + size] = vec[row : row + 1, 0:size]
                row += 1
        for copy in copies:
            copy.wait()

    pl.when(section == 0)(lambda: write(taps_of[0], groups_of[0], own_of[0], got_of[0]))
    pl.when(section != 0)(lambda: write(taps_of[1], groups_of[1], own_of[1], got_of[1]))


def unpack(taps_of, groups_of, enc, dec, width, inner):
    pieces = enc[0] + enc[1] + dec[0] + dec[1]
    rows = max(4 * part[0].shape[0] for part in (enc[0], dec[0]))
    return pl.pallas_call(
        functools.partial(unpack_kernel, taps_of, groups_of),
        in_specs=[ANY] * len(pieces),
        out_specs=[ANY] * 3 + [VMEM] * 5,
        out_shape=[
            shape((inner, width), F32), shape((inner, width), F32), shape((taps_of[0], inner, inner), F32),
            shape((1, width), F32), shape((1, width), F32), shape((2, inner), F32), shape((2, inner), F32),
            shape((1, width), F32),
        ],
        scratch_shapes=[
            pltpu.VMEM((inner, width), F32), pltpu.VMEM((inner, width), F32), pltpu.VMEM((taps_of[0], inner, inner), F32),
            pltpu.VMEM((rows, LANES), BF), pltpu.VMEM((4, VEC_ROWS, LANES), BF),
            pltpu.SemaphoreType.DMA((10 + taps_of[0],)),
        ],
        compiler_params=pltpu.CompilerParams(vmem_limit_bytes=SMALL_LIMIT),
        name="unpack",
    )(*pieces)


def swap_sections(value):
    return lax.ppermute(value, "section", [(0, 1), (1, 0)])


def swap_dp(value, masks):
    count = lax.axis_size("dp")
    pairs = [(s * count + i, s * count + (i ^ masks[s])) for s in range(2) for i in range(count)]
    return lax.ppermute(value, ("section", "dp"), pairs)


def rounded_sum(terms, rows):
    total = terms[0][rows].astype(F32)
    for term in terms[1:]:
        total = total + term[rows].astype(F32)
    return total.astype(BF)


def masks_of(bits, other):
    return [other << own[0] for own in bits]


def reduce_steps(keep, got, groups, receiver, vec=None):
    count = lax.axis_size("dp")
    steps = list(zip(*groups))
    terms = [keep, got]

    def loaded(part, riding):
        return part if vec is None or not riding else jnp.concatenate([part, vec], 0)

    for number, bits in enumerate(steps):
        size = terms[0].shape[0] >> len(bits[0])
        others = range(1, 2 ** len(bits[0]))
        parts = [rounded_sum(terms, slice(other * size, (other + 1) * size)) for other in others]
        parts = [loaded(part, number > 0) for part in parts]
        gate = yield parts
        came = after([swap_dp(part, masks_of(bits, other)) for part, other in zip(parts, others)], gate)
        terms = [term[:size] for term in terms] + [part[:size] for part in came]
        if vec is not None and number > 0:
            vec = rounded_sum([vec] + [part[size:] for part in came], slice(None))
    value = rounded_sum(terms, slice(None))
    rest = list(range(sum(len(bits) for bits in groups[0]), count.bit_length() - 1))
    for bits in zip(rest, rest[1:] + rest[:1]):
        size = value.shape[0]
        whole = loaded(value, True)
        gate = yield [whole]
        whole = rounded_sum([whole, after(swap_dp(whole, [1 << bit for bit in bits]), gate)], slice(None))
        value, vec = whole[:size], (None if vec is None else whole[size:])
    pieces = [value]
    for bits in reversed(steps[1:]):
        if len(pieces) > 1:
            value = jnp.concatenate(pieces, 0)
        gate = yield [value]
        came = [swap_dp(value, masks_of(bits, other)) for other in range(1, 2 ** len(bits[0]))]
        pieces = [value] + after(came, gate)
    if vec is not None:
        pieces = pieces + [vec]
    if len(pieces) > 1:
        value = jnp.concatenate(pieces, 0)
    gate = yield [value]
    sender = 1 - receiver
    masks = masks_of(steps[0], 1)
    ways = ((receiver, masks[receiver]), (sender, 0), (sender, masks[sender]))
    came = []
    for source, mask in ways:
        pairs = [(source * count + i, receiver * count + (i ^ mask)) for i in range(count)]
        came.append(lax.ppermute(value, ("section", "dp"), pairs))
    yield [value] + after(came, gate)


class Steps:
    def __init__(self, *args):
        self.steps = reduce_steps(*args)
        self.ready = next(self.steps)

    def step(self, gate=()):
        self.ready = self.steps.send(gate)
        return self.ready

    def finish(self):
        while len(self.ready) != 4:
            self.step()
        return self.ready[:2], self.ready[2:]


def after(values, earlier):
    return lax.optimization_barrier((values, earlier))[0] if earlier else values


def shards(
    section_inputs,
    seq_lengths,
    dilations,
    gains_in,
    biases_in,
    gains_mid,
    biases_mid,
    out_bias,
    w_in,
    w_out,
    conv_taps,
):
    section = lax.axis_index("section")
    count = lax.axis_size("dp")
    groups_of = (scatter_groups(count, False), scatter_groups(count, False))
    rows = jnp.swapaxes(section_inputs[0], 1, 2)
    width = rows.shape[1]
    inner = w_out.shape[1]
    taps_of = (conv_taps.shape[1], DEC_TAPS)

    own_w = (jnp.swapaxes(w_in[0], 0, 1), w_out[0], conv_taps[0])
    send_rows = pick_rows(rows)
    got_w = tuple(swap_sections(member) for member in own_w)
    got_rows = swap_sections(after(send_rows, got_w))
    small = pack_small(gains_in, biases_in, gains_mid[0], biases_mid[0], out_bias, dilations)
    got_small = swap_sections(small)

    outs, send_y, grad_dec, keep_dec, send_dec, vec, *kept = main_call(
        taps_of, groups_of[1], seq_lengths, rows, got_rows, small, got_small, own_w, got_w
    )
    dec = Steps(keep_dec, swap_sections(send_dec), groups_of[1], 1, vec)
    gradient = after(grad_dec, dec.ready)
    grad_projected, vec, keep_enc, send_enc = encoder_call(
        taps_of[0], groups_of[0], seq_lengths, gradient, small, got_small, kept, own_w[1], got_w[1], own_w[2], got_w[2]
    )
    got_y = swap_sections(send_y)
    enc_early = swap_sections(send_enc)
    grad_projected = after(grad_projected, dec.step())
    grads_x, send_gx, vec = first_call(
        0, grad_dec, grad_dec, grad_projected, vec, kept[0:3], small, got_small, own_w[0], got_w[0]
    )

    def joined(pair, got):
        pair = lax.dynamic_update_slice_in_dim(pair, got[None], 1 - section, 0)
        return jnp.swapaxes(pair, 1, 2)[None]

    enc = Steps(keep_enc, enc_early, groups_of[0], 0, vec)
    got_gx = swap_sections(send_gx)
    outputs = joined(outs, got_y)
    input_grads = joined(grads_x, got_gx)
    named = {"d": dec, "e": enc}
    last = ()
    for name in SEQ:
        if name in named:
            if len(named[name].ready) != 4:
                last = named[name].step(last)
        else:
            last = [*last, outputs if name == "y" else input_grads]
    enc = enc.finish()
    dec = dec.finish()
    grads = unpack(taps_of, groups_of, enc, dec, width, inner)
    return (
        outputs,
        input_grads,
        grads[3],
        grads[4],
        grads[5][None],
        grads[6][None],
        grads[7],
        jnp.swapaxes(grads[0], 0, 1)[None],
        grads[1][None],
        grads[2][None],
    )


def solution(mesh):
    in_specs = (
        P("section", None, "dp", None),
        P(None, "dp"),
        P("section"),
        P("section", None),
        P("section", None),
        P("section", None, None),
        P("section", None, None),
        P("section", None),
        P("section", None, None),
        P("section", None, None),
        P("section", None, None, None),
    )
    out_specs = (
        P("section", None, "dp", None),
        P("section", None, "dp", None),
        P("section", None),
        P("section", None),
        P("section", None, None),
        P("section", None, None),
        P("section", None),
        P("section", None, None),
        P("section", None, None),
        P("section", None, None, None),
    )
    return jax.shard_map(shards, mesh=mesh, in_specs=in_specs, out_specs=out_specs, check_vma=False)
```

```python
import functools

import jax
import jax.numpy as jnp
from jax import lax
from jax.experimental import pallas as pl
from jax.experimental.pallas import tpu as pltpu
from jax.sharding import PartitionSpec as P

DEC_TAPS = 3
EPS = 1e-05
LANES = 128
CHUNK = 80
VEC_ROWS = 48
SMALL_ROWS = 8
PIECES = 5
LOOPS = (False, False, True)
BF = jnp.bfloat16
F32 = jnp.float32
VMEM_LIMIT = 62 * 2**20
SMALL_LIMIT = 62 * 2**20
SEQ = "ddeedeyxdede"
ANY = pl.BlockSpec(memory_space=pl.ANY)
SMEM = pl.BlockSpec(memory_space=pltpu.SMEM)
VMEM = pl.BlockSpec(memory_space=pltpu.VMEM)


def shape(dims, dtype):
    return jax.ShapeDtypeStruct(tuple(dims), dtype)


def nn(left, right):
    return jnp.dot(left, right, preferred_element_type=F32)


def nt(left, right):
    return lax.dot_general(left, right, (((1,), (1,)), ((), ())), preferred_element_type=F32)


def tn(left, right):
    return lax.dot_general(left, right, (((0,), (0,)), ((), ())), preferred_element_type=F32)


def lane_block(index):
    return pl.ds(pl.multiple_of(index * LANES, LANES), LANES)


def chunks(rows):
    size = CHUNK if rows % CHUNK == 0 else 16
    return [slice(at, at + size) for at in range(0, rows, size)]


def folded(values):
    return jnp.sum(values.reshape(values.shape[0] // 8, 8, values.shape[1]), 0)


def column(vector):
    return jnp.broadcast_to(vector, (LANES, vector.shape[1])).T


def norm_forward(source, half_gain, half_bias, normed, slope, hidden, devs, row, units):
    feats, tokens = source.shape
    scale = 1.0 / feats

    def stats(here):
        base = source[0:1, here].astype(F32)
        total = jnp.zeros((8, LANES), F32)
        squares = jnp.zeros((8, LANES), F32)
        for part in chunks(feats):
            moved = source[part, here].astype(F32) - base
            total = total + folded(moved)
            squares = squares + folded(moved * moved)
        average = jnp.sum(total, 0, keepdims=True) * scale
        variance = jnp.sum(squares, 0, keepdims=True) * scale - average * average
        inverse_dev = lax.rsqrt(jnp.maximum(variance, 0.0) + EPS)
        return (average + base) * inverse_dev, inverse_dev

    def finish(here, offset, inverse_dev):
        devs[row : row + 1, here] = inverse_dev
        for part in chunks(feats):
            values = source[part, here].astype(F32) * inverse_dev - offset
            gain = half_gain[part, :]
            half = values * gain + half_bias[part, :]
            tan = jnp.tanh(half)
            weight = 1.0 + tan
            out = half * weight
            normed[part, here] = values.astype(BF)
            slope[part, here] = ((weight + out * (1.0 - tan)) * gain).astype(BF)
            hidden[part, here] = out.astype(hidden.dtype)

    if units is None:

        def body(unit, carry):
            following = stats(lane_block(jnp.minimum(unit + 1, tokens // LANES - 1)))
            finish(lane_block(unit), *carry)
            return following

        lax.fori_loop(0, tokens // LANES, body, stats(lane_block(0)))
        return
    for unit in units:
        here = slice(unit * LANES, (unit + 1) * LANES)
        finish(here, *stats(here))


def norm_backward(gradient, slope, normed, devs, row, gain_sums, bias_sums, means, emit, loops):
    feats, tokens = gradient.shape
    units = tokens // LANES
    scale = 1.0 / feats
    means[...] = jnp.zeros_like(means)

    def collect(rows, size):
        gain_sum = jnp.zeros((size, LANES), F32)
        bias_sum = jnp.zeros((size, LANES), F32)
        for unit in range(units):
            here = slice(unit * LANES, (unit + 1) * LANES)
            scaled = gradient[rows, here] * slope[rows, here].astype(F32)
            weighted = scaled * normed[rows, here].astype(F32)
            gain_sum = gain_sum + weighted
            bias_sum = bias_sum + scaled
            means[0:8, here] += folded(scaled)
            means[8:16, here] += folded(weighted)
        gain_sums[rows, :] = gain_sum
        bias_sums[rows, :] = bias_sum

    def finish(here):
        inverse_dev = devs[row : row + 1, here]
        first = jnp.sum(means[0:8, here], 0, keepdims=True) * (scale * inverse_dev)
        second = jnp.sum(means[8:16, here], 0, keepdims=True) * (scale * inverse_dev)
        for part in chunks(feats):
            scaled = gradient[part, here] * slope[part, here].astype(F32)
            emit(part, here, scaled * inverse_dev - first - normed[part, here].astype(F32) * second)

    if loops:
        size = chunks(feats)[0].stop

        def one_chunk(index, _):
            collect(pl.ds(pl.multiple_of(index * size, 16), size), size)
            return 0

        def one_unit(unit, _):
            finish(lane_block(unit))
            return 0

        lax.fori_loop(0, feats // size, one_chunk, 0)
        lax.fori_loop(0, units, one_unit, 0, unroll=2)
        return
    for part in chunks(feats):
        collect(part, part.stop - part.start)
    for unit in range(units):
        finish(slice(unit * LANES, (unit + 1) * LANES))


def write_shifts(source, target, begins, offsets, units):
    feats, tokens = source.shape
    count = tokens // LANES
    block = lambda unit: slice(unit * LANES, (unit + 1) * LANES)
    for unit in units:
        joined_behind = (begins(unit) == 0).astype(F32) if unit > 0 else None
        joined_ahead = (begins(unit + 1) == 0).astype(F32) if unit < count - 1 else None
        for part in chunks(feats):
            size = part.stop - part.start
            lane = lax.broadcasted_iota(jnp.int32, (size, LANES), 1)
            zero = jnp.zeros((size, LANES), F32)
            current = source[part, block(unit)].astype(F32)
            behind = zero if unit == 0 else source[part, block(unit - 1)].astype(F32) * joined_behind
            ahead = zero if unit == count - 1 else source[part, block(unit + 1)].astype(F32) * joined_ahead
            for position, (sign, step) in enumerate(offsets):
                if sign == 0:
                    moved = current
                elif sign < 0:
                    moved = pltpu.roll(jnp.where(lane < LANES - step, current, behind), step, 1)
                else:
                    moved = pltpu.roll(jnp.where(lane >= step, current, ahead), LANES - step, 1)
                rows = slice(feats * position + part.start, feats * position + part.stop)
                target[rows, block(unit)] = moved.astype(BF)


def tap_offsets(taps, dilation, flip):
    result = []
    for position in range(taps):
        factor = (position - 2) * (-1 if flip else 1)
        result.append(((factor > 0) - (factor < 0), abs(factor) * dilation))
    return result


def layout(taps, width, inner):
    wide = pl.cdiv(width, LANES) * inner
    taps_at = wide
    tails_at = taps_at + taps * (inner // LANES) * inner
    w_in_at = tails_at + inner
    vec_at = w_in_at + wide
    return taps_at, tails_at, w_in_at, vec_at, vec_at + VEC_ROWS


def scatter_groups(count, full):
    total = count.bit_length() - 1
    rest = [list(range(2, min(4, total)))] if full and total > 2 else []
    return [[[bit] for bit in bits if bit < total] + rest for bits in ((0, 1), (1, 0))]


def share_count(groups):
    return 2 ** sum(len(bits) for bits in groups)


def padded_rows(rows, groups):
    unit = 2 * 16 * share_count(groups[0])
    return pl.cdiv(rows, unit) * unit


def put_slabs(buf, row, matrix):
    rows, cols = matrix.shape
    for q in range(pl.cdiv(cols, LANES)):
        part = matrix[:, LANES * q : min(cols, LANES * (q + 1))]
        if part.shape[1] < LANES:
            part = jnp.concatenate([part, jnp.zeros((rows, LANES - part.shape[1]), F32)], 1)
        buf[row + q * rows : row + (q + 1) * rows, :] = part.astype(BF)


def put_taps(buf, taps, width, shifted, grad_mixed):
    inner = grad_mixed.shape[0]
    taps_at, tails_at, _, _, _ = layout(taps, width, inner)
    whole = inner // LANES
    tail = inner - whole * LANES
    for k in range(taps):
        grad = nt(shifted[inner * k : inner * (k + 1), :], grad_mixed[...])
        for q in range(whole):
            at = taps_at + inner * (whole * k + q)
            buf[at : at + inner, :] = grad[:, LANES * q : LANES * (q + 1)].astype(BF)
        buf[tails_at : tails_at + inner, tail * k : tail * (k + 1)] = grad[:, LANES * whole :].astype(BF)
    buf[tails_at : tails_at + inner, tail * taps :] = jnp.zeros((inner, LANES - tail * taps), BF)


def row_sums(acc):
    return jnp.sum(acc.T, 0, keepdims=True)


def put_vectors(buf, at, vec, sums):
    vec[...] = jnp.zeros_like(vec)
    row = 0
    for total in sums:
        for lane in range(0, total.shape[1], LANES):
            part = total[:, lane : lane + LANES]
            vec[row : row + 1, 0 : part.shape[1]] = part
            row += 1
    buf[at : at + VEC_ROWS, :] = vec[...].astype(BF)


def relative_index(position, groups):
    result = 0
    for bits in reversed(groups):
        size = 2 ** len(bits)
        result = result + (position & (size - 1)) * 2 ** bits[0]
        position = position >> len(bits)
    return result


def owner_of(position, side, groups, index):
    both = [relative_index(position, order) for order in groups]
    mask = sum(2**bit for bits in groups[0] for bit in bits)
    return jnp.where(side == 0, both[0], both[1]) ^ (index & mask)


def position_of(owner, side, groups, index):
    distance = owner ^ index
    position = 0
    for bits in groups[side]:
        position = position * 2 ** len(bits) + ((distance >> bits[0]) & (2 ** len(bits) - 1))
    return position


class RowsOut:
    def __init__(self, buf, keep, send, section, index, groups, sems):
        self.buf, self.keep, self.send, self.sems = buf, keep, send, sems
        self.section, self.index, self.groups = section, index, groups
        self.count = share_count(groups[0])
        self.share = keep.shape[0] // self.count
        self.sizes = []

    def start(self, first, last):
        for number in range(2 * self.count):
            low, high = max(first, number * self.share), min(last, (number + 1) * self.share)
            if low >= high:
                continue
            side, owner = divmod(number, self.count)
            place = position_of(owner, side, self.groups, self.index) * self.share + (low - number * self.share)
            target = pl.ds(pl.multiple_of(place, 16), high - low)
            source = self.buf.at[low:high]
            sem = self.sems.at[len(self.sizes)]
            pl.when(self.section == side)(pltpu.make_async_copy(source, self.keep.at[target], sem).start)
            pl.when(self.section != side)(pltpu.make_async_copy(source, self.send.at[target], sem).start)
            self.sizes.append(high - low)

    def wait(self):
        for number, size in enumerate(self.sizes):
            source, target = self.buf.at[0:size], self.keep.at[0:size]
            pltpu.make_async_copy(source, target, self.sems.at[number]).wait()


def forward_block(taps, begins, dilation, x, y, weights, turned, cols, kept, hmid, prod, ready):
    w_in_t, w_out, conv = weights
    w_out_t, conv_t = turned
    g1, b1, g2, b2, g3, b3, ob = cols
    n1, s1, r, n2, s2, n3, s3, hin, shifted, hout = kept
    inner, tokens = hmid.shape
    units = tokens // LANES
    narrow = prod.at[0:inner]
    parts = [range(at, min(at + units // 2, units)) for at in range(0, units, units // 2)]
    columns = [slice(part.start * LANES, part.stop * LANES) for part in parts]
    offsets = tap_offsets(taps, dilation, False)

    def mix(part):
        narrow[:, columns[part]] = nn(conv_t[:, 0 : taps * inner], shifted[:, columns[part]])

    def leave(part):
        here = columns[part]
        bias = jnp.concatenate([ob[...]] * len(parts[part]), 1)
        y[:, here] = (x[:, here].astype(F32) + nn(w_out_t[...], hout[:, here]) + bias).astype(BF)

    norm_forward(x, g1, b1, n1, s1, hin, r, 0, None)
    ready(0)
    narrow[...] = nn(w_in_t[...], hin[...])
    ready(1)
    norm_forward(narrow, g2, b2, n2, s2, hmid, r, 1, parts[0])
    for k in range(taps):
        conv_t[:, inner * k : inner * (k + 1)] = conv[k].T
    w_out_t[...] = w_out[...].T
    norm_forward(narrow, g2, b2, n2, s2, hmid, r, 1, parts[1])
    write_shifts(hmid, shifted, begins, offsets, parts[0])
    mix(0)
    write_shifts(hmid, shifted, begins, offsets, parts[1])
    mix(1)
    norm_forward(narrow, g3, b3, n3, s3, hout, r, 2, parts[0])
    leave(0)
    norm_forward(narrow, g3, b3, n3, s3, hout, r, 2, parts[1])
    leave(1)


def fill_columns(small, cols):
    g1, b1, g2, b2, g3, b3, ob = cols
    width, inner = g1.shape[0], g2.shape[0]
    for target, row, scale in ((g1, 0, 0.5), (b1, 1, 0.5), (ob, 2, 1.0)):
        target[...] = column(small[row : row + 1, 0:width] * scale)
    for target, row in ((g2, 3), (b2, 4), (g3, 5), (b3, 6)):
        target[...] = column(small[row : row + 1, 0:inner] * 0.5)


def back_third(gy, w_out, kept, prod, means, grad_mixed, gain_sums, bias_sums, beside):
    n3, s3, r = kept
    inner = w_out.shape[0]
    narrow = prod.at[0:inner]
    narrow[...] = nn(w_out[...], gy[...])
    beside()

    def emit(part, here, value):
        grad_mixed[part, here] = value.astype(BF)

    norm_backward(narrow, s3, n3, r, 2, gain_sums, bias_sums, means, emit, LOOPS[0])


def back_second(
    taps, begins, dilation, conv_w, kept, prod, means, grad_mixed, moved, grad_projected, gain_sums, bias_sums, ready,
    weights=None,
):
    n2, s2, r = kept
    inner = grad_mixed.shape[0]
    narrow = prod.at[0:inner]
    write_shifts(grad_mixed, moved, begins, tap_offsets(taps, dilation, True), range(grad_mixed.shape[1] // LANES))
    if weights is not None:
        weights()
    narrow[...] = nn(conv_w[...], moved[...])
    ready()

    def emit(part, here, value):
        grad_projected[part, here] = value.astype(BF)

    norm_backward(narrow, s2, n2, r, 1, gain_sums, bias_sums, means, emit, LOOPS[1])


def back_first(gy, w_in_t, kept, prod, means, grad_projected, gx, gain_sums, bias_sums, ready):
    n1, s1, r = kept
    prod[...] = tn(w_in_t[...], grad_projected[...])
    ready()

    def emit(part, here, value):
        gx[part, here] = (gy[part, here].astype(F32) + value).astype(BF)

    norm_backward(prod, s1, n1, r, 0, gain_sums, bias_sums, means, emit, LOOPS[2])


def put_w_out(buf, hout_ones, gy):
    grad = nt(hout_ones[...], gy[...])
    inner = hout_ones.shape[0] - 16
    put_slabs(buf, 0, grad[0:inner])
    return grad[inner : inner + 1]


def gain_and_bias(gain, sums):
    return [row_sums(acc[...]) / gain for acc in sums]


def put_rows(target, rows):
    target[...] = jnp.zeros_like(target)
    for at, row in enumerate(rows):
        target[at : at + 1, 0 : row.shape[1]] = row


def gains_of(small, width, inner):
    return small[0:1, 0:width], small[3:4, 0:inner], small[5:6, 0:inner]


def pick_small(leading, own, got):
    flag = leading.astype(F32)
    return own[...] * flag + got[...] * (1.0 - flag)


def start_all(copies):
    for copy in copies:
        copy.start()


def pick_rows_kernel(rows, send, hold, sem):
    section = lax.axis_index("section")
    size = send.shape[0] // PIECES
    parts = [slice(size * i, size * (i + 1)) for i in range(PIECES)]
    arrive = [
        pltpu.make_async_copy(rows.at[1 - section, part], hold.at[part], sem.at[i]) for i, part in enumerate(parts)
    ]
    leave = [pltpu.make_async_copy(hold.at[part], send.at[part], sem.at[PIECES + i]) for i, part in enumerate(parts)]
    start_all(arrive)
    for come, go in zip(arrive, leave):
        come.wait()
        go.start()
    for go in leave:
        go.wait()


def pick_rows(rows):
    return pl.pallas_call(
        pick_rows_kernel,
        in_specs=[ANY],
        out_specs=ANY,
        out_shape=shape(rows.shape[1:], BF),
        scratch_shapes=[pltpu.VMEM(rows.shape[1:], BF), pltpu.SemaphoreType.DMA((2 * PIECES,))],
        compiler_params=pltpu.CompilerParams(vmem_limit_bytes=VMEM_LIMIT),
        cost_estimate=pl.CostEstimate(flops=0, bytes_accessed=8 * 2**20, transcendentals=0),
        name="pick_rows",
    )(rows)


def pack_small_kernel(gin, bin_, gmid, bmid, out_bias, dilation, small):
    width, inner = gin.shape[1], gmid.shape[1]
    small[...] = jnp.zeros_like(small)
    for row, ref in ((0, gin), (1, bin_), (2, out_bias)):
        small[row : row + 1, 0:width] = ref[...]
    for row, ref, which in ((3, gmid, 0), (4, bmid, 0), (5, gmid, 1), (6, bmid, 1)):
        small[row : row + 1, 0:inner] = ref[which : which + 1, :]
    small[7:8, :] = jnp.full((1, small.shape[1]), dilation[0].astype(F32), F32)


def pack_small(gin, bin_, gmid, bmid, out_bias, dilation):
    return pl.pallas_call(
        pack_small_kernel,
        in_specs=[VMEM] * 5 + [SMEM],
        out_specs=VMEM,
        out_shape=shape((SMALL_ROWS, gin.shape[1]), F32),
        compiler_params=pltpu.CompilerParams(vmem_limit_bytes=VMEM_LIMIT),
        name="pack_small",
    )(gin, bin_, gmid, bmid, out_bias, dilation)


def kept_shapes(taps, width, inner, tokens):
    wide, narrow = (width, tokens), (inner, tokens)
    return [
        (wide, BF), (wide, BF), ((8, tokens), F32), (narrow, BF), (narrow, BF), (narrow, BF), (narrow, BF),
        (wide, BF), ((inner * taps, tokens), BF), (narrow, BF),
    ]


def column_shapes(width, inner):
    return [(width, LANES)] * 2 + [(inner, LANES)] * 4 + [(width, LANES)]


def main_kernel(taps_of, groups, *refs):
    refs = list(refs)

    def take(number):
        taken = refs[:number]
        del refs[:number]
        return taken

    seq, rows, got, small_own, small_got = take(5)
    own_w, got_w = take(3), take(3)
    outs, send_y, grad_out, keep_buf, send_buf, vec_out = take(6)
    kept_out = take(10)
    x, cot = take(2)
    enc_w, dec_w = take(3), take(3)
    small = take(2)
    enc_kept, dec_kept = take(10), take(10)
    cols = take(7)
    hmid, prod, means, y_enc, gx, w_out_t, conv_t, conv_w, grad_mixed, grad_projected, moved, buf = take(12)
    ag1, ab1, ag2, ab2, ag3, ab3, vec, sem, row_sems = take(9)

    section = lax.axis_index("section")
    index = lax.axis_index("dp")
    leading = section == 0
    width, tokens = x.shape
    inner = hmid.shape[0]
    small[0][...] = pick_small(leading, small_own, small_got)
    small[1][...] = pick_small(leading, small_got, small_own)
    dilation = [jnp.max(member[7:8, 0:LANES]).astype(jnp.int32) for member in small]

    def begins(unit):
        return seq[section, unit]

    loads = [(x, rows.at[0], got), (enc_w[0], own_w[0], got_w[0]), (enc_w[2], own_w[2], got_w[2])]
    loads += [(enc_w[1], own_w[1], got_w[1]), (dec_w[0], got_w[0], own_w[0]), (dec_w[1], got_w[1], own_w[1])]
    loads += [(dec_w[2], got_w[2].at[0 : taps_of[1]], own_w[2].at[0 : taps_of[1]]), (cot, got, rows.at[1])]

    def load(at):
        target, first, second = loads[at]
        pl.when(leading)(pltpu.make_async_copy(first, target, sem.at[at]).start)
        pl.when(jnp.logical_not(leading))(pltpu.make_async_copy(second, target, sem.at[at]).start)

    for at in range(4):
        load(at)

    def ready(at):
        pltpu.make_async_copy(loads[at][1], loads[at][0], sem.at[at]).wait()

    fill_columns(small[0], cols)
    hout_ones = dec_kept[9]
    dec_kept[9] = hout_ones.at[0:inner]
    hout_ones[inner:, :] = jnp.ones((16, tokens), BF)
    ready(0)

    def enc_ready(which):
        for at in ((1,), (2, 3))[which]:
            ready(at)
        if which:
            for at in range(4, 8):
                load(at)

    turned = (w_out_t, conv_t)
    forward_block(taps_of[0], begins, dilation[0], x, y_enc, enc_w, turned, cols, enc_kept, hmid, prod, enc_ready)
    saves = [pltpu.make_async_copy(a, b, sem.at[8 + i]) for i, (a, b) in enumerate(zip(enc_kept, kept_out))]
    start_all(saves)

    fill_columns(small[1], cols)
    for at in range(4, 8):
        ready(at)
    for k in range(taps_of[1]):
        conv_w[:, inner * k : inner * (k + 1)] = dec_w[2][k]
    y_dec = x
    forward_block(
        taps_of[1], begins, dilation[1], y_enc, y_dec, dec_w, turned, cols, dec_kept, hmid, prod, lambda which: None
    )
    pl.when(leading)(pltpu.make_async_copy(y_enc, outs.at[0], sem.at[18]).start)
    pl.when(leading)(pltpu.make_async_copy(y_dec, send_y, sem.at[19]).start)
    pl.when(jnp.logical_not(leading))(pltpu.make_async_copy(y_dec, outs.at[1], sem.at[18]).start)
    pl.when(jnp.logical_not(leading))(pltpu.make_async_copy(y_enc, send_y, sem.at[19]).start)

    n1, s1, r, n2, s2, n3, s3, hin, shifted, hout = dec_kept
    rows_out = RowsOut(buf, keep_buf, send_buf, section, index, groups, row_sems)
    w_in_at, end = layout(taps_of[1], width, inner)[2:4]

    bias = []

    def third_beside():
        bias.append(put_w_out(buf, hout_ones, cot))

    def first_beside():
        put_slabs(buf, w_in_at, nt(grad_projected[...], hin[...]))

    back_third(cot, dec_w[1], (n3, s3, r), prod, means, grad_mixed, ag3, ab3, third_beside)
    put_taps(buf, taps_of[1], width, shifted, grad_mixed)
    back_second(
        taps_of[1], begins, dilation[1], conv_w, (n2, s2, r), prod, means, grad_mixed, moved, grad_projected, ag2, ab2,
        lambda: None,
    )
    rows_out.start(0, w_in_at)
    back_first(cot, dec_w[0], (n1, s1, r), prod, means, grad_projected, gx, ag1, ab1, first_beside)
    rows_out.start(w_in_at, end)
    last = pltpu.make_async_copy(gx, grad_out, sem.at[20])
    last.start()
    g1, g2, g3 = gains_of(small[1], width, inner)
    first, second, third = gain_and_bias(g1, (ag1, ab1)), gain_and_bias(g2, (ag2, ab2)), gain_and_bias(g3, (ag3, ab3))
    put_vectors(vec_out, 0, vec, first + [second[0], third[0], second[1], third[1]] + bias)
    rows_out.wait()
    wait_all(saves + [last])
    pltpu.make_async_copy(y_enc, outs.at[0], sem.at[18]).wait()
    pltpu.make_async_copy(y_dec, send_y, sem.at[19]).wait()


def main_call(taps_of, groups, seq, rows, got, small_own, small_got, own_w, got_w):
    _, width, tokens = rows.shape
    inner = own_w[1].shape[0]
    half = padded_rows(layout(taps_of[1], width, inner)[3], groups) // 2
    wide, narrow = (width, tokens), (inner, tokens)
    weight_shapes = [(inner, width), (inner, width)]
    scratch = [(wide, BF)] * 2
    for taps in taps_of:
        scratch += [(dims, BF) for dims in weight_shapes + [(taps, inner, inner)]]
    scratch += [((SMALL_ROWS, width), F32)] * 2
    scratch += kept_shapes(taps_of[0], width, inner, tokens) + kept_shapes(taps_of[1], width, inner, tokens)[:-1]
    scratch += [((inner + 16, tokens), BF)]
    scratch += [(dims, F32) for dims in column_shapes(width, inner)]
    scratch += [
        (narrow, BF), (wide, F32), ((16, tokens), F32), (wide, BF), (wide, BF), ((width, inner), BF),
        ((inner, inner * taps_of[0]), BF), ((inner, inner * taps_of[1]), BF),
        (narrow, BF), (narrow, BF), ((inner * taps_of[1], tokens), BF), ((2 * half, LANES), BF),
    ]
    scratch += [((width, LANES), F32)] * 2 + [((inner, LANES), F32)] * 4 + [((VEC_ROWS, LANES), F32)]
    block = shape((half, LANES), BF)
    outs = [shape((2,) + wide, BF), shape(wide, BF), shape(wide, BF), block, block, shape((VEC_ROWS, LANES), BF)]
    outs += [shape(dims, dtype) for dims, dtype in kept_shapes(taps_of[0], width, inner, tokens)]
    flops = 2 * tokens * inner * (2 * width + taps_of[0] * inner + 3 * (2 * width + taps_of[1] * inner))
    return pl.pallas_call(
        functools.partial(main_kernel, taps_of, groups),
        in_specs=[SMEM, ANY, ANY, VMEM, VMEM] + [ANY] * 6,
        out_specs=[ANY] * 5 + [VMEM] + [ANY] * 10,
        out_shape=outs,
        scratch_shapes=[pltpu.VMEM(dims, dtype) for dims, dtype in scratch]
        + [pltpu.SemaphoreType.DMA((24,)), pltpu.SemaphoreType.DMA((8 * share_count(groups[0]),))],
        compiler_params=pltpu.CompilerParams(vmem_limit_bytes=VMEM_LIMIT),
        cost_estimate=pl.CostEstimate(flops=4 * flops, bytes_accessed=60 * 2**20, transcendentals=0),
        name="main_blocks",
    )(seq, rows, got, small_own, small_got, *own_w, *got_w)


def load_weight(leading, own, got, target, sem):
    pl.when(leading)(pltpu.make_async_copy(own, target, sem).start)
    pl.when(jnp.logical_not(leading))(pltpu.make_async_copy(got, target, sem).start)
    return pltpu.make_async_copy(own, target, sem)


def wait_all(copies):
    for copy in copies:
        copy.wait()


def encoder_kernel(
    taps, groups,
    seq, gy_in, small_own, small_got, n3_in, s3_in, r_in, shifted_in, hout_in, n2_in, s2_in, hin_in, own_out, got_out,
    own_conv, got_conv,
    grad_projected_out, vec_out, keep_buf, send_buf,
    gy, n3, s3, r, shifted, hout_ones, n2, s2, hin, w_out, conv, conv_w, prod, means, grad_mixed, moved, grad_projected,
    buf, ag3, ab3, ag2, ab2, sem, row_sems,
):
    section = lax.axis_index("section")
    leading = section == 0
    width, tokens = gy.shape
    inner = w_out.shape[0]
    w_in_at, end = layout(taps, width, inner)[2:4]
    hout = hout_ones.at[0:inner]
    pairs = (
        (gy_in, gy), (s3_in, s3), (n3_in, n3), (r_in, r), (hout_in, hout), (shifted_in, shifted), (n2_in, n2), (s2_in, s2),
        (hin_in, hin),
    )
    loads = [pltpu.make_async_copy(a, b, sem.at[2 + i]) for i, (a, b) in enumerate(pairs)]
    loads[0].start()
    weight = load_weight(leading, own_out, got_out, w_out, sem.at[0])
    start_all(loads[1:5])
    conv_weight = load_weight(leading, own_conv, got_conv, conv, sem.at[1])
    start_all(loads[5:])
    hout_ones[inner:, :] = jnp.ones((16, tokens), BF)
    small = pick_small(leading, small_own, small_got)
    dilation = jnp.max(small[7:8, 0:LANES]).astype(jnp.int32)

    def begins(unit):
        return seq[section, unit]

    def weights():
        conv_weight.wait()
        for k in range(taps):
            conv_w[:, inner * k : inner * (k + 1)] = conv[k]

    wait_all([weight, loads[0]])
    bias = []

    def third_beside():
        wait_all(loads[1:5])
        bias.append(put_w_out(buf, hout_ones, gy))

    back_third(gy, w_out, (n3, s3, r), prod, means, grad_mixed, ag3, ab3, third_beside)
    wait_all([loads[5]])
    put_taps(buf, taps, width, shifted, grad_mixed)
    back_second(
        taps, begins, dilation, conv_w, (n2, s2, r), prod, means, grad_mixed, moved, grad_projected, ag2, ab2,
        lambda: wait_all(loads[6:8]), weights,
    )
    out = pltpu.make_async_copy(grad_projected, grad_projected_out, sem.at[11])
    out.start()
    rows_out = RowsOut(buf, keep_buf, send_buf, section, lax.axis_index("dp"), groups, row_sems)
    rows_out.start(0, w_in_at)
    loads[8].wait()
    put_slabs(buf, w_in_at, nt(grad_projected[...], hin[...]))
    rows_out.start(w_in_at, end)
    _, g2, g3 = gains_of(small, width, inner)
    second, third = gain_and_bias(g2, (ag2, ab2)), gain_and_bias(g3, (ag3, ab3))
    put_rows(vec_out, [second[0], third[0], second[1], third[1]] + bias)
    out.wait()
    rows_out.wait()


def encoder_call(taps, groups, seq, gy, small_own, small_got, kept, own_out, got_out, own_conv, got_conv):
    width, tokens = gy.shape
    inner = own_out.shape[0]
    n1, s1, r, n2, s2, n3, s3, hin, shifted, hout = kept
    rows = layout(taps, width, inner)[3]
    half = padded_rows(rows, groups) // 2
    wide, narrow = (width, tokens), (inner, tokens)
    scratch = [
        (wide, BF), (narrow, BF), (narrow, BF), ((8, tokens), F32), ((inner * taps, tokens), BF),
        ((inner + 16, tokens), BF), (narrow, BF), (narrow, BF), (wide, BF), ((inner, width), BF),
        ((taps, inner, inner), BF), ((inner, inner * taps), BF), (narrow, F32), ((16, tokens), F32), (narrow, BF),
        ((inner * taps, tokens), BF), (narrow, BF), ((rows, LANES), BF),
    ]
    scratch += [((inner, LANES), F32)] * 4
    flops = 2 * tokens * inner * (3 * width + 2 * taps * inner)
    block = shape((half, LANES), BF)
    return pl.pallas_call(
        functools.partial(encoder_kernel, taps, groups),
        in_specs=[SMEM, ANY, VMEM, VMEM] + [ANY] * 12,
        out_specs=[ANY, VMEM, ANY, ANY],
        out_shape=[shape(narrow, BF), shape((SMALL_ROWS, width), F32), block, block],
        scratch_shapes=[pltpu.VMEM(dims, dtype) for dims, dtype in scratch]
        + [pltpu.SemaphoreType.DMA((12,)), pltpu.SemaphoreType.DMA((8 * share_count(groups[0]),))],
        compiler_params=pltpu.CompilerParams(vmem_limit_bytes=SMALL_LIMIT),
        cost_estimate=pl.CostEstimate(flops=4 * flops, bytes_accessed=20 * 2**20, transcendentals=0),
        name="encoder_back",
    )(
        seq, gy, small_own, small_got, n3, s3, r, shifted, hout, n2, s2, hin, own_out, got_out, own_conv, got_conv
    )


def first_kernel(
    block, gy_first, gy_second, grad_projected_in, small_own, small_got, vecs, n1_in, s1_in, r_in, own_in, got_in,
    *refs,
):
    outs_of, refs = refs[: 2 - block], refs[2 - block :]
    vec_out, gy, grad_projected, n1, s1, r, w_in_t, prod, means, gx, ag1, ab1, vec, sem = refs
    leading = lax.axis_index("section") == 0
    mine = leading if block == 0 else jnp.logical_not(leading)
    width, inner = gy.shape[0], grad_projected.shape[0]
    pairs = ((grad_projected_in, grad_projected), (s1_in, s1), (n1_in, n1), (r_in, r))
    loads = [pltpu.make_async_copy(a, b, sem.at[2 + i]) for i, (a, b) in enumerate(pairs)]
    loads[0].start()
    weight = load_weight(mine, own_in, got_in, w_in_t, sem.at[0])
    start_all(loads[1:])
    loads.append(load_weight(leading, gy_first, gy_second, gy, sem.at[1]))
    small = pick_small(mine, small_own, small_got)
    wait_all([loads[0], weight])

    def save(value, at_home, away, sem):
        pl.when(leading)(pltpu.make_async_copy(value, at_home, sem).start)
        pl.when(jnp.logical_not(leading))(pltpu.make_async_copy(value, away, sem).start)
        return pltpu.make_async_copy(value, away, sem)

    waits = []

    def ready():
        wait_all(loads[1:])
        if block == 0:
            outs, send = outs_of
            waits.append(save(gy, send, outs.at[1], sem.at[6]))

    back_first(gy, w_in_t, (n1, s1, r), prod, means, grad_projected, gx, ag1, ab1, ready)
    if block == 0:
        outs, send = outs_of
        waits.append(save(gx, outs.at[0], send, sem.at[7]))
    else:
        waits.append(pltpu.make_async_copy(gx, outs_of[0], sem.at[7]))
        waits[-1].start()
    sums = gain_and_bias(gains_of(small, width, inner)[0], (ag1, ab1))
    sums += [vecs[row : row + 1, 0:size] for row, size in enumerate((inner, inner, inner, inner, width))]
    put_vectors(vec_out, 0, vec, sums)
    wait_all(waits)


def first_call(block, gy_first, gy_second, grad_projected, vecs, kept, small_own, small_got, own_in, got_in):
    n1, s1, r = kept
    width, tokens = n1.shape
    inner = grad_projected.shape[0]
    wide, narrow = (width, tokens), (inner, tokens)
    scratch = [
        (wide, BF), (narrow, BF), (wide, BF), (wide, BF), ((8, tokens), F32), ((inner, width), BF), (wide, F32),
        ((16, tokens), F32), (wide, BF), ((width, LANES), F32), ((width, LANES), F32), ((VEC_ROWS, LANES), F32),
    ]
    outs = [shape((2,) + wide, BF), shape(wide, BF)] if block == 0 else [shape(wide, BF)]
    flops = 2 * tokens * inner * width
    return pl.pallas_call(
        functools.partial(first_kernel, block),
        in_specs=[ANY] * 3 + [VMEM] * 3 + [ANY] * 5,
        out_specs=[ANY] * len(outs) + [VMEM],
        out_shape=outs + [shape((VEC_ROWS, LANES), BF)],
        scratch_shapes=[pltpu.VMEM(dims, dtype) for dims, dtype in scratch] + [pltpu.SemaphoreType.DMA((8,))],
        compiler_params=pltpu.CompilerParams(vmem_limit_bytes=SMALL_LIMIT),
        cost_estimate=pl.CostEstimate(flops=8 * flops, bytes_accessed=20 * 2**20, transcendentals=0),
        name="first_%d" % block,
    )(gy_first, gy_second, grad_projected, small_own, small_got, vecs, n1, s1, r, own_in, got_in)


def load_weight(first, one, other, target, sem):
    pl.when(first)(pltpu.make_async_copy(one, target, sem).start)
    pl.when(jnp.logical_not(first))(pltpu.make_async_copy(other, target, sem).start)
    return pltpu.make_async_copy(one, target, sem)


def wait_all(copies):
    for copy in copies:
        copy.wait()


def unpack_kernel(taps_of, groups_of, *refs):
    refs = list(refs)

    def take(number):
        taken = refs[:number]
        del refs[:number]
        return taken

    own_of, got_of = [], []
    for _ in range(2):
        own_of.append(take(2))
        got_of.append(take(2))
    w_in_t_out, w_out_out, conv_out, gin, bin_, gmid, bmid, out_bias, w_in_t, w_out, conv, buf, extra, sem = refs
    inner, width = w_out.shape
    whole = inner // LANES
    tail = inner - whole * LANES
    slots = conv.shape[0]
    section = lax.axis_index("section")
    index = lax.axis_index("dp")

    def write(taps, groups, own, got):
        rows = own[0].shape[0] - VEC_ROWS
        count = share_count(groups[0])
        share = 2 * rows // count

        def body(position, _):
            for which, (pieces, side) in enumerate(((own, section), (got, 1 - section))):
                for at, ref in enumerate(pieces):
                    owner = owner_of(position + at * (count // 2), side, groups, index)
                    start = side * (2 * rows) + owner * share
                    pltpu.make_async_copy(
                        ref.at[pl.ds(pl.multiple_of(position * share, 16), share)],
                        buf.at[pl.ds(pl.multiple_of(start, 16), share)],
                        sem.at[2 * which + at],
                    ).start()
            return 0

        lax.fori_loop(0, count // 2, body, 0)
        pieces = list(own) + list(got)
        vectors = [
            pltpu.make_async_copy(ref.at[pl.ds(rows, VEC_ROWS)], extra.at[at], sem.at[4 + at])
            for at, ref in enumerate(pieces)
        ]
        start_all(vectors)
        for at, ref in enumerate(pieces):
            pltpu.make_async_copy(ref.at[pl.ds(0, rows)], buf.at[pl.ds(0, rows)], sem.at[at]).wait()
        wait_all(vectors)
        taps_at, tails_at, w_in_at, _, _ = layout(taps, width, inner)

        def wide(target, row):
            for at in range(0, width, LANES):
                q = at // LANES
                size = min(LANES, width - at)
                target[:, at : at + size] = buf[row + q * inner : row + (q + 1) * inner, 0:size].astype(F32)

        copies = []

        def leave(source, target):
            copies.append(pltpu.make_async_copy(source, target, sem.at[8 + len(copies)]))
            copies[-1].start()

        wide(w_out, 0)
        leave(w_out, w_out_out)
        tails = buf[tails_at : tails_at + inner, :].astype(F32)
        for k in range(slots):
            if k >= taps:
                conv[k] = jnp.zeros((inner, inner), F32)
            else:
                for q in range(whole):
                    at = taps_at + inner * (whole * k + q)
                    conv[k, :, LANES * q : LANES * (q + 1)] = buf[at : at + inner, :].astype(F32)
                conv[k, :, LANES * whole :] = tails[:, tail * k : tail * (k + 1)]
            leave(conv.at[k], conv_out.at[k])
        wide(w_in_t, w_in_at)
        leave(w_in_t, w_in_t_out)
        vec = sum(extra[at].astype(F32) for at in range(4))
        row = 0
        for target, member in ((gin, 0), (bin_, 0), (gmid, 0), (gmid, 1), (bmid, 0), (bmid, 1), (out_bias, 0)):
            for at in range(0, target.shape[1], LANES):
                size = min(LANES, target.shape[1] - at)
                target[member : member + 1, at : at + size] = vec[row : row + 1, 0:size]
                row += 1
        for copy in copies:
            copy.wait()

    pl.when(section == 0)(lambda: write(taps_of[0], groups_of[0], own_of[0], got_of[0]))
    pl.when(section != 0)(lambda: write(taps_of[1], groups_of[1], own_of[1], got_of[1]))


def unpack(taps_of, groups_of, enc, dec, width, inner):
    pieces = enc[0] + enc[1] + dec[0] + dec[1]
    rows = max(4 * part[0].shape[0] for part in (enc[0], dec[0]))
    return pl.pallas_call(
        functools.partial(unpack_kernel, taps_of, groups_of),
        in_specs=[ANY] * len(pieces),
        out_specs=[ANY] * 3 + [VMEM] * 5,
        out_shape=[
            shape((inner, width), F32), shape((inner, width), F32), shape((taps_of[0], inner, inner), F32),
            shape((1, width), F32), shape((1, width), F32), shape((2, inner), F32), shape((2, inner), F32),
            shape((1, width), F32),
        ],
        scratch_shapes=[
            pltpu.VMEM((inner, width), F32), pltpu.VMEM((inner, width), F32), pltpu.VMEM((taps_of[0], inner, inner), F32),
            pltpu.VMEM((rows, LANES), BF), pltpu.VMEM((4, VEC_ROWS, LANES), BF),
            pltpu.SemaphoreType.DMA((10 + taps_of[0],)),
        ],
        compiler_params=pltpu.CompilerParams(vmem_limit_bytes=SMALL_LIMIT),
        name="unpack",
    )(*pieces)


def swap_sections(value):
    return lax.ppermute(value, "section", [(0, 1), (1, 0)])


def swap_dp(value, masks):
    count = lax.axis_size("dp")
    pairs = [(s * count + i, s * count + (i ^ masks[s])) for s in range(2) for i in range(count)]
    return lax.ppermute(value, ("section", "dp"), pairs)


def rounded_sum(terms, rows):
    total = terms[0][rows].astype(F32)
    for term in terms[1:]:
        total = total + term[rows].astype(F32)
    return total.astype(BF)


def masks_of(bits, other):
    return [other << own[0] for own in bits]


def reduce_steps(keep, got, groups, receiver, vec=None):
    count = lax.axis_size("dp")
    steps = list(zip(*groups))
    terms = [keep, got]

    def loaded(part, riding):
        return part if vec is None or not riding else jnp.concatenate([part, vec], 0)

    for number, bits in enumerate(steps):
        size = terms[0].shape[0] >> len(bits[0])
        others = range(1, 2 ** len(bits[0]))
        parts = [rounded_sum(terms, slice(other * size, (other + 1) * size)) for other in others]
        parts = [loaded(part, number > 0) for part in parts]
        gate = yield parts
        came = after([swap_dp(part, masks_of(bits, other)) for part, other in zip(parts, others)], gate)
        terms = [term[:size] for term in terms] + [part[:size] for part in came]
        if vec is not None and number > 0:
            vec = rounded_sum([vec] + [part[size:] for part in came], slice(None))
    value = rounded_sum(terms, slice(None))
    rest = list(range(sum(len(bits) for bits in groups[0]), count.bit_length() - 1))
    for bits in zip(rest, rest[1:] + rest[:1]):
        size = value.shape[0]
        whole = loaded(value, True)
        gate = yield [whole]
        whole = rounded_sum([whole, after(swap_dp(whole, [1 << bit for bit in bits]), gate)], slice(None))
        value, vec = whole[:size], (None if vec is None else whole[size:])
    pieces = [value]
    for bits in reversed(steps[1:]):
        if len(pieces) > 1:
            value = jnp.concatenate(pieces, 0)
        gate = yield [value]
        came = [swap_dp(value, masks_of(bits, other)) for other in range(1, 2 ** len(bits[0]))]
        pieces = [value] + after(came, gate)
    if vec is not None:
        pieces = pieces + [vec]
    if len(pieces) > 1:
        value = jnp.concatenate(pieces, 0)
    gate = yield [value]
    sender = 1 - receiver
    masks = masks_of(steps[0], 1)
    ways = ((receiver, masks[receiver]), (sender, 0), (sender, masks[sender]))
    came = []
    for source, mask in ways:
        pairs = [(source * count + i, receiver * count + (i ^ mask)) for i in range(count)]
        came.append(lax.ppermute(value, ("section", "dp"), pairs))
    yield [value] + after(came, gate)


class Steps:
    def __init__(self, *args):
        self.steps = reduce_steps(*args)
        self.ready = next(self.steps)

    def step(self, gate=()):
        self.ready = self.steps.send(gate)
        return self.ready

    def finish(self):
        while len(self.ready) != 4:
            self.step()
        return self.ready[:2], self.ready[2:]


def after(values, earlier):
    return lax.optimization_barrier((values, earlier))[0] if earlier else values


def shards(
    section_inputs,
    seq_lengths,
    dilations,
    gains_in,
    biases_in,
    gains_mid,
    biases_mid,
    out_bias,
    w_in,
    w_out,
    conv_taps,
):
    section = lax.axis_index("section")
    count = lax.axis_size("dp")
    groups_of = (scatter_groups(count, False), scatter_groups(count, False))
    rows = jnp.swapaxes(section_inputs[0], 1, 2)
    width = rows.shape[1]
    inner = w_out.shape[1]
    taps_of = (conv_taps.shape[1], DEC_TAPS)

    own_w = (jnp.swapaxes(w_in[0], 0, 1), w_out[0], conv_taps[0])
    send_rows = pick_rows(rows)
    got_w = tuple(swap_sections(member) for member in own_w)
    got_rows = swap_sections(after(send_rows, got_w))
    small = pack_small(gains_in, biases_in, gains_mid[0], biases_mid[0], out_bias, dilations)
    got_small = swap_sections(small)

    outs, send_y, grad_dec, keep_dec, send_dec, vec, *kept = main_call(
        taps_of, groups_of[1], seq_lengths, rows, got_rows, small, got_small, own_w, got_w
    )
    dec = Steps(keep_dec, swap_sections(send_dec), groups_of[1], 1, vec)
    gradient = after(grad_dec, dec.ready)
    grad_projected, vec, keep_enc, send_enc = encoder_call(
        taps_of[0], groups_of[0], seq_lengths, gradient, small, got_small, kept, own_w[1], got_w[1], own_w[2], got_w[2]
    )
    got_y = swap_sections(send_y)
    enc_early = swap_sections(send_enc)
    grad_projected = after(grad_projected, dec.step())
    grads_x, send_gx, vec = first_call(
        0, grad_dec, grad_dec, grad_projected, vec, kept[0:3], small, got_small, own_w[0], got_w[0]
    )

    def joined(pair, got):
        pair = lax.dynamic_update_slice_in_dim(pair, got[None], 1 - section, 0)
        return jnp.swapaxes(pair, 1, 2)[None]

    enc = Steps(keep_enc, enc_early, groups_of[0], 0, vec)
    got_gx = swap_sections(send_gx)
    outputs = joined(outs, got_y)
    input_grads = joined(grads_x, got_gx)
    named = {"d": dec, "e": enc}
    last = ()
    for name in SEQ:
        if name in named:
            if len(named[name].ready) != 4:
                last = named[name].step(last)
        else:
            last = [*last, outputs if name == "y" else input_grads]
    enc = enc.finish()
    dec = dec.finish()
    grads = unpack(taps_of, groups_of, enc, dec, width, inner)
    return (
        outputs,
        input_grads,
        grads[3],
        grads[4],
        grads[5][None],
        grads[6][None],
        grads[7],
        jnp.swapaxes(grads[0], 0, 1)[None],
        grads[1][None],
        grads[2][None],
    )


def solution(mesh):
    in_specs = (
        P("section", None, "dp", None),
        P(None, "dp"),
        P("section"),
        P("section", None),
        P("section", None),
        P("section", None, None),
        P("section", None, None),
        P("section", None),
        P("section", None, None),
        P("section", None, None),
        P("section", None, None, None),
    )
    out_specs = (
        P("section", None, "dp", None),
        P("section", None, "dp", None),
        P("section", None),
        P("section", None),
        P("section", None, None),
        P("section", None, None),
        P("section", None),
        P("section", None, None),
        P("section", None, None),
        P("section", None, None, None),
    )
    return jax.shard_map(shards, mesh=mesh, in_specs=in_specs, out_specs=out_specs, check_vma=False)
```

```python
import functools

import jax
import jax.numpy as jnp
from jax import lax
from jax.experimental import pallas as pl
from jax.experimental.pallas import tpu as pltpu
from jax.sharding import PartitionSpec as P

DEC_TAPS = 3
EPS = 1e-05
LANES = 128
CHUNK = 80
VEC_ROWS = 48
SMALL_ROWS = 8
PIECES = 5
LOOPS = (False, False, True)
BF = jnp.bfloat16
F32 = jnp.float32
VMEM_LIMIT = 62 * 2**20
SMALL_LIMIT = 62 * 2**20
SEQ = "ddeedeyxdede"
ANY = pl.BlockSpec(memory_space=pl.ANY)
SMEM = pl.BlockSpec(memory_space=pltpu.SMEM)
VMEM = pl.BlockSpec(memory_space=pltpu.VMEM)


def shape(dims, dtype):
    return jax.ShapeDtypeStruct(tuple(dims), dtype)


def nn(left, right):
    return jnp.dot(left, right, preferred_element_type=F32)


def nt(left, right):
    return lax.dot_general(left, right, (((1,), (1,)), ((), ())), preferred_element_type=F32)


def tn(left, right):
    return lax.dot_general(left, right, (((0,), (0,)), ((), ())), preferred_element_type=F32)


def lane_block(index):
    return pl.ds(pl.multiple_of(index * LANES, LANES), LANES)


def chunks(rows):
    size = CHUNK if rows % CHUNK == 0 else 16
    return [slice(at, at + size) for at in range(0, rows, size)]


def folded(values):
    return jnp.sum(values.reshape(values.shape[0] // 8, 8, values.shape[1]), 0)


def column(vector):
    return jnp.broadcast_to(vector, (LANES, vector.shape[1])).T


def norm_forward(source, half_gain, half_bias, normed, slope, hidden, devs, row, units):
    feats, tokens = source.shape
    scale = 1.0 / feats

    def stats(here):
        base = source[0:1, here].astype(F32)
        total = jnp.zeros((8, LANES), F32)
        squares = jnp.zeros((8, LANES), F32)
        for part in chunks(feats):
            moved = source[part, here].astype(F32) - base
            total = total + folded(moved)
            squares = squares + folded(moved * moved)
        average = jnp.sum(total, 0, keepdims=True) * scale
        variance = jnp.sum(squares, 0, keepdims=True) * scale - average * average
        inverse_dev = lax.rsqrt(jnp.maximum(variance, 0.0) + EPS)
        return (average + base) * inverse_dev, inverse_dev

    def finish(here, offset, inverse_dev):
        devs[row : row + 1, here] = inverse_dev
        for part in chunks(feats):
            values = source[part, here].astype(F32) * inverse_dev - offset
            gain = half_gain[part, :]
            half = values * gain + half_bias[part, :]
            tan = jnp.tanh(half)
            weight = 1.0 + tan
            out = half * weight
            normed[part, here] = values.astype(BF)
            slope[part, here] = ((weight + out * (1.0 - tan)) * gain).astype(BF)
            hidden[part, here] = out.astype(hidden.dtype)

    if units is None:

        def body(unit, carry):
            following = stats(lane_block(jnp.minimum(unit + 1, tokens // LANES - 1)))
            finish(lane_block(unit), *carry)
            return following

        lax.fori_loop(0, tokens // LANES, body, stats(lane_block(0)))
        return
    for unit in units:
        here = slice(unit * LANES, (unit + 1) * LANES)
        finish(here, *stats(here))


def norm_backward(gradient, slope, normed, devs, row, gain_sums, bias_sums, means, emit, loops):
    feats, tokens = gradient.shape
    units = tokens // LANES
    scale = 1.0 / feats
    means[...] = jnp.zeros_like(means)

    def collect(rows, size):
        gain_sum = jnp.zeros((size, LANES), F32)
        bias_sum = jnp.zeros((size, LANES), F32)
        for unit in range(units):
            here = slice(unit * LANES, (unit + 1) * LANES)
            scaled = gradient[rows, here] * slope[rows, here].astype(F32)
            weighted = scaled * normed[rows, here].astype(F32)
            gain_sum = gain_sum + weighted
            bias_sum = bias_sum + scaled
            means[0:8, here] += folded(scaled)
            means[8:16, here] += folded(weighted)
        gain_sums[rows, :] = gain_sum
        bias_sums[rows, :] = bias_sum

    def finish(here):
        inverse_dev = devs[row : row + 1, here]
        first = jnp.sum(means[0:8, here], 0, keepdims=True) * (scale * inverse_dev)
        second = jnp.sum(means[8:16, here], 0, keepdims=True) * (scale * inverse_dev)
        for part in chunks(feats):
            scaled = gradient[part, here] * slope[part, here].astype(F32)
            emit(part, here, scaled * inverse_dev - first - normed[part, here].astype(F32) * second)

    if loops:
        size = chunks(feats)[0].stop

        def one_chunk(index, _):
            collect(pl.ds(pl.multiple_of(index * size, 16), size), size)
            return 0

        def one_unit(unit, _):
            finish(lane_block(unit))
            return 0

        lax.fori_loop(0, feats // size, one_chunk, 0)
        lax.fori_loop(0, units, one_unit, 0, unroll=2)
        return
    for part in chunks(feats):
        collect(part, part.stop - part.start)
    for unit in range(units):
        finish(slice(unit * LANES, (unit + 1) * LANES))


def write_shifts(source, target, begins, offsets, units):
    feats, tokens = source.shape
    count = tokens // LANES
    block = lambda unit: slice(unit * LANES, (unit + 1) * LANES)
    for unit in units:
        joined_behind = (begins(unit) == 0).astype(F32) if unit > 0 else None
        joined_ahead = (begins(unit + 1) == 0).astype(F32) if unit < count - 1 else None
        for part in chunks(feats):
            size = part.stop - part.start
            lane = lax.broadcasted_iota(jnp.int32, (size, LANES), 1)
            zero = jnp.zeros((size, LANES), F32)
            current = source[part, block(unit)].astype(F32)
            behind = zero if unit == 0 else source[part, block(unit - 1)].astype(F32) * joined_behind
            ahead = zero if unit == count - 1 else source[part, block(unit + 1)].astype(F32) * joined_ahead
            for position, (sign, step) in enumerate(offsets):
                if sign == 0:
                    moved = current
                elif sign < 0:
                    moved = pltpu.roll(jnp.where(lane < LANES - step, current, behind), step, 1)
                else:
                    moved = pltpu.roll(jnp.where(lane >= step, current, ahead), LANES - step, 1)
                rows = slice(feats * position + part.start, feats * position + part.stop)
                target[rows, block(unit)] = moved.astype(BF)


def tap_offsets(taps, dilation, flip):
    result = []
    for position in range(taps):
        factor = (position - 2) * (-1 if flip else 1)
        result.append(((factor > 0) - (factor < 0), abs(factor) * dilation))
    return result


def layout(taps, width, inner):
    wide = width // LANES * inner
    taps_at = wide
    w_in_at = taps_at + taps * (inner // LANES) * inner
    tails_at = w_in_at + wide
    (_, _), (last, _) = tail_places(taps, width, inner)
    return taps_at, w_in_at, tails_at, tails_at + (last + 1) * inner


def tail_places(taps, width, inner):
    size = width % LANES
    places = []
    group, lane = 0, taps * (inner % LANES)
    for _ in range(2):
        if lane + size > LANES:
            group, lane = group + 1, 0
        places.append((group, lane))
        lane += size
    return places


def scatter_groups(count, full):
    total = count.bit_length() - 1
    rest = [list(range(2, min(4, total)))] if full and total > 2 else []
    return [[[bit] for bit in bits if bit < total] + rest for bits in ((0, 1), (1, 0))]


def share_count(groups):
    return 2 ** sum(len(bits) for bits in groups)


def padded_rows(rows, groups):
    unit = 2 * 16 * share_count(groups[0])
    return pl.cdiv(rows, unit) * unit


def put_wide(buf, row, matrix, tails_at, place):
    rows, cols = matrix.shape
    whole = cols // LANES
    for q in range(whole):
        buf[row + q * rows : row + (q + 1) * rows, :] = matrix[:, LANES * q : LANES * (q + 1)].astype(BF)
    if cols > whole * LANES:
        group, lane = place
        at = tails_at + group * rows
        buf[at : at + rows, lane : lane + cols - whole * LANES] = matrix[:, LANES * whole :].astype(BF)


def put_taps(buf, taps, width, shifted, grad_mixed):
    inner = grad_mixed.shape[0]
    taps_at, _, tails_at, _ = layout(taps, width, inner)
    whole = inner // LANES
    tail = inner - whole * LANES
    for k in range(taps):
        grad = nt(shifted[inner * k : inner * (k + 1), :], grad_mixed[...])
        for q in range(whole):
            at = taps_at + inner * (whole * k + q)
            buf[at : at + inner, :] = grad[:, LANES * q : LANES * (q + 1)].astype(BF)
        buf[tails_at : tails_at + inner, tail * k : tail * (k + 1)] = grad[:, LANES * whole :].astype(BF)


def row_sums(acc):
    return jnp.sum(acc.T, 0, keepdims=True)


def put_vectors(buf, at, vec, sums):
    vec[...] = jnp.zeros_like(vec)
    row = 0
    for total in sums:
        for lane in range(0, total.shape[1], LANES):
            part = total[:, lane : lane + LANES]
            vec[row : row + 1, 0 : part.shape[1]] = part
            row += 1
    buf[at : at + VEC_ROWS, :] = vec[...].astype(BF)


def relative_index(position, groups):
    result = 0
    for bits in reversed(groups):
        size = 2 ** len(bits)
        result = result + (position & (size - 1)) * 2 ** bits[0]
        position = position >> len(bits)
    return result


def owner_of(position, side, groups, index):
    both = [relative_index(position, order) for order in groups]
    mask = sum(2**bit for bits in groups[0] for bit in bits)
    return jnp.where(side == 0, both[0], both[1]) ^ (index & mask)


def position_of(owner, side, groups, index):
    distance = owner ^ index
    position = 0
    for bits in groups[side]:
        position = position * 2 ** len(bits) + ((distance >> bits[0]) & (2 ** len(bits) - 1))
    return position


class RowsOut:
    def __init__(self, buf, keep, send, section, index, groups, sems):
        self.buf, self.keep, self.send, self.sems = buf, keep, send, sems
        self.section, self.index, self.groups = section, index, groups
        self.count = share_count(groups[0])
        self.share = keep.shape[0] // self.count
        self.sizes = []

    def start(self, first, last):
        for number in range(2 * self.count):
            low, high = max(first, number * self.share), min(last, (number + 1) * self.share)
            if low >= high:
                continue
            side, owner = divmod(number, self.count)
            place = position_of(owner, side, self.groups, self.index) * self.share + (low - number * self.share)
            target = pl.ds(pl.multiple_of(place, 16), high - low)
            source = self.buf.at[low:high]
            sem = self.sems.at[len(self.sizes)]
            pl.when(self.section == side)(pltpu.make_async_copy(source, self.keep.at[target], sem).start)
            pl.when(self.section != side)(pltpu.make_async_copy(source, self.send.at[target], sem).start)
            self.sizes.append(high - low)

    def wait(self):
        for number, size in enumerate(self.sizes):
            source, target = self.buf.at[0:size], self.keep.at[0:size]
            pltpu.make_async_copy(source, target, self.sems.at[number]).wait()


def forward_block(taps, begins, dilation, x, y, weights, turned, cols, kept, hmid, prod, ready):
    w_in_t, w_out, conv = weights
    w_out_t, conv_t = turned
    g1, b1, g2, b2, g3, b3, ob = cols
    n1, s1, r, n2, s2, n3, s3, hin, shifted, hout = kept
    inner, tokens = hmid.shape
    units = tokens // LANES
    narrow = prod.at[0:inner]
    parts = [range(at, min(at + units // 2, units)) for at in range(0, units, units // 2)]
    columns = [slice(part.start * LANES, part.stop * LANES) for part in parts]
    offsets = tap_offsets(taps, dilation, False)

    def mix(part):
        narrow[:, columns[part]] = nn(conv_t[:, 0 : taps * inner], shifted[:, columns[part]])

    def leave(part):
        here = columns[part]
        bias = jnp.concatenate([ob[...]] * len(parts[part]), 1)
        y[:, here] = (x[:, here].astype(F32) + nn(w_out_t[...], hout[:, here]) + bias).astype(BF)

    norm_forward(x, g1, b1, n1, s1, hin, r, 0, None)
    ready(0)
    narrow[...] = nn(w_in_t[...], hin[...])
    ready(1)
    norm_forward(narrow, g2, b2, n2, s2, hmid, r, 1, parts[0])
    for k in range(taps):
        conv_t[:, inner * k : inner * (k + 1)] = conv[k].T
    w_out_t[...] = w_out[...].T
    norm_forward(narrow, g2, b2, n2, s2, hmid, r, 1, parts[1])
    write_shifts(hmid, shifted, begins, offsets, parts[0])
    mix(0)
    write_shifts(hmid, shifted, begins, offsets, parts[1])
    mix(1)
    norm_forward(narrow, g3, b3, n3, s3, hout, r, 2, parts[0])
    leave(0)
    norm_forward(narrow, g3, b3, n3, s3, hout, r, 2, parts[1])
    leave(1)


def fill_columns(small, cols):
    g1, b1, g2, b2, g3, b3, ob = cols
    width, inner = g1.shape[0], g2.shape[0]
    for target, row, scale in ((g1, 0, 0.5), (b1, 1, 0.5), (ob, 2, 1.0)):
        target[...] = column(small[row : row + 1, 0:width] * scale)
    for target, row in ((g2, 3), (b2, 4), (g3, 5), (b3, 6)):
        target[...] = column(small[row : row + 1, 0:inner] * 0.5)


def back_third(gy, w_out, kept, prod, means, grad_mixed, gain_sums, bias_sums, beside):
    n3, s3, r = kept
    inner = w_out.shape[0]
    narrow = prod.at[0:inner]
    narrow[...] = nn(w_out[...], gy[...])
    beside()

    def emit(part, here, value):
        grad_mixed[part, here] = value.astype(BF)

    norm_backward(narrow, s3, n3, r, 2, gain_sums, bias_sums, means, emit, LOOPS[0])


def back_second(
    taps, begins, dilation, conv_w, kept, prod, means, grad_mixed, moved, grad_projected, gain_sums, bias_sums, ready,
    weights=None,
):
    n2, s2, r = kept
    inner = grad_mixed.shape[0]
    narrow = prod.at[0:inner]
    write_shifts(grad_mixed, moved, begins, tap_offsets(taps, dilation, True), range(grad_mixed.shape[1] // LANES))
    if weights is not None:
        weights()
    narrow[...] = nn(conv_w[...], moved[...])
    ready()

    def emit(part, here, value):
        grad_projected[part, here] = value.astype(BF)

    norm_backward(narrow, s2, n2, r, 1, gain_sums, bias_sums, means, emit, LOOPS[1])


def back_first(gy, w_in_t, kept, prod, means, grad_projected, gx, gain_sums, bias_sums, ready):
    n1, s1, r = kept
    prod[...] = tn(w_in_t[...], grad_projected[...])
    ready()

    def emit(part, here, value):
        gx[part, here] = (gy[part, here].astype(F32) + value).astype(BF)

    norm_backward(prod, s1, n1, r, 0, gain_sums, bias_sums, means, emit, LOOPS[2])


def put_w_out(buf, taps, hout_ones, gy):
    grad = nt(hout_ones[...], gy[...])
    inner, width = hout_ones.shape[0] - 16, gy.shape[0]
    _, _, tails_at, end = layout(taps, width, inner)
    buf[tails_at:end, :] = jnp.zeros((end - tails_at, LANES), BF)
    put_wide(buf, 0, grad[0:inner], tails_at, tail_places(taps, width, inner)[0])
    return grad[inner : inner + 1]


def put_w_in(buf, taps, grad_projected, hin):
    inner, width = grad_projected.shape[0], hin.shape[0]
    _, w_in_at, tails_at, _ = layout(taps, width, inner)
    put_wide(buf, w_in_at, nt(grad_projected[...], hin[...]), tails_at, tail_places(taps, width, inner)[1])


def gain_and_bias(gain, sums):
    return [row_sums(acc[...]) / gain for acc in sums]


def put_rows(target, rows):
    target[...] = jnp.zeros_like(target)
    for at, row in enumerate(rows):
        target[at : at + 1, 0 : row.shape[1]] = row


def gains_of(small, width, inner):
    return small[0:1, 0:width], small[3:4, 0:inner], small[5:6, 0:inner]


def pick_small(leading, own, got):
    flag = leading.astype(F32)
    return own[...] * flag + got[...] * (1.0 - flag)


def start_all(copies):
    for copy in copies:
        copy.start()


def pick_rows_kernel(rows, send, hold, sem):
    section = lax.axis_index("section")
    size = send.shape[0] // PIECES
    parts = [slice(size * i, size * (i + 1)) for i in range(PIECES)]
    arrive = [
        pltpu.make_async_copy(rows.at[1 - section, part], hold.at[part], sem.at[i]) for i, part in enumerate(parts)
    ]
    leave = [pltpu.make_async_copy(hold.at[part], send.at[part], sem.at[PIECES + i]) for i, part in enumerate(parts)]
    start_all(arrive)
    for come, go in zip(arrive, leave):
        come.wait()
        go.start()
    for go in leave:
        go.wait()


def pick_rows(rows):
    return pl.pallas_call(
        pick_rows_kernel,
        in_specs=[ANY],
        out_specs=ANY,
        out_shape=shape(rows.shape[1:], BF),
        scratch_shapes=[pltpu.VMEM(rows.shape[1:], BF), pltpu.SemaphoreType.DMA((2 * PIECES,))],
        compiler_params=pltpu.CompilerParams(vmem_limit_bytes=VMEM_LIMIT),
        cost_estimate=pl.CostEstimate(flops=0, bytes_accessed=8 * 2**20, transcendentals=0),
        name="pick_rows",
    )(rows)


def pack_small_kernel(gin, bin_, gmid, bmid, out_bias, dilation, small):
    width, inner = gin.shape[1], gmid.shape[1]
    small[...] = jnp.zeros_like(small)
    for row, ref in ((0, gin), (1, bin_), (2, out_bias)):
        small[row : row + 1, 0:width] = ref[...]
    for row, ref, which in ((3, gmid, 0), (4, bmid, 0), (5, gmid, 1), (6, bmid, 1)):
        small[row : row + 1, 0:inner] = ref[which : which + 1, :]
    small[7:8, :] = jnp.full((1, small.shape[1]), dilation[0].astype(F32), F32)


def pack_small(gin, bin_, gmid, bmid, out_bias, dilation):
    return pl.pallas_call(
        pack_small_kernel,
        in_specs=[VMEM] * 5 + [SMEM],
        out_specs=VMEM,
        out_shape=shape((SMALL_ROWS, gin.shape[1]), F32),
        compiler_params=pltpu.CompilerParams(vmem_limit_bytes=VMEM_LIMIT),
        name="pack_small",
    )(gin, bin_, gmid, bmid, out_bias, dilation)


def kept_shapes(taps, width, inner, tokens):
    wide, narrow = (width, tokens), (inner, tokens)
    return [
        (wide, BF), (wide, BF), ((8, tokens), F32), (narrow, BF), (narrow, BF), (narrow, BF), (narrow, BF),
        (wide, BF), ((inner * taps, tokens), BF), (narrow, BF),
    ]


def column_shapes(width, inner):
    return [(width, LANES)] * 2 + [(inner, LANES)] * 4 + [(width, LANES)]


def main_kernel(taps_of, groups, *refs):
    refs = list(refs)

    def take(number):
        taken = refs[:number]
        del refs[:number]
        return taken

    seq, rows, got, small_own, small_got = take(5)
    own_w, got_w = take(3), take(3)
    outs, send_y, grad_out, keep_buf, send_buf, vec_out = take(6)
    kept_out = take(10)
    x, cot = take(2)
    enc_w, dec_w = take(3), take(3)
    small = take(2)
    enc_kept, dec_kept = take(10), take(10)
    cols = take(7)
    hmid, prod, means, y_enc, gx, w_out_t, conv_t, conv_w, grad_mixed, grad_projected, moved, buf = take(12)
    ag1, ab1, ag2, ab2, ag3, ab3, vec, sem, row_sems = take(9)

    section = lax.axis_index("section")
    index = lax.axis_index("dp")
    leading = section == 0
    width, tokens = x.shape
    inner = hmid.shape[0]
    small[0][...] = pick_small(leading, small_own, small_got)
    small[1][...] = pick_small(leading, small_got, small_own)
    dilation = [jnp.max(member[7:8, 0:LANES]).astype(jnp.int32) for member in small]

    def begins(unit):
        return seq[section, unit]

    loads = [(x, rows.at[0], got), (enc_w[0], own_w[0], got_w[0]), (enc_w[2], own_w[2], got_w[2])]
    loads += [(enc_w[1], own_w[1], got_w[1]), (dec_w[0], got_w[0], own_w[0]), (dec_w[1], got_w[1], own_w[1])]
    loads += [(dec_w[2], got_w[2].at[0 : taps_of[1]], own_w[2].at[0 : taps_of[1]]), (cot, got, rows.at[1])]

    def load(at):
        target, first, second = loads[at]
        pl.when(leading)(pltpu.make_async_copy(first, target, sem.at[at]).start)
        pl.when(jnp.logical_not(leading))(pltpu.make_async_copy(second, target, sem.at[at]).start)

    for at in range(4):
        load(at)

    def ready(at):
        pltpu.make_async_copy(loads[at][1], loads[at][0], sem.at[at]).wait()

    fill_columns(small[0], cols)
    hout_ones = dec_kept[9]
    dec_kept[9] = hout_ones.at[0:inner]
    hout_ones[inner:, :] = jnp.ones((16, tokens), BF)
    ready(0)

    def enc_ready(which):
        for at in ((1,), (2, 3))[which]:
            ready(at)
        if which:
            for at in range(4, 8):
                load(at)

    turned = (w_out_t, conv_t)
    forward_block(taps_of[0], begins, dilation[0], x, y_enc, enc_w, turned, cols, enc_kept, hmid, prod, enc_ready)
    saves = [pltpu.make_async_copy(a, b, sem.at[8 + i]) for i, (a, b) in enumerate(zip(enc_kept, kept_out))]
    start_all(saves)

    fill_columns(small[1], cols)
    for at in range(4, 8):
        ready(at)
    for k in range(taps_of[1]):
        conv_w[:, inner * k : inner * (k + 1)] = dec_w[2][k]
    y_dec = x
    forward_block(
        taps_of[1], begins, dilation[1], y_enc, y_dec, dec_w, turned, cols, dec_kept, hmid, prod, lambda which: None
    )
    pl.when(leading)(pltpu.make_async_copy(y_enc, outs.at[0], sem.at[18]).start)
    pl.when(leading)(pltpu.make_async_copy(y_dec, send_y, sem.at[19]).start)
    pl.when(jnp.logical_not(leading))(pltpu.make_async_copy(y_dec, outs.at[1], sem.at[18]).start)
    pl.when(jnp.logical_not(leading))(pltpu.make_async_copy(y_enc, send_y, sem.at[19]).start)

    n1, s1, r, n2, s2, n3, s3, hin, shifted, hout = dec_kept
    rows_out = RowsOut(buf, keep_buf, send_buf, section, index, groups, row_sems)
    w_in_at, _, end = layout(taps_of[1], width, inner)[1:]

    bias = []

    def third_beside():
        bias.append(put_w_out(buf, taps_of[1], hout_ones, cot))

    def first_beside():
        put_w_in(buf, taps_of[1], grad_projected, hin)

    back_third(cot, dec_w[1], (n3, s3, r), prod, means, grad_mixed, ag3, ab3, third_beside)
    put_taps(buf, taps_of[1], width, shifted, grad_mixed)
    back_second(
        taps_of[1], begins, dilation[1], conv_w, (n2, s2, r), prod, means, grad_mixed, moved, grad_projected, ag2, ab2,
        lambda: None,
    )
    rows_out.start(0, w_in_at)
    back_first(cot, dec_w[0], (n1, s1, r), prod, means, grad_projected, gx, ag1, ab1, first_beside)
    rows_out.start(w_in_at, end)
    last = pltpu.make_async_copy(gx, grad_out, sem.at[20])
    last.start()
    g1, g2, g3 = gains_of(small[1], width, inner)
    first, second, third = gain_and_bias(g1, (ag1, ab1)), gain_and_bias(g2, (ag2, ab2)), gain_and_bias(g3, (ag3, ab3))
    put_vectors(vec_out, 0, vec, first + [second[0], third[0], second[1], third[1]] + bias)
    rows_out.wait()
    wait_all(saves + [last])
    pltpu.make_async_copy(y_enc, outs.at[0], sem.at[18]).wait()
    pltpu.make_async_copy(y_dec, send_y, sem.at[19]).wait()


def main_call(taps_of, groups, seq, rows, got, small_own, small_got, own_w, got_w):
    _, width, tokens = rows.shape
    inner = own_w[1].shape[0]
    half = padded_rows(layout(taps_of[1], width, inner)[3], groups) // 2
    wide, narrow = (width, tokens), (inner, tokens)
    weight_shapes = [(inner, width), (inner, width)]
    scratch = [(wide, BF)] * 2
    for taps in taps_of:
        scratch += [(dims, BF) for dims in weight_shapes + [(taps, inner, inner)]]
    scratch += [((SMALL_ROWS, width), F32)] * 2
    scratch += kept_shapes(taps_of[0], width, inner, tokens) + kept_shapes(taps_of[1], width, inner, tokens)[:-1]
    scratch += [((inner + 16, tokens), BF)]
    scratch += [(dims, F32) for dims in column_shapes(width, inner)]
    scratch += [
        (narrow, BF), (wide, F32), ((16, tokens), F32), (wide, BF), (wide, BF), ((width, inner), BF),
        ((inner, inner * taps_of[0]), BF), ((inner, inner * taps_of[1]), BF),
        (narrow, BF), (narrow, BF), ((inner * taps_of[1], tokens), BF), ((2 * half, LANES), BF),
    ]
    scratch += [((width, LANES), F32)] * 2 + [((inner, LANES), F32)] * 4 + [((VEC_ROWS, LANES), F32)]
    block = shape((half, LANES), BF)
    outs = [shape((2,) + wide, BF), shape(wide, BF), shape(wide, BF), block, block, shape((VEC_ROWS, LANES), BF)]
    outs += [shape(dims, dtype) for dims, dtype in kept_shapes(taps_of[0], width, inner, tokens)]
    flops = 2 * tokens * inner * (2 * width + taps_of[0] * inner + 3 * (2 * width + taps_of[1] * inner))
    return pl.pallas_call(
        functools.partial(main_kernel, taps_of, groups),
        in_specs=[SMEM, ANY, ANY, VMEM, VMEM] + [ANY] * 6,
        out_specs=[ANY] * 5 + [VMEM] + [ANY] * 10,
        out_shape=outs,
        scratch_shapes=[pltpu.VMEM(dims, dtype) for dims, dtype in scratch]
        + [pltpu.SemaphoreType.DMA((24,)), pltpu.SemaphoreType.DMA((8 * share_count(groups[0]),))],
        compiler_params=pltpu.CompilerParams(vmem_limit_bytes=VMEM_LIMIT),
        cost_estimate=pl.CostEstimate(flops=4 * flops, bytes_accessed=60 * 2**20, transcendentals=0),
        name="main_blocks",
    )(seq, rows, got, small_own, small_got, *own_w, *got_w)


def load_weight(leading, own, got, target, sem):
    pl.when(leading)(pltpu.make_async_copy(own, target, sem).start)
    pl.when(jnp.logical_not(leading))(pltpu.make_async_copy(got, target, sem).start)
    return pltpu.make_async_copy(own, target, sem)


def wait_all(copies):
    for copy in copies:
        copy.wait()


def encoder_kernel(
    taps, groups,
    seq, gy_in, small_own, small_got, n3_in, s3_in, r_in, shifted_in, hout_in, n2_in, s2_in, hin_in, own_out, got_out,
    own_conv, got_conv,
    grad_projected_out, vec_out, keep_buf, send_buf,
    gy, n3, s3, r, shifted, hout_ones, n2, s2, hin, w_out, conv, conv_w, prod, means, grad_mixed, moved, grad_projected,
    buf, ag3, ab3, ag2, ab2, sem, row_sems,
):
    section = lax.axis_index("section")
    leading = section == 0
    width, tokens = gy.shape
    inner = w_out.shape[0]
    w_in_at, _, end = layout(taps, width, inner)[1:]
    hout = hout_ones.at[0:inner]
    pairs = (
        (gy_in, gy), (s3_in, s3), (n3_in, n3), (r_in, r), (hout_in, hout), (shifted_in, shifted), (n2_in, n2), (s2_in, s2),
        (hin_in, hin),
    )
    loads = [pltpu.make_async_copy(a, b, sem.at[2 + i]) for i, (a, b) in enumerate(pairs)]
    loads[0].start()
    weight = load_weight(leading, own_out, got_out, w_out, sem.at[0])
    start_all(loads[1:5])
    conv_weight = load_weight(leading, own_conv, got_conv, conv, sem.at[1])
    start_all(loads[5:])
    hout_ones[inner:, :] = jnp.ones((16, tokens), BF)
    small = pick_small(leading, small_own, small_got)
    dilation = jnp.max(small[7:8, 0:LANES]).astype(jnp.int32)

    def begins(unit):
        return seq[section, unit]

    def weights():
        conv_weight.wait()
        for k in range(taps):
            conv_w[:, inner * k : inner * (k + 1)] = conv[k]

    wait_all([weight, loads[0]])
    bias = []

    def third_beside():
        wait_all(loads[1:5])
        bias.append(put_w_out(buf, taps, hout_ones, gy))

    back_third(gy, w_out, (n3, s3, r), prod, means, grad_mixed, ag3, ab3, third_beside)
    wait_all([loads[5]])
    put_taps(buf, taps, width, shifted, grad_mixed)
    back_second(
        taps, begins, dilation, conv_w, (n2, s2, r), prod, means, grad_mixed, moved, grad_projected, ag2, ab2,
        lambda: wait_all(loads[6:8]), weights,
    )
    out = pltpu.make_async_copy(grad_projected, grad_projected_out, sem.at[11])
    out.start()
    rows_out = RowsOut(buf, keep_buf, send_buf, section, lax.axis_index("dp"), groups, row_sems)
    rows_out.start(0, w_in_at)
    loads[8].wait()
    put_w_in(buf, taps, grad_projected, hin)
    rows_out.start(w_in_at, end)
    _, g2, g3 = gains_of(small, width, inner)
    second, third = gain_and_bias(g2, (ag2, ab2)), gain_and_bias(g3, (ag3, ab3))
    put_rows(vec_out, [second[0], third[0], second[1], third[1]] + bias)
    out.wait()
    rows_out.wait()


def encoder_call(taps, groups, seq, gy, small_own, small_got, kept, own_out, got_out, own_conv, got_conv):
    width, tokens = gy.shape
    inner = own_out.shape[0]
    n1, s1, r, n2, s2, n3, s3, hin, shifted, hout = kept
    rows = layout(taps, width, inner)[3]
    half = padded_rows(rows, groups) // 2
    wide, narrow = (width, tokens), (inner, tokens)
    scratch = [
        (wide, BF), (narrow, BF), (narrow, BF), ((8, tokens), F32), ((inner * taps, tokens), BF),
        ((inner + 16, tokens), BF), (narrow, BF), (narrow, BF), (wide, BF), ((inner, width), BF),
        ((taps, inner, inner), BF), ((inner, inner * taps), BF), (narrow, F32), ((16, tokens), F32), (narrow, BF),
        ((inner * taps, tokens), BF), (narrow, BF), ((rows, LANES), BF),
    ]
    scratch += [((inner, LANES), F32)] * 4
    flops = 2 * tokens * inner * (3 * width + 2 * taps * inner)
    block = shape((half, LANES), BF)
    return pl.pallas_call(
        functools.partial(encoder_kernel, taps, groups),
        in_specs=[SMEM, ANY, VMEM, VMEM] + [ANY] * 12,
        out_specs=[ANY, VMEM, ANY, ANY],
        out_shape=[shape(narrow, BF), shape((SMALL_ROWS, width), F32), block, block],
        scratch_shapes=[pltpu.VMEM(dims, dtype) for dims, dtype in scratch]
        + [pltpu.SemaphoreType.DMA((12,)), pltpu.SemaphoreType.DMA((8 * share_count(groups[0]),))],
        compiler_params=pltpu.CompilerParams(vmem_limit_bytes=SMALL_LIMIT),
        cost_estimate=pl.CostEstimate(flops=4 * flops, bytes_accessed=20 * 2**20, transcendentals=0),
        name="encoder_back",
    )(
        seq, gy, small_own, small_got, n3, s3, r, shifted, hout, n2, s2, hin, own_out, got_out, own_conv, got_conv
    )


def first_kernel(
    block, gy_first, gy_second, grad_projected_in, small_own, small_got, vecs, n1_in, s1_in, r_in, own_in, got_in,
    *refs,
):
    outs_of, refs = refs[: 2 - block], refs[2 - block :]
    vec_out, gy, grad_projected, n1, s1, r, w_in_t, prod, means, gx, ag1, ab1, vec, sem = refs
    leading = lax.axis_index("section") == 0
    mine = leading if block == 0 else jnp.logical_not(leading)
    width, inner = gy.shape[0], grad_projected.shape[0]
    pairs = ((grad_projected_in, grad_projected), (s1_in, s1), (n1_in, n1), (r_in, r))
    loads = [pltpu.make_async_copy(a, b, sem.at[2 + i]) for i, (a, b) in enumerate(pairs)]
    loads[0].start()
    weight = load_weight(mine, own_in, got_in, w_in_t, sem.at[0])
    start_all(loads[1:])
    loads.append(load_weight(leading, gy_first, gy_second, gy, sem.at[1]))
    small = pick_small(mine, small_own, small_got)
    wait_all([loads[0], weight])

    def save(value, at_home, away, sem):
        pl.when(leading)(pltpu.make_async_copy(value, at_home, sem).start)
        pl.when(jnp.logical_not(leading))(pltpu.make_async_copy(value, away, sem).start)
        return pltpu.make_async_copy(value, away, sem)

    waits = []

    def ready():
        wait_all(loads[1:])
        if block == 0:
            outs, send = outs_of
            waits.append(save(gy, send, outs.at[1], sem.at[6]))

    back_first(gy, w_in_t, (n1, s1, r), prod, means, grad_projected, gx, ag1, ab1, ready)
    if block == 0:
        outs, send = outs_of
        waits.append(save(gx, outs.at[0], send, sem.at[7]))
    else:
        waits.append(pltpu.make_async_copy(gx, outs_of[0], sem.at[7]))
        waits[-1].start()
    sums = gain_and_bias(gains_of(small, width, inner)[0], (ag1, ab1))
    sums += [vecs[row : row + 1, 0:size] for row, size in enumerate((inner, inner, inner, inner, width))]
    put_vectors(vec_out, 0, vec, sums)
    wait_all(waits)


def first_call(block, gy_first, gy_second, grad_projected, vecs, kept, small_own, small_got, own_in, got_in):
    n1, s1, r = kept
    width, tokens = n1.shape
    inner = grad_projected.shape[0]
    wide, narrow = (width, tokens), (inner, tokens)
    scratch = [
        (wide, BF), (narrow, BF), (wide, BF), (wide, BF), ((8, tokens), F32), ((inner, width), BF), (wide, F32),
        ((16, tokens), F32), (wide, BF), ((width, LANES), F32), ((width, LANES), F32), ((VEC_ROWS, LANES), F32),
    ]
    outs = [shape((2,) + wide, BF), shape(wide, BF)] if block == 0 else [shape(wide, BF)]
    flops = 2 * tokens * inner * width
    return pl.pallas_call(
        functools.partial(first_kernel, block),
        in_specs=[ANY] * 3 + [VMEM] * 3 + [ANY] * 5,
        out_specs=[ANY] * len(outs) + [VMEM],
        out_shape=outs + [shape((VEC_ROWS, LANES), BF)],
        scratch_shapes=[pltpu.VMEM(dims, dtype) for dims, dtype in scratch] + [pltpu.SemaphoreType.DMA((8,))],
        compiler_params=pltpu.CompilerParams(vmem_limit_bytes=SMALL_LIMIT),
        cost_estimate=pl.CostEstimate(flops=8 * flops, bytes_accessed=20 * 2**20, transcendentals=0),
        name="first_%d" % block,
    )(gy_first, gy_second, grad_projected, small_own, small_got, vecs, n1, s1, r, own_in, got_in)


def load_weight(first, one, other, target, sem):
    pl.when(first)(pltpu.make_async_copy(one, target, sem).start)
    pl.when(jnp.logical_not(first))(pltpu.make_async_copy(other, target, sem).start)
    return pltpu.make_async_copy(one, target, sem)


def wait_all(copies):
    for copy in copies:
        copy.wait()


def unpack_kernel(taps_of, groups_of, *refs):
    refs = list(refs)

    def take(number):
        taken = refs[:number]
        del refs[:number]
        return taken

    own_of, got_of = [], []
    for _ in range(2):
        own_of.append(take(2))
        got_of.append(take(2))
    w_in_t_out, w_out_out, conv_out, gin, bin_, gmid, bmid, out_bias, w_in_t, w_out, conv, buf, extra, sem = refs
    inner, width = w_out.shape
    whole = inner // LANES
    tail = inner - whole * LANES
    slots = conv.shape[0]
    section = lax.axis_index("section")
    index = lax.axis_index("dp")

    def write(taps, groups, own, got):
        rows = own[0].shape[0] - VEC_ROWS
        count = share_count(groups[0])
        share = 2 * rows // count

        def body(position, _):
            for which, (pieces, side) in enumerate(((own, section), (got, 1 - section))):
                for at, ref in enumerate(pieces):
                    owner = owner_of(position + at * (count // 2), side, groups, index)
                    start = side * (2 * rows) + owner * share
                    pltpu.make_async_copy(
                        ref.at[pl.ds(pl.multiple_of(position * share, 16), share)],
                        buf.at[pl.ds(pl.multiple_of(start, 16), share)],
                        sem.at[2 * which + at],
                    ).start()
            return 0

        lax.fori_loop(0, count // 2, body, 0)
        pieces = list(own) + list(got)
        vectors = [
            pltpu.make_async_copy(ref.at[pl.ds(rows, VEC_ROWS)], extra.at[at], sem.at[4 + at])
            for at, ref in enumerate(pieces)
        ]
        start_all(vectors)
        for at, ref in enumerate(pieces):
            pltpu.make_async_copy(ref.at[pl.ds(0, rows)], buf.at[pl.ds(0, rows)], sem.at[at]).wait()
        wait_all(vectors)
        taps_at, w_in_at, tails_at, _ = layout(taps, width, inner)
        places = tail_places(taps, width, inner)

        def wide(target, row, place):
            groups = width // LANES
            for q in range(groups):
                at = row + q * inner
                target[:, LANES * q : LANES * (q + 1)] = buf[at : at + inner, :].astype(F32)
            if width > groups * LANES:
                group, lane = place
                at = tails_at + group * inner
                rest = buf[at : at + inner, :].astype(F32)
                target[:, LANES * groups :] = rest[:, lane : lane + width - groups * LANES]

        copies = []

        def leave(source, target):
            copies.append(pltpu.make_async_copy(source, target, sem.at[8 + len(copies)]))
            copies[-1].start()

        wide(w_out, 0, places[0])
        leave(w_out, w_out_out)
        tails = buf[tails_at : tails_at + inner, :].astype(F32)
        for k in range(slots):
            if k >= taps:
                conv[k] = jnp.zeros((inner, inner), F32)
            else:
                for q in range(whole):
                    at = taps_at + inner * (whole * k + q)
                    conv[k, :, LANES * q : LANES * (q + 1)] = buf[at : at + inner, :].astype(F32)
                conv[k, :, LANES * whole :] = tails[:, tail * k : tail * (k + 1)]
            leave(conv.at[k], conv_out.at[k])
        wide(w_in_t, w_in_at, places[1])
        leave(w_in_t, w_in_t_out)
        vec = sum(extra[at].astype(F32) for at in range(4))
        row = 0
        for target, member in ((gin, 0), (bin_, 0), (gmid, 0), (gmid, 1), (bmid, 0), (bmid, 1), (out_bias, 0)):
            for at in range(0, target.shape[1], LANES):
                size = min(LANES, target.shape[1] - at)
                target[member : member + 1, at : at + size] = vec[row : row + 1, 0:size]
                row += 1
        for copy in copies:
            copy.wait()

    pl.when(section == 0)(lambda: write(taps_of[0], groups_of[0], own_of[0], got_of[0]))
    pl.when(section != 0)(lambda: write(taps_of[1], groups_of[1], own_of[1], got_of[1]))


def unpack(taps_of, groups_of, enc, dec, width, inner):
    pieces = enc[0] + enc[1] + dec[0] + dec[1]
    rows = max(4 * part[0].shape[0] for part in (enc[0], dec[0]))
    return pl.pallas_call(
        functools.partial(unpack_kernel, taps_of, groups_of),
        in_specs=[ANY] * len(pieces),
        out_specs=[ANY] * 3 + [VMEM] * 5,
        out_shape=[
            shape((inner, width), F32), shape((inner, width), F32), shape((taps_of[0], inner, inner), F32),
            shape((1, width), F32), shape((1, width), F32), shape((2, inner), F32), shape((2, inner), F32),
            shape((1, width), F32),
        ],
        scratch_shapes=[
            pltpu.VMEM((inner, width), F32), pltpu.VMEM((inner, width), F32), pltpu.VMEM((taps_of[0], inner, inner), F32),
            pltpu.VMEM((rows, LANES), BF), pltpu.VMEM((4, VEC_ROWS, LANES), BF),
            pltpu.SemaphoreType.DMA((10 + taps_of[0],)),
        ],
        compiler_params=pltpu.CompilerParams(vmem_limit_bytes=SMALL_LIMIT),
        name="unpack",
    )(*pieces)


def swap_sections(value):
    return lax.ppermute(value, "section", [(0, 1), (1, 0)])


def swap_dp(value, masks):
    count = lax.axis_size("dp")
    pairs = [(s * count + i, s * count + (i ^ masks[s])) for s in range(2) for i in range(count)]
    return lax.ppermute(value, ("section", "dp"), pairs)


def rounded_sum(terms, rows):
    total = terms[0][rows].astype(F32)
    for term in terms[1:]:
        total = total + term[rows].astype(F32)
    return total.astype(BF)


def masks_of(bits, other):
    return [other << own[0] for own in bits]


def reduce_steps(keep, got, groups, receiver, vec=None):
    count = lax.axis_size("dp")
    steps = list(zip(*groups))
    terms = [keep, got]

    def loaded(part, riding):
        return part if vec is None or not riding else jnp.concatenate([part, vec], 0)

    for number, bits in enumerate(steps):
        size = terms[0].shape[0] >> len(bits[0])
        others = range(1, 2 ** len(bits[0]))
        parts = [rounded_sum(terms, slice(other * size, (other + 1) * size)) for other in others]
        parts = [loaded(part, number > 0) for part in parts]
        gate = yield parts
        came = after([swap_dp(part, masks_of(bits, other)) for part, other in zip(parts, others)], gate)
        terms = [term[:size] for term in terms] + [part[:size] for part in came]
        if vec is not None and number > 0:
            vec = rounded_sum([vec] + [part[size:] for part in came], slice(None))
    value = rounded_sum(terms, slice(None))
    rest = list(range(sum(len(bits) for bits in groups[0]), count.bit_length() - 1))
    for bits in zip(rest, rest[1:] + rest[:1]):
        size = value.shape[0]
        whole = loaded(value, True)
        gate = yield [whole]
        whole = rounded_sum([whole, after(swap_dp(whole, [1 << bit for bit in bits]), gate)], slice(None))
        value, vec = whole[:size], (None if vec is None else whole[size:])
    pieces = [value]
    for bits in reversed(steps[1:]):
        if len(pieces) > 1:
            value = jnp.concatenate(pieces, 0)
        gate = yield [value]
        came = [swap_dp(value, masks_of(bits, other)) for other in range(1, 2 ** len(bits[0]))]
        pieces = [value] + after(came, gate)
    if vec is not None:
        pieces = pieces + [vec]
    if len(pieces) > 1:
        value = jnp.concatenate(pieces, 0)
    gate = yield [value]
    sender = 1 - receiver
    masks = masks_of(steps[0], 1)
    ways = ((receiver, masks[receiver]), (sender, 0), (sender, masks[sender]))
    came = []
    for source, mask in ways:
        pairs = [(source * count + i, receiver * count + (i ^ mask)) for i in range(count)]
        came.append(lax.ppermute(value, ("section", "dp"), pairs))
    yield [value] + after(came, gate)


class Steps:
    def __init__(self, *args):
        self.steps = reduce_steps(*args)
        self.ready = next(self.steps)

    def step(self, gate=()):
        self.ready = self.steps.send(gate)
        return self.ready

    def finish(self):
        while len(self.ready) != 4:
            self.step()
        return self.ready[:2], self.ready[2:]


def after(values, earlier):
    return lax.optimization_barrier((values, earlier))[0] if earlier else values


def shards(
    section_inputs,
    seq_lengths,
    dilations,
    gains_in,
    biases_in,
    gains_mid,
    biases_mid,
    out_bias,
    w_in,
    w_out,
    conv_taps,
):
    section = lax.axis_index("section")
    count = lax.axis_size("dp")
    groups_of = (scatter_groups(count, False), scatter_groups(count, False))
    rows = jnp.swapaxes(section_inputs[0], 1, 2)
    width = rows.shape[1]
    inner = w_out.shape[1]
    taps_of = (conv_taps.shape[1], DEC_TAPS)

    own_w = (jnp.swapaxes(w_in[0], 0, 1), w_out[0], conv_taps[0])
    send_rows = pick_rows(rows)
    got_w = tuple(swap_sections(member) for member in own_w)
    got_rows = swap_sections(after(send_rows, got_w))
    small = pack_small(gains_in, biases_in, gains_mid[0], biases_mid[0], out_bias, dilations)
    got_small = swap_sections(small)

    outs, send_y, grad_dec, keep_dec, send_dec, vec, *kept = main_call(
        taps_of, groups_of[1], seq_lengths, rows, got_rows, small, got_small, own_w, got_w
    )
    dec = Steps(keep_dec, swap_sections(send_dec), groups_of[1], 1, vec)
    gradient = after(grad_dec, dec.ready)
    grad_projected, vec, keep_enc, send_enc = encoder_call(
        taps_of[0], groups_of[0], seq_lengths, gradient, small, got_small, kept, own_w[1], got_w[1], own_w[2], got_w[2]
    )
    got_y = swap_sections(send_y)
    enc_early = swap_sections(send_enc)
    grad_projected = after(grad_projected, dec.step())
    grads_x, send_gx, vec = first_call(
        0, grad_dec, grad_dec, grad_projected, vec, kept[0:3], small, got_small, own_w[0], got_w[0]
    )

    def joined(pair, got):
        pair = lax.dynamic_update_slice_in_dim(pair, got[None], 1 - section, 0)
        return jnp.swapaxes(pair, 1, 2)[None]

    enc = Steps(keep_enc, enc_early, groups_of[0], 0, vec)
    got_gx = swap_sections(send_gx)
    outputs = joined(outs, got_y)
    input_grads = joined(grads_x, got_gx)
    named = {"d": dec, "e": enc}
    last = ()
    for name in SEQ:
        if name in named:
            if len(named[name].ready) != 4:
                last = named[name].step(last)
        else:
            last = [*last, outputs if name == "y" else input_grads]
    enc = enc.finish()
    dec = dec.finish()
    grads = unpack(taps_of, groups_of, enc, dec, width, inner)
    return (
        outputs,
        input_grads,
        grads[3],
        grads[4],
        grads[5][None],
        grads[6][None],
        grads[7],
        jnp.swapaxes(grads[0], 0, 1)[None],
        grads[1][None],
        grads[2][None],
    )


def solution(mesh):
    in_specs = (
        P("section", None, "dp", None),
        P(None, "dp"),
        P("section"),
        P("section", None),
        P("section", None),
        P("section", None, None),
        P("section", None, None),
        P("section", None),
        P("section", None, None),
        P("section", None, None),
        P("section", None, None, None),
    )
    out_specs = (
        P("section", None, "dp", None),
        P("section", None, "dp", None),
        P("section", None),
        P("section", None),
        P("section", None, None),
        P("section", None, None),
        P("section", None),
        P("section", None, None),
        P("section", None, None),
        P("section", None, None, None),
    )
    return jax.shard_map(shards, mesh=mesh, in_specs=in_specs, out_specs=out_specs, check_vma=False)
```

```python
import functools

import jax
import jax.numpy as jnp
from jax import lax
from jax.experimental import pallas as pl
from jax.experimental.pallas import tpu as pltpu
from jax.sharding import PartitionSpec as P

DEC_TAPS = 3
EPS = 1e-05
LANES = 128
CHUNK = 80
VEC_ROWS = 48
SMALL_ROWS = 8
PIECES = 5
LOOPS = (False, True, False)
BF = jnp.bfloat16
F32 = jnp.float32
VMEM_LIMIT = 62 * 2**20
SMALL_LIMIT = 62 * 2**20
SEQ = "ddeedeyxdede"
ANY = pl.BlockSpec(memory_space=pl.ANY)
SMEM = pl.BlockSpec(memory_space=pltpu.SMEM)
VMEM = pl.BlockSpec(memory_space=pltpu.VMEM)


def shape(dims, dtype):
    return jax.ShapeDtypeStruct(tuple(dims), dtype)


def nn(left, right):
    return jnp.dot(left, right, preferred_element_type=F32)


def nt(left, right):
    return lax.dot_general(left, right, (((1,), (1,)), ((), ())), preferred_element_type=F32)


def tn(left, right):
    return lax.dot_general(left, right, (((0,), (0,)), ((), ())), preferred_element_type=F32)


def lane_block(index):
    return pl.ds(pl.multiple_of(index * LANES, LANES), LANES)


def chunks(rows):
    size = CHUNK if rows % CHUNK == 0 else 16
    return [slice(at, at + size) for at in range(0, rows, size)]


def folded(values):
    return jnp.sum(values.reshape(values.shape[0] // 8, 8, values.shape[1]), 0)


def column(vector):
    return jnp.broadcast_to(vector, (LANES, vector.shape[1])).T


def norm_forward(source, half_gain, half_bias, normed, slope, hidden, devs, row, units):
    feats, tokens = source.shape
    scale = 1.0 / feats

    def stats(here):
        base = source[0:1, here].astype(F32)
        total = jnp.zeros((8, LANES), F32)
        squares = jnp.zeros((8, LANES), F32)
        for part in chunks(feats):
            moved = source[part, here].astype(F32) - base
            total = total + folded(moved)
            squares = squares + folded(moved * moved)
        average = jnp.sum(total, 0, keepdims=True) * scale
        variance = jnp.sum(squares, 0, keepdims=True) * scale - average * average
        inverse_dev = lax.rsqrt(jnp.maximum(variance, 0.0) + EPS)
        return (average + base) * inverse_dev, inverse_dev

    def finish(here, offset, inverse_dev):
        devs[row : row + 1, here] = inverse_dev
        for part in chunks(feats):
            values = source[part, here].astype(F32) * inverse_dev - offset
            gain = half_gain[part, :]
            half = values * gain + half_bias[part, :]
            tan = jnp.tanh(half)
            weight = 1.0 + tan
            out = half * weight
            normed[part, here] = values.astype(BF)
            slope[part, here] = ((weight + out * (1.0 - tan)) * gain).astype(BF)
            hidden[part, here] = out.astype(hidden.dtype)

    if units is None:

        def body(unit, carry):
            following = stats(lane_block(jnp.minimum(unit + 1, tokens // LANES - 1)))
            finish(lane_block(unit), *carry)
            return following

        lax.fori_loop(0, tokens // LANES, body, stats(lane_block(0)))
        return
    for unit in units:
        here = slice(unit * LANES, (unit + 1) * LANES)
        finish(here, *stats(here))


def norm_backward(gradient, slope, normed, devs, row, gain_sums, bias_sums, means, emit, loops):
    feats, tokens = gradient.shape
    units = tokens // LANES
    scale = 1.0 / feats
    means[...] = jnp.zeros_like(means)

    def collect(rows, size):
        gain_sum = jnp.zeros((size, LANES), F32)
        bias_sum = jnp.zeros((size, LANES), F32)
        for unit in range(units):
            here = slice(unit * LANES, (unit + 1) * LANES)
            scaled = gradient[rows, here] * slope[rows, here].astype(F32)
            weighted = scaled * normed[rows, here].astype(F32)
            gain_sum = gain_sum + weighted
            bias_sum = bias_sum + scaled
            means[0:8, here] += folded(scaled)
            means[8:16, here] += folded(weighted)
        gain_sums[rows, :] = gain_sum
        bias_sums[rows, :] = bias_sum

    def finish(here):
        inverse_dev = devs[row : row + 1, here]
        first = jnp.sum(means[0:8, here], 0, keepdims=True) * (scale * inverse_dev)
        second = jnp.sum(means[8:16, here], 0, keepdims=True) * (scale * inverse_dev)
        for part in chunks(feats):
            scaled = gradient[part, here] * slope[part, here].astype(F32)
            emit(part, here, scaled * inverse_dev - first - normed[part, here].astype(F32) * second)

    if loops:
        size = chunks(feats)[0].stop

        def one_chunk(index, _):
            collect(pl.ds(pl.multiple_of(index * size, 16), size), size)
            return 0

        def one_unit(unit, _):
            finish(lane_block(unit))
            return 0

        lax.fori_loop(0, feats // size, one_chunk, 0)
        lax.fori_loop(0, units, one_unit, 0, unroll=2)
        return
    for part in chunks(feats):
        collect(part, part.stop - part.start)
    for unit in range(units):
        finish(slice(unit * LANES, (unit + 1) * LANES))


def write_shifts(source, target, begins, offsets, units):
    feats, tokens = source.shape
    count = tokens // LANES
    block = lambda unit: slice(unit * LANES, (unit + 1) * LANES)
    for unit in units:
        joined_behind = (begins(unit) == 0).astype(F32) if unit > 0 else None
        joined_ahead = (begins(unit + 1) == 0).astype(F32) if unit < count - 1 else None
        for part in chunks(feats):
            size = part.stop - part.start
            lane = lax.broadcasted_iota(jnp.int32, (size, LANES), 1)
            zero = jnp.zeros((size, LANES), F32)
            current = source[part, block(unit)].astype(F32)
            behind = zero if unit == 0 else source[part, block(unit - 1)].astype(F32) * joined_behind
            ahead = zero if unit == count - 1 else source[part, block(unit + 1)].astype(F32) * joined_ahead
            for position, (sign, step) in enumerate(offsets):
                if sign == 0:
                    moved = current
                elif sign < 0:
                    moved = pltpu.roll(jnp.where(lane < LANES - step, current, behind), step, 1)
                else:
                    moved = pltpu.roll(jnp.where(lane >= step, current, ahead), LANES - step, 1)
                rows = slice(feats * position + part.start, feats * position + part.stop)
                target[rows, block(unit)] = moved.astype(BF)


def tap_offsets(taps, dilation, flip):
    result = []
    for position in range(taps):
        factor = (position - 2) * (-1 if flip else 1)
        result.append(((factor > 0) - (factor < 0), abs(factor) * dilation))
    return result


def layout(taps, width, inner):
    wide = width // LANES * inner
    taps_at = wide
    w_in_at = taps_at + taps * (inner // LANES) * inner
    tails_at = w_in_at + wide
    (_, _), (last, _) = tail_places(taps, width, inner)
    return taps_at, w_in_at, tails_at, tails_at + (last + 1) * inner


def tail_places(taps, width, inner):
    size = width % LANES
    places = []
    group, lane = 0, taps * (inner % LANES)
    for _ in range(2):
        if lane + size > LANES:
            group, lane = group + 1, 0
        places.append((group, lane))
        lane += size
    return places


def scatter_groups(count, full):
    total = count.bit_length() - 1
    rest = [list(range(2, min(4, total)))] if full and total > 2 else []
    return [[[bit] for bit in bits if bit < total] + rest for bits in ((0, 1), (1, 0))]


def share_count(groups):
    return 2 ** sum(len(bits) for bits in groups)


def padded_rows(rows, groups):
    unit = 2 * 16 * share_count(groups[0])
    return pl.cdiv(rows, unit) * unit


def put_wide(buf, row, matrix, tails_at, place):
    rows, cols = matrix.shape
    whole = cols // LANES
    for q in range(whole):
        buf[row + q * rows : row + (q + 1) * rows, :] = matrix[:, LANES * q : LANES * (q + 1)].astype(BF)
    if cols > whole * LANES:
        group, lane = place
        at = tails_at + group * rows
        buf[at : at + rows, lane : lane + cols - whole * LANES] = matrix[:, LANES * whole :].astype(BF)


def put_taps(buf, taps, width, shifted, grad_mixed):
    inner = grad_mixed.shape[0]
    taps_at, _, tails_at, _ = layout(taps, width, inner)
    whole = inner // LANES
    tail = inner - whole * LANES
    for k in range(taps):
        grad = nt(shifted[inner * k : inner * (k + 1), :], grad_mixed[...])
        for q in range(whole):
            at = taps_at + inner * (whole * k + q)
            buf[at : at + inner, :] = grad[:, LANES * q : LANES * (q + 1)].astype(BF)
        buf[tails_at : tails_at + inner, tail * k : tail * (k + 1)] = grad[:, LANES * whole :].astype(BF)


def row_sums(acc):
    return jnp.sum(acc.T, 0, keepdims=True)


def put_vectors(buf, at, vec, sums):
    vec[...] = jnp.zeros_like(vec)
    row = 0
    for total in sums:
        for lane in range(0, total.shape[1], LANES):
            part = total[:, lane : lane + LANES]
            vec[row : row + 1, 0 : part.shape[1]] = part
            row += 1
    buf[at : at + VEC_ROWS, :] = vec[...].astype(BF)


def relative_index(position, groups):
    result = 0
    for bits in reversed(groups):
        size = 2 ** len(bits)
        result = result + (position & (size - 1)) * 2 ** bits[0]
        position = position >> len(bits)
    return result


def owner_of(position, side, groups, index):
    both = [relative_index(position, order) for order in groups]
    mask = sum(2**bit for bits in groups[0] for bit in bits)
    return jnp.where(side == 0, both[0], both[1]) ^ (index & mask)


def position_of(owner, side, groups, index):
    distance = owner ^ index
    position = 0
    for bits in groups[side]:
        position = position * 2 ** len(bits) + ((distance >> bits[0]) & (2 ** len(bits) - 1))
    return position


class RowsOut:
    def __init__(self, buf, keep, send, section, index, groups, sems):
        self.buf, self.keep, self.send, self.sems = buf, keep, send, sems
        self.section, self.index, self.groups = section, index, groups
        self.count = share_count(groups[0])
        self.share = keep.shape[0] // self.count
        self.sizes = []

    def start(self, first, last):
        for number in range(2 * self.count):
            low, high = max(first, number * self.share), min(last, (number + 1) * self.share)
            if low >= high:
                continue
            side, owner = divmod(number, self.count)
            place = position_of(owner, side, self.groups, self.index) * self.share + (low - number * self.share)
            target = pl.ds(pl.multiple_of(place, 16), high - low)
            source = self.buf.at[low:high]
            sem = self.sems.at[len(self.sizes)]
            pl.when(self.section == side)(pltpu.make_async_copy(source, self.keep.at[target], sem).start)
            pl.when(self.section != side)(pltpu.make_async_copy(source, self.send.at[target], sem).start)
            self.sizes.append(high - low)

    def wait(self):
        for number, size in enumerate(self.sizes):
            source, target = self.buf.at[0:size], self.keep.at[0:size]
            pltpu.make_async_copy(source, target, self.sems.at[number]).wait()


def forward_block(taps, begins, dilation, x, y, weights, turned, cols, kept, hmid, prod, ready):
    w_in_t, w_out, conv = weights
    w_out_t, conv_t = turned
    g1, b1, g2, b2, g3, b3, ob = cols
    n1, s1, r, n2, s2, n3, s3, hin, shifted, hout = kept
    inner, tokens = hmid.shape
    units = tokens // LANES
    narrow = prod.at[0:inner]
    parts = [range(at, min(at + units // 2, units)) for at in range(0, units, units // 2)]
    columns = [slice(part.start * LANES, part.stop * LANES) for part in parts]
    offsets = tap_offsets(taps, dilation, False)

    def mix(part):
        narrow[:, columns[part]] = nn(conv_t[:, 0 : taps * inner], shifted[:, columns[part]])

    def leave(part):
        here = columns[part]
        bias = jnp.concatenate([ob[...]] * len(parts[part]), 1)
        y[:, here] = (x[:, here].astype(F32) + nn(w_out_t[...], hout[:, here]) + bias).astype(BF)

    norm_forward(x, g1, b1, n1, s1, hin, r, 0, None)
    ready(0)
    narrow[...] = nn(w_in_t[...], hin[...])
    ready(1)
    norm_forward(narrow, g2, b2, n2, s2, hmid, r, 1, parts[0])
    for k in range(taps):
        conv_t[:, inner * k : inner * (k + 1)] = conv[k].T
    w_out_t[...] = w_out[...].T
    norm_forward(narrow, g2, b2, n2, s2, hmid, r, 1, parts[1])
    write_shifts(hmid, shifted, begins, offsets, parts[0])
    mix(0)
    write_shifts(hmid, shifted, begins, offsets, parts[1])
    mix(1)
    norm_forward(narrow, g3, b3, n3, s3, hout, r, 2, parts[0])
    leave(0)
    norm_forward(narrow, g3, b3, n3, s3, hout, r, 2, parts[1])
    leave(1)


def fill_columns(small, cols):
    g1, b1, g2, b2, g3, b3, ob = cols
    width, inner = g1.shape[0], g2.shape[0]
    for target, row, scale in ((g1, 0, 0.5), (b1, 1, 0.5), (ob, 2, 1.0)):
        target[...] = column(small[row : row + 1, 0:width] * scale)
    for target, row in ((g2, 3), (b2, 4), (g3, 5), (b3, 6)):
        target[...] = column(small[row : row + 1, 0:inner] * 0.5)


def back_third(gy, w_out, kept, prod, means, grad_mixed, gain_sums, bias_sums, beside):
    n3, s3, r = kept
    inner = w_out.shape[0]
    narrow = prod.at[0:inner]
    narrow[...] = nn(w_out[...], gy[...])
    beside()

    def emit(part, here, value):
        grad_mixed[part, here] = value.astype(BF)

    norm_backward(narrow, s3, n3, r, 2, gain_sums, bias_sums, means, emit, LOOPS[0])


def back_second(
    taps, begins, dilation, conv_w, kept, prod, means, grad_mixed, moved, grad_projected, gain_sums, bias_sums, ready,
    weights=None,
):
    n2, s2, r = kept
    inner = grad_mixed.shape[0]
    narrow = prod.at[0:inner]
    write_shifts(grad_mixed, moved, begins, tap_offsets(taps, dilation, True), range(grad_mixed.shape[1] // LANES))
    if weights is not None:
        weights()
    narrow[...] = nn(conv_w[...], moved[...])
    ready()

    def emit(part, here, value):
        grad_projected[part, here] = value.astype(BF)

    norm_backward(narrow, s2, n2, r, 1, gain_sums, bias_sums, means, emit, LOOPS[1])


def back_first(gy, w_in_t, kept, prod, means, grad_projected, gx, gain_sums, bias_sums, ready):
    n1, s1, r = kept
    prod[...] = tn(w_in_t[...], grad_projected[...])
    ready()

    def emit(part, here, value):
        gx[part, here] = (gy[part, here].astype(F32) + value).astype(BF)

    norm_backward(prod, s1, n1, r, 0, gain_sums, bias_sums, means, emit, LOOPS[2])


def put_w_out(buf, taps, hout_ones, gy):
    grad = nt(hout_ones[...], gy[...])
    inner, width = hout_ones.shape[0] - 16, gy.shape[0]
    _, _, tails_at, end = layout(taps, width, inner)
    buf[tails_at:end, :] = jnp.zeros((end - tails_at, LANES), BF)
    put_wide(buf, 0, grad[0:inner], tails_at, tail_places(taps, width, inner)[0])
    return grad[inner : inner + 1]


def put_w_in(buf, taps, grad_projected, hin):
    inner, width = grad_projected.shape[0], hin.shape[0]
    _, w_in_at, tails_at, _ = layout(taps, width, inner)
    put_wide(buf, w_in_at, nt(grad_projected[...], hin[...]), tails_at, tail_places(taps, width, inner)[1])


def gain_and_bias(gain, sums):
    return [row_sums(acc[...]) / gain for acc in sums]


def put_rows(target, rows):
    target[...] = jnp.zeros_like(target)
    for at, row in enumerate(rows):
        target[at : at + 1, 0 : row.shape[1]] = row


def gains_of(small, width, inner):
    return small[0:1, 0:width], small[3:4, 0:inner], small[5:6, 0:inner]


def pick_small(leading, own, got):
    flag = leading.astype(F32)
    return own[...] * flag + got[...] * (1.0 - flag)


def start_all(copies):
    for copy in copies:
        copy.start()


def pick_rows_kernel(rows, send, hold, sem):
    section = lax.axis_index("section")
    size = send.shape[0] // PIECES
    parts = [slice(size * i, size * (i + 1)) for i in range(PIECES)]
    arrive = [
        pltpu.make_async_copy(rows.at[1 - section, part], hold.at[part], sem.at[i]) for i, part in enumerate(parts)
    ]
    leave = [pltpu.make_async_copy(hold.at[part], send.at[part], sem.at[PIECES + i]) for i, part in enumerate(parts)]
    start_all(arrive)
    for come, go in zip(arrive, leave):
        come.wait()
        go.start()
    for go in leave:
        go.wait()


def pick_rows(rows):
    return pl.pallas_call(
        pick_rows_kernel,
        in_specs=[ANY],
        out_specs=ANY,
        out_shape=shape(rows.shape[1:], BF),
        scratch_shapes=[pltpu.VMEM(rows.shape[1:], BF), pltpu.SemaphoreType.DMA((2 * PIECES,))],
        compiler_params=pltpu.CompilerParams(vmem_limit_bytes=VMEM_LIMIT),
        cost_estimate=pl.CostEstimate(flops=0, bytes_accessed=8 * 2**20, transcendentals=0),
        name="pick_rows",
    )(rows)


def pack_small_kernel(gin, bin_, gmid, bmid, out_bias, dilation, small):
    width, inner = gin.shape[1], gmid.shape[1]
    small[...] = jnp.zeros_like(small)
    for row, ref in ((0, gin), (1, bin_), (2, out_bias)):
        small[row : row + 1, 0:width] = ref[...]
    for row, ref, which in ((3, gmid, 0), (4, bmid, 0), (5, gmid, 1), (6, bmid, 1)):
        small[row : row + 1, 0:inner] = ref[which : which + 1, :]
    small[7:8, :] = jnp.full((1, small.shape[1]), dilation[0].astype(F32), F32)


def pack_small(gin, bin_, gmid, bmid, out_bias, dilation):
    return pl.pallas_call(
        pack_small_kernel,
        in_specs=[VMEM] * 5 + [SMEM],
        out_specs=VMEM,
        out_shape=shape((SMALL_ROWS, gin.shape[1]), F32),
        compiler_params=pltpu.CompilerParams(vmem_limit_bytes=VMEM_LIMIT),
        name="pack_small",
    )(gin, bin_, gmid, bmid, out_bias, dilation)


def kept_shapes(taps, width, inner, tokens):
    wide, narrow = (width, tokens), (inner, tokens)
    return [
        (wide, BF), (wide, BF), ((8, tokens), F32), (narrow, BF), (narrow, BF), (narrow, BF), (narrow, BF),
        (wide, BF), ((inner * taps, tokens), BF), (narrow, BF),
    ]


def column_shapes(width, inner):
    return [(width, LANES)] * 2 + [(inner, LANES)] * 4 + [(width, LANES)]


def main_kernel(taps_of, groups, *refs):
    refs = list(refs)

    def take(number):
        taken = refs[:number]
        del refs[:number]
        return taken

    seq, rows, got, small_own, small_got = take(5)
    own_w, got_w = take(3), take(3)
    outs, send_y, grad_out, keep_buf, send_buf, vec_out = take(6)
    kept_out = take(10)
    x, cot = take(2)
    enc_w, dec_w = take(3), take(3)
    small = take(2)
    enc_kept, dec_kept = take(10), take(10)
    cols = take(7)
    hmid, prod, means, y_enc, gx, w_out_t, conv_t, conv_w, grad_mixed, grad_projected, moved, buf = take(12)
    ag1, ab1, ag2, ab2, ag3, ab3, vec, sem, row_sems = take(9)

    section = lax.axis_index("section")
    index = lax.axis_index("dp")
    leading = section == 0
    width, tokens = x.shape
    inner = hmid.shape[0]
    small[0][...] = pick_small(leading, small_own, small_got)
    small[1][...] = pick_small(leading, small_got, small_own)
    dilation = [jnp.max(member[7:8, 0:LANES]).astype(jnp.int32) for member in small]

    def begins(unit):
        return seq[section, unit]

    loads = [(x, rows.at[0], got), (enc_w[0], own_w[0], got_w[0]), (enc_w[2], own_w[2], got_w[2])]
    loads += [(enc_w[1], own_w[1], got_w[1]), (dec_w[0], got_w[0], own_w[0]), (dec_w[1], got_w[1], own_w[1])]
    loads += [(dec_w[2], got_w[2].at[0 : taps_of[1]], own_w[2].at[0 : taps_of[1]]), (cot, got, rows.at[1])]

    def load(at):
        target, first, second = loads[at]
        pl.when(leading)(pltpu.make_async_copy(first, target, sem.at[at]).start)
        pl.when(jnp.logical_not(leading))(pltpu.make_async_copy(second, target, sem.at[at]).start)

    for at in range(4):
        load(at)

    def ready(at):
        pltpu.make_async_copy(loads[at][1], loads[at][0], sem.at[at]).wait()

    fill_columns(small[0], cols)
    hout_ones = dec_kept[9]
    dec_kept[9] = hout_ones.at[0:inner]
    hout_ones[inner:, :] = jnp.ones((16, tokens), BF)
    ready(0)

    def enc_ready(which):
        for at in ((1,), (2, 3))[which]:
            ready(at)
        if which:
            for at in range(4, 8):
                load(at)

    turned = (w_out_t, conv_t)
    forward_block(taps_of[0], begins, dilation[0], x, y_enc, enc_w, turned, cols, enc_kept, hmid, prod, enc_ready)
    saves = [pltpu.make_async_copy(a, b, sem.at[8 + i]) for i, (a, b) in enumerate(zip(enc_kept, kept_out))]
    start_all(saves)

    fill_columns(small[1], cols)
    for at in range(4, 8):
        ready(at)
    for k in range(taps_of[1]):
        conv_w[:, inner * k : inner * (k + 1)] = dec_w[2][k]
    y_dec = x
    forward_block(
        taps_of[1], begins, dilation[1], y_enc, y_dec, dec_w, turned, cols, dec_kept, hmid, prod, lambda which: None
    )
    pl.when(leading)(pltpu.make_async_copy(y_enc, outs.at[0], sem.at[18]).start)
    pl.when(leading)(pltpu.make_async_copy(y_dec, send_y, sem.at[19]).start)
    pl.when(jnp.logical_not(leading))(pltpu.make_async_copy(y_dec, outs.at[1], sem.at[18]).start)
    pl.when(jnp.logical_not(leading))(pltpu.make_async_copy(y_enc, send_y, sem.at[19]).start)

    n1, s1, r, n2, s2, n3, s3, hin, shifted, hout = dec_kept
    rows_out = RowsOut(buf, keep_buf, send_buf, section, index, groups, row_sems)
    w_in_at, _, end = layout(taps_of[1], width, inner)[1:]

    bias = []

    def third_beside():
        bias.append(put_w_out(buf, taps_of[1], hout_ones, cot))

    def first_beside():
        put_w_in(buf, taps_of[1], grad_projected, hin)

    back_third(cot, dec_w[1], (n3, s3, r), prod, means, grad_mixed, ag3, ab3, third_beside)
    put_taps(buf, taps_of[1], width, shifted, grad_mixed)
    back_second(
        taps_of[1], begins, dilation[1], conv_w, (n2, s2, r), prod, means, grad_mixed, moved, grad_projected, ag2, ab2,
        lambda: None,
    )
    rows_out.start(0, w_in_at)
    back_first(cot, dec_w[0], (n1, s1, r), prod, means, grad_projected, gx, ag1, ab1, first_beside)
    rows_out.start(w_in_at, end)
    last = pltpu.make_async_copy(gx, grad_out, sem.at[20])
    last.start()
    g1, g2, g3 = gains_of(small[1], width, inner)
    first, second, third = gain_and_bias(g1, (ag1, ab1)), gain_and_bias(g2, (ag2, ab2)), gain_and_bias(g3, (ag3, ab3))
    put_vectors(vec_out, 0, vec, first + [second[0], third[0], second[1], third[1]] + bias)
    rows_out.wait()
    wait_all(saves + [last])
    pltpu.make_async_copy(y_enc, outs.at[0], sem.at[18]).wait()
    pltpu.make_async_copy(y_dec, send_y, sem.at[19]).wait()


def main_call(taps_of, groups, seq, rows, got, small_own, small_got, own_w, got_w):
    _, width, tokens = rows.shape
    inner = own_w[1].shape[0]
    half = padded_rows(layout(taps_of[1], width, inner)[3], groups) // 2
    wide, narrow = (width, tokens), (inner, tokens)
    weight_shapes = [(inner, width), (inner, width)]
    scratch = [(wide, BF)] * 2
    for taps in taps_of:
        scratch += [(dims, BF) for dims in weight_shapes + [(taps, inner, inner)]]
    scratch += [((SMALL_ROWS, width), F32)] * 2
    scratch += kept_shapes(taps_of[0], width, inner, tokens) + kept_shapes(taps_of[1], width, inner, tokens)[:-1]
    scratch += [((inner + 16, tokens), BF)]
    scratch += [(dims, F32) for dims in column_shapes(width, inner)]
    scratch += [
        (narrow, BF), (wide, F32), ((16, tokens), F32), (wide, BF), (wide, BF), ((width, inner), BF),
        ((inner, inner * taps_of[0]), BF), ((inner, inner * taps_of[1]), BF),
        (narrow, BF), (narrow, BF), ((inner * taps_of[1], tokens), BF), ((2 * half, LANES), BF),
    ]
    scratch += [((width, LANES), F32)] * 2 + [((inner, LANES), F32)] * 4 + [((VEC_ROWS, LANES), F32)]
    block = shape((half, LANES), BF)
    outs = [shape((2,) + wide, BF), shape(wide, BF), shape(wide, BF), block, block, shape((VEC_ROWS, LANES), BF)]
    outs += [shape(dims, dtype) for dims, dtype in kept_shapes(taps_of[0], width, inner, tokens)]
    flops = 2 * tokens * inner * (2 * width + taps_of[0] * inner + 3 * (2 * width + taps_of[1] * inner))
    return pl.pallas_call(
        functools.partial(main_kernel, taps_of, groups),
        in_specs=[SMEM, ANY, ANY, VMEM, VMEM] + [ANY] * 6,
        out_specs=[ANY] * 5 + [VMEM] + [ANY] * 10,
        out_shape=outs,
        scratch_shapes=[pltpu.VMEM(dims, dtype) for dims, dtype in scratch]
        + [pltpu.SemaphoreType.DMA((24,)), pltpu.SemaphoreType.DMA((8 * share_count(groups[0]),))],
        compiler_params=pltpu.CompilerParams(vmem_limit_bytes=VMEM_LIMIT),
        cost_estimate=pl.CostEstimate(flops=4 * flops, bytes_accessed=60 * 2**20, transcendentals=0),
        name="main_blocks",
    )(seq, rows, got, small_own, small_got, *own_w, *got_w)


def load_weight(leading, own, got, target, sem):
    pl.when(leading)(pltpu.make_async_copy(own, target, sem).start)
    pl.when(jnp.logical_not(leading))(pltpu.make_async_copy(got, target, sem).start)
    return pltpu.make_async_copy(own, target, sem)


def wait_all(copies):
    for copy in copies:
        copy.wait()


def encoder_kernel(
    taps, groups,
    seq, gy_in, small_own, small_got, n3_in, s3_in, r_in, shifted_in, hout_in, n2_in, s2_in, hin_in, own_out, got_out,
    own_conv, got_conv,
    grad_projected_out, vec_out, keep_buf, send_buf,
    gy, n3, s3, r, shifted, hout_ones, n2, s2, hin, w_out, conv, conv_w, prod, means, grad_mixed, moved, grad_projected,
    buf, ag3, ab3, ag2, ab2, sem, row_sems,
):
    section = lax.axis_index("section")
    leading = section == 0
    width, tokens = gy.shape
    inner = w_out.shape[0]
    w_in_at, _, end = layout(taps, width, inner)[1:]
    hout = hout_ones.at[0:inner]
    pairs = (
        (gy_in, gy), (s3_in, s3), (n3_in, n3), (r_in, r), (hout_in, hout), (shifted_in, shifted), (n2_in, n2), (s2_in, s2),
        (hin_in, hin),
    )
    loads = [pltpu.make_async_copy(a, b, sem.at[2 + i]) for i, (a, b) in enumerate(pairs)]
    loads[0].start()
    weight = load_weight(leading, own_out, got_out, w_out, sem.at[0])
    start_all(loads[1:5])
    conv_weight = load_weight(leading, own_conv, got_conv, conv, sem.at[1])
    start_all(loads[5:])
    hout_ones[inner:, :] = jnp.ones((16, tokens), BF)
    small = pick_small(leading, small_own, small_got)
    dilation = jnp.max(small[7:8, 0:LANES]).astype(jnp.int32)

    def begins(unit):
        return seq[section, unit]

    def weights():
        conv_weight.wait()
        for k in range(taps):
            conv_w[:, inner * k : inner * (k + 1)] = conv[k]

    wait_all([weight, loads[0]])
    bias = []

    def third_beside():
        wait_all(loads[1:5])
        bias.append(put_w_out(buf, taps, hout_ones, gy))

    back_third(gy, w_out, (n3, s3, r), prod, means, grad_mixed, ag3, ab3, third_beside)
    wait_all([loads[5]])
    put_taps(buf, taps, width, shifted, grad_mixed)
    back_second(
        taps, begins, dilation, conv_w, (n2, s2, r), prod, means, grad_mixed, moved, grad_projected, ag2, ab2,
        lambda: wait_all(loads[6:8]), weights,
    )
    out = pltpu.make_async_copy(grad_projected, grad_projected_out, sem.at[11])
    out.start()
    rows_out = RowsOut(buf, keep_buf, send_buf, section, lax.axis_index("dp"), groups, row_sems)
    rows_out.start(0, w_in_at)
    loads[8].wait()
    put_w_in(buf, taps, grad_projected, hin)
    rows_out.start(w_in_at, end)
    _, g2, g3 = gains_of(small, width, inner)
    second, third = gain_and_bias(g2, (ag2, ab2)), gain_and_bias(g3, (ag3, ab3))
    put_rows(vec_out, [second[0], third[0], second[1], third[1]] + bias)
    out.wait()
    rows_out.wait()


def encoder_call(taps, groups, seq, gy, small_own, small_got, kept, own_out, got_out, own_conv, got_conv):
    width, tokens = gy.shape
    inner = own_out.shape[0]
    n1, s1, r, n2, s2, n3, s3, hin, shifted, hout = kept
    rows = layout(taps, width, inner)[3]
    half = padded_rows(rows, groups) // 2
    wide, narrow = (width, tokens), (inner, tokens)
    scratch = [
        (wide, BF), (narrow, BF), (narrow, BF), ((8, tokens), F32), ((inner * taps, tokens), BF),
        ((inner + 16, tokens), BF), (narrow, BF), (narrow, BF), (wide, BF), ((inner, width), BF),
        ((taps, inner, inner), BF), ((inner, inner * taps), BF), (narrow, F32), ((16, tokens), F32), (narrow, BF),
        ((inner * taps, tokens), BF), (narrow, BF), ((rows, LANES), BF),
    ]
    scratch += [((inner, LANES), F32)] * 4
    flops = 2 * tokens * inner * (3 * width + 2 * taps * inner)
    block = shape((half, LANES), BF)
    return pl.pallas_call(
        functools.partial(encoder_kernel, taps, groups),
        in_specs=[SMEM, ANY, VMEM, VMEM] + [ANY] * 12,
        out_specs=[ANY, VMEM, ANY, ANY],
        out_shape=[shape(narrow, BF), shape((SMALL_ROWS, width), F32), block, block],
        scratch_shapes=[pltpu.VMEM(dims, dtype) for dims, dtype in scratch]
        + [pltpu.SemaphoreType.DMA((12,)), pltpu.SemaphoreType.DMA((8 * share_count(groups[0]),))],
        compiler_params=pltpu.CompilerParams(vmem_limit_bytes=SMALL_LIMIT),
        cost_estimate=pl.CostEstimate(flops=4 * flops, bytes_accessed=20 * 2**20, transcendentals=0),
        name="encoder_back",
    )(
        seq, gy, small_own, small_got, n3, s3, r, shifted, hout, n2, s2, hin, own_out, got_out, own_conv, got_conv
    )


def first_kernel(
    block, gy_first, gy_second, grad_projected_in, small_own, small_got, vecs, n1_in, s1_in, r_in, own_in, got_in,
    *refs,
):
    outs_of, refs = refs[: 2 - block], refs[2 - block :]
    vec_out, gy, grad_projected, n1, s1, r, w_in_t, prod, means, gx, ag1, ab1, vec, sem = refs
    leading = lax.axis_index("section") == 0
    mine = leading if block == 0 else jnp.logical_not(leading)
    width, inner = gy.shape[0], grad_projected.shape[0]
    pairs = ((grad_projected_in, grad_projected), (s1_in, s1), (n1_in, n1), (r_in, r))
    loads = [pltpu.make_async_copy(a, b, sem.at[2 + i]) for i, (a, b) in enumerate(pairs)]
    loads[0].start()
    weight = load_weight(mine, own_in, got_in, w_in_t, sem.at[0])
    start_all(loads[1:])
    loads.append(load_weight(leading, gy_first, gy_second, gy, sem.at[1]))
    small = pick_small(mine, small_own, small_got)
    wait_all([loads[0], weight])

    def save(value, at_home, away, sem):
        pl.when(leading)(pltpu.make_async_copy(value, at_home, sem).start)
        pl.when(jnp.logical_not(leading))(pltpu.make_async_copy(value, away, sem).start)
        return pltpu.make_async_copy(value, away, sem)

    waits = []

    def ready():
        wait_all(loads[1:])
        if block == 0:
            outs, send = outs_of
            waits.append(save(gy, send, outs.at[1], sem.at[6]))

    back_first(gy, w_in_t, (n1, s1, r), prod, means, grad_projected, gx, ag1, ab1, ready)
    if block == 0:
        outs, send = outs_of
        waits.append(save(gx, outs.at[0], send, sem.at[7]))
    else:
        waits.append(pltpu.make_async_copy(gx, outs_of[0], sem.at[7]))
        waits[-1].start()
    sums = gain_and_bias(gains_of(small, width, inner)[0], (ag1, ab1))
    sums += [vecs[row : row + 1, 0:size] for row, size in enumerate((inner, inner, inner, inner, width))]
    put_vectors(vec_out, 0, vec, sums)
    wait_all(waits)


def first_call(block, gy_first, gy_second, grad_projected, vecs, kept, small_own, small_got, own_in, got_in):
    n1, s1, r = kept
    width, tokens = n1.shape
    inner = grad_projected.shape[0]
    wide, narrow = (width, tokens), (inner, tokens)
    scratch = [
        (wide, BF), (narrow, BF), (wide, BF), (wide, BF), ((8, tokens), F32), ((inner, width), BF), (wide, F32),
        ((16, tokens), F32), (wide, BF), ((width, LANES), F32), ((width, LANES), F32), ((VEC_ROWS, LANES), F32),
    ]
    outs = [shape((2,) + wide, BF), shape(wide, BF)] if block == 0 else [shape(wide, BF)]
    flops = 2 * tokens * inner * width
    return pl.pallas_call(
        functools.partial(first_kernel, block),
        in_specs=[ANY] * 3 + [VMEM] * 3 + [ANY] * 5,
        out_specs=[ANY] * len(outs) + [VMEM],
        out_shape=outs + [shape((VEC_ROWS, LANES), BF)],
        scratch_shapes=[pltpu.VMEM(dims, dtype) for dims, dtype in scratch] + [pltpu.SemaphoreType.DMA((8,))],
        compiler_params=pltpu.CompilerParams(vmem_limit_bytes=SMALL_LIMIT),
        cost_estimate=pl.CostEstimate(flops=8 * flops, bytes_accessed=20 * 2**20, transcendentals=0),
        name="first_%d" % block,
    )(gy_first, gy_second, grad_projected, small_own, small_got, vecs, n1, s1, r, own_in, got_in)


def load_weight(first, one, other, target, sem):
    pl.when(first)(pltpu.make_async_copy(one, target, sem).start)
    pl.when(jnp.logical_not(first))(pltpu.make_async_copy(other, target, sem).start)
    return pltpu.make_async_copy(one, target, sem)


def wait_all(copies):
    for copy in copies:
        copy.wait()


def unpack_kernel(taps_of, groups_of, *refs):
    refs = list(refs)

    def take(number):
        taken = refs[:number]
        del refs[:number]
        return taken

    own_of, got_of = [], []
    for _ in range(2):
        own_of.append(take(2))
        got_of.append(take(2))
    w_in_t_out, w_out_out, conv_out, gin, bin_, gmid, bmid, out_bias, w_in_t, w_out, conv, buf, extra, sem = refs
    inner, width = w_out.shape
    whole = inner // LANES
    tail = inner - whole * LANES
    slots = conv.shape[0]
    section = lax.axis_index("section")
    index = lax.axis_index("dp")

    def write(taps, groups, own, got):
        rows = own[0].shape[0] - VEC_ROWS
        count = share_count(groups[0])
        share = 2 * rows // count

        def body(position, _):
            for which, (pieces, side) in enumerate(((own, section), (got, 1 - section))):
                for at, ref in enumerate(pieces):
                    owner = owner_of(position + at * (count // 2), side, groups, index)
                    start = side * (2 * rows) + owner * share
                    pltpu.make_async_copy(
                        ref.at[pl.ds(pl.multiple_of(position * share, 16), share)],
                        buf.at[pl.ds(pl.multiple_of(start, 16), share)],
                        sem.at[2 * which + at],
                    ).start()
            return 0

        lax.fori_loop(0, count // 2, body, 0)
        pieces = list(own) + list(got)
        vectors = [
            pltpu.make_async_copy(ref.at[pl.ds(rows, VEC_ROWS)], extra.at[at], sem.at[4 + at])
            for at, ref in enumerate(pieces)
        ]
        start_all(vectors)
        for at, ref in enumerate(pieces):
            pltpu.make_async_copy(ref.at[pl.ds(0, rows)], buf.at[pl.ds(0, rows)], sem.at[at]).wait()
        wait_all(vectors)
        taps_at, w_in_at, tails_at, _ = layout(taps, width, inner)
        places = tail_places(taps, width, inner)

        def wide(target, row, place):
            groups = width // LANES
            for q in range(groups):
                at = row + q * inner
                target[:, LANES * q : LANES * (q + 1)] = buf[at : at + inner, :].astype(F32)
            if width > groups * LANES:
                group, lane = place
                at = tails_at + group * inner
                rest = buf[at : at + inner, :].astype(F32)
                target[:, LANES * groups :] = rest[:, lane : lane + width - groups * LANES]

        copies = []

        def leave(source, target):
            copies.append(pltpu.make_async_copy(source, target, sem.at[8 + len(copies)]))
            copies[-1].start()

        wide(w_out, 0, places[0])
        leave(w_out, w_out_out)
        tails = buf[tails_at : tails_at + inner, :].astype(F32)
        for k in range(slots):
            if k >= taps:
                conv[k] = jnp.zeros((inner, inner), F32)
            else:
                for q in range(whole):
                    at = taps_at + inner * (whole * k + q)
                    conv[k, :, LANES * q : LANES * (q + 1)] = buf[at : at + inner, :].astype(F32)
                conv[k, :, LANES * whole :] = tails[:, tail * k : tail * (k + 1)]
            leave(conv.at[k], conv_out.at[k])
        wide(w_in_t, w_in_at, places[1])
        leave(w_in_t, w_in_t_out)
        vec = sum(extra[at].astype(F32) for at in range(4))
        row = 0
        for target, member in ((gin, 0), (bin_, 0), (gmid, 0), (gmid, 1), (bmid, 0), (bmid, 1), (out_bias, 0)):
            for at in range(0, target.shape[1], LANES):
                size = min(LANES, target.shape[1] - at)
                target[member : member + 1, at : at + size] = vec[row : row + 1, 0:size]
                row += 1
        for copy in copies:
            copy.wait()

    pl.when(section == 0)(lambda: write(taps_of[0], groups_of[0], own_of[0], got_of[0]))
    pl.when(section != 0)(lambda: write(taps_of[1], groups_of[1], own_of[1], got_of[1]))


def unpack(taps_of, groups_of, enc, dec, width, inner):
    pieces = enc[0] + enc[1] + dec[0] + dec[1]
    rows = max(4 * part[0].shape[0] for part in (enc[0], dec[0]))
    return pl.pallas_call(
        functools.partial(unpack_kernel, taps_of, groups_of),
        in_specs=[ANY] * len(pieces),
        out_specs=[ANY] * 3 + [VMEM] * 5,
        out_shape=[
            shape((inner, width), F32), shape((inner, width), F32), shape((taps_of[0], inner, inner), F32),
            shape((1, width), F32), shape((1, width), F32), shape((2, inner), F32), shape((2, inner), F32),
            shape((1, width), F32),
        ],
        scratch_shapes=[
            pltpu.VMEM((inner, width), F32), pltpu.VMEM((inner, width), F32), pltpu.VMEM((taps_of[0], inner, inner), F32),
            pltpu.VMEM((rows, LANES), BF), pltpu.VMEM((4, VEC_ROWS, LANES), BF),
            pltpu.SemaphoreType.DMA((10 + taps_of[0],)),
        ],
        compiler_params=pltpu.CompilerParams(vmem_limit_bytes=SMALL_LIMIT),
        name="unpack",
    )(*pieces)


def swap_sections(value):
    return lax.ppermute(value, "section", [(0, 1), (1, 0)])


def swap_dp(value, masks):
    count = lax.axis_size("dp")
    pairs = [(s * count + i, s * count + (i ^ masks[s])) for s in range(2) for i in range(count)]
    return lax.ppermute(value, ("section", "dp"), pairs)


def rounded_sum(terms, rows):
    total = terms[0][rows].astype(F32)
    for term in terms[1:]:
        total = total + term[rows].astype(F32)
    return total.astype(BF)


def masks_of(bits, other):
    return [other << own[0] for own in bits]


def reduce_steps(keep, got, groups, receiver, vec=None):
    count = lax.axis_size("dp")
    steps = list(zip(*groups))
    terms = [keep, got]

    def loaded(part, riding):
        return part if vec is None or not riding else jnp.concatenate([part, vec], 0)

    for number, bits in enumerate(steps):
        size = terms[0].shape[0] >> len(bits[0])
        others = range(1, 2 ** len(bits[0]))
        parts = [rounded_sum(terms, slice(other * size, (other + 1) * size)) for other in others]
        parts = [loaded(part, number > 0) for part in parts]
        gate = yield parts
        came = after([swap_dp(part, masks_of(bits, other)) for part, other in zip(parts, others)], gate)
        terms = [term[:size] for term in terms] + [part[:size] for part in came]
        if vec is not None and number > 0:
            vec = rounded_sum([vec] + [part[size:] for part in came], slice(None))
    value = rounded_sum(terms, slice(None))
    rest = list(range(sum(len(bits) for bits in groups[0]), count.bit_length() - 1))
    for bits in zip(rest, rest[1:] + rest[:1]):
        size = value.shape[0]
        whole = loaded(value, True)
        gate = yield [whole]
        whole = rounded_sum([whole, after(swap_dp(whole, [1 << bit for bit in bits]), gate)], slice(None))
        value, vec = whole[:size], (None if vec is None else whole[size:])
    pieces = [value]
    for bits in reversed(steps[1:]):
        if len(pieces) > 1:
            value = jnp.concatenate(pieces, 0)
        gate = yield [value]
        came = [swap_dp(value, masks_of(bits, other)) for other in range(1, 2 ** len(bits[0]))]
        pieces = [value] + after(came, gate)
    if vec is not None:
        pieces = pieces + [vec]
    if len(pieces) > 1:
        value = jnp.concatenate(pieces, 0)
    gate = yield [value]
    sender = 1 - receiver
    masks = masks_of(steps[0], 1)
    ways = ((receiver, masks[receiver]), (sender, 0), (sender, masks[sender]))
    came = []
    for source, mask in ways:
        pairs = [(source * count + i, receiver * count + (i ^ mask)) for i in range(count)]
        came.append(lax.ppermute(value, ("section", "dp"), pairs))
    yield [value] + after(came, gate)


class Steps:
    def __init__(self, *args):
        self.steps = reduce_steps(*args)
        self.ready = next(self.steps)

    def step(self, gate=()):
        self.ready = self.steps.send(gate)
        return self.ready

    def finish(self):
        while len(self.ready) != 4:
            self.step()
        return self.ready[:2], self.ready[2:]


def after(values, earlier):
    return lax.optimization_barrier((values, earlier))[0] if earlier else values


def shards(
    section_inputs,
    seq_lengths,
    dilations,
    gains_in,
    biases_in,
    gains_mid,
    biases_mid,
    out_bias,
    w_in,
    w_out,
    conv_taps,
):
    section = lax.axis_index("section")
    count = lax.axis_size("dp")
    groups_of = (scatter_groups(count, False), scatter_groups(count, False))
    rows = jnp.swapaxes(section_inputs[0], 1, 2)
    width = rows.shape[1]
    inner = w_out.shape[1]
    taps_of = (conv_taps.shape[1], DEC_TAPS)

    own_w = (jnp.swapaxes(w_in[0], 0, 1), w_out[0], conv_taps[0])
    send_rows = pick_rows(rows)
    got_w = tuple(swap_sections(member) for member in own_w)
    got_rows = swap_sections(after(send_rows, got_w))
    small = pack_small(gains_in, biases_in, gains_mid[0], biases_mid[0], out_bias, dilations)
    got_small = swap_sections(small)

    outs, send_y, grad_dec, keep_dec, send_dec, vec, *kept = main_call(
        taps_of, groups_of[1], seq_lengths, rows, got_rows, small, got_small, own_w, got_w
    )
    dec = Steps(keep_dec, swap_sections(send_dec), groups_of[1], 1, vec)
    gradient = after(grad_dec, dec.ready)
    grad_projected, vec, keep_enc, send_enc = encoder_call(
        taps_of[0], groups_of[0], seq_lengths, gradient, small, got_small, kept, own_w[1], got_w[1], own_w[2], got_w[2]
    )
    got_y = swap_sections(send_y)
    enc_early = swap_sections(send_enc)
    grad_projected = after(grad_projected, dec.step())
    grads_x, send_gx, vec = first_call(
        0, grad_dec, grad_dec, grad_projected, vec, kept[0:3], small, got_small, own_w[0], got_w[0]
    )

    def joined(pair, got):
        pair = lax.dynamic_update_slice_in_dim(pair, got[None], 1 - section, 0)
        return jnp.swapaxes(pair, 1, 2)[None]

    enc = Steps(keep_enc, enc_early, groups_of[0], 0, vec)
    got_gx = swap_sections(send_gx)
    outputs = joined(outs, got_y)
    input_grads = joined(grads_x, got_gx)
    named = {"d": dec, "e": enc}
    last = ()
    for name in SEQ:
        if name in named:
            if len(named[name].ready) != 4:
                last = named[name].step(last)
        else:
            last = [*last, outputs if name == "y" else input_grads]
    enc = enc.finish()
    dec = dec.finish()
    grads = unpack(taps_of, groups_of, enc, dec, width, inner)
    return (
        outputs,
        input_grads,
        grads[3],
        grads[4],
        grads[5][None],
        grads[6][None],
        grads[7],
        jnp.swapaxes(grads[0], 0, 1)[None],
        grads[1][None],
        grads[2][None],
    )


def solution(mesh):
    in_specs = (
        P("section", None, "dp", None),
        P(None, "dp"),
        P("section"),
        P("section", None),
        P("section", None),
        P("section", None, None),
        P("section", None, None),
        P("section", None),
        P("section", None, None),
        P("section", None, None),
        P("section", None, None, None),
    )
    out_specs = (
        P("section", None, "dp", None),
        P("section", None, "dp", None),
        P("section", None),
        P("section", None),
        P("section", None, None),
        P("section", None, None),
        P("section", None),
        P("section", None, None),
        P("section", None, None),
        P("section", None, None, None),
    )
    return jax.shard_map(shards, mesh=mesh, in_specs=in_specs, out_specs=out_specs, check_vma=False)
```
